32 devices in a mesh: dp: 8 (over z, x), rep: 4 (over y, core).
Axes of the slice: x: 2, y: 2, z: 4, core: 2. Of those that a mesh axis runs over, the one named last changes fastest.
Arguments:
- content_stream: bfloat16 [32, 512, 768], P(('dp', 'rep')), may hold values from -6 to 6
- query_stream: bfloat16 [32, 512, 768], P(('dp', 'rep')), may hold values from -6 to 6
- segments: int32 [32, 512], P(('dp', 'rep')), may hold values from 0 to 6, never falling along the last dimension, each value on 1 to 192 neighbouring positions
- perm_order: int32 [32, 512], P(('dp', 'rep')), may hold values from 0 to 511, each once within a row
- predicted: int32 [32, 512], P(('dp', 'rep')), may hold values 0 or 1
- buckets: int32 [1023], replicated, may hold values from 0 to 31, as said below
- bias_table: bfloat16 [32, 12], replicated, may hold values from -4 to 4
- project_one: bfloat16 [768, 2304], P('dp', 'rep'), may hold values from -0.21875 to 0.21875
- output_one: bfloat16 [768, 768], P('dp', 'rep'), may hold values from -1.75 to 1.75
- expand_one: bfloat16 [768, 3072], P('dp', 'rep'), may hold values from -0.21875 to 0.21875
- contract_one: bfloat16 [3072, 768], P('dp', 'rep'), may hold values from -0.109375 to 0.109375
- vectors_one: bfloat16 [12, 768], P('rep', 'dp'), may hold values from -2 to 2, as said below
- project_two: bfloat16 [768, 2304], P('dp', 'rep'), may hold values from -0.21875 to 0.21875
- output_two: bfloat16 [768, 768], P('dp', 'rep'), may hold values from -1.75 to 1.75
- expand_two: bfloat16 [768, 3072], P('dp', 'rep'), may hold values from -0.21875 to 0.21875
- contract_two: bfloat16 [3072, 768], P('dp', 'rep'), may hold values from -0.109375 to 0.109375
- vectors_two: bfloat16 [12, 768], P('rep', 'dp'), may hold values from -2 to 2, as said below
- content_cotangent: bfloat16 [32, 512, 768], P(('dp', 'rep')), may hold values from -6 to 6
- query_cotangent: bfloat16 [32, 512, 768], P(('dp', 'rep')), may hold values from -6 to 6
Outputs:
- content_result: bfloat16 [32, 512, 768], P(('dp', 'rep'))
- query_result: bfloat16 [32, 512, 768], P(('dp', 'rep'))
- content_gradient: float32 [32, 512, 768], P(('dp', 'rep'))
- query_gradient: float32 [32, 512, 768], P(('dp', 'rep'))
- table_gradient: float32 [32, 12], replicated
- project_one_gradient: float32 [768, 2304], P('dp', 'rep')
- output_one_gradient: float32 [768, 768], P('dp', 'rep')
- expand_one_gradient: float32 [768, 3072], P('dp', 'rep')
- contract_one_gradient: float32 [3072, 768], P('dp', 'rep')
- vectors_one_gradient: float32 [12, 768], P('rep', 'dp')
- project_two_gradient: float32 [768, 2304], P('dp', 'rep')
- output_two_gradient: float32 [768, 768], P('dp', 'rep')
- expand_two_gradient: float32 [768, 3072], P('dp', 'rep')
- contract_two_gradient: float32 [3072, 768], P('dp', 'rep')
- vectors_two_gradient: float32 [12, 768], P('rep', 'dp')
The draws below stay inside these ranges and needn't reach their ends.
Inputs may be any that keep to these rules, and one draw needn't show every extreme that they name: `segments`: in each row segment numbers never fall; 6 marks the padding at the row's end, the numbers below it are documents. `perm_order`: each row is a permutation of 0 to 511; within a document a smaller number comes earlier in the permuted order. `buckets`: entry 511 + d is the bucket of relative position d (key minus query): 0 at d = 0, at most 15 for d < 0, 16 or more for d > 0, never falling as the magnitude grows on either side. `vectors_one`: rows 3 and 6 lie near 1. `vectors_two`: rows 3 and 6 lie near 1.
All inputs are finite; a program needn't handle non-finite values. No bound on the sum of `predicted` on one device may be relied on, other than what follows from the above.
Results may differ from the reference program's by a relative error of at most 0.023.
Values may be sent and summed in bfloat16 or wider, within the bound.
A program may use at most 320 MiB of HBM per device.

```python
import math
import jax
import jax.numpy as jnp
import numpy as np
from jax import lax

D = 768
H = 12
HD = 64
FF = 3072
NB = 32
ROW = 512
DOCS = 6
ROWS = 32
VEC = 12


def vector_layout(noise):
    rows = jnp.arange(VEC)[:, None]
    gains = (rows == 3) | (rows == 6)
    return jnp.where(gains, 1.0 + 0.15 * noise, 0.5 * noise).astype(jnp.float32)


def draw_vectors_one(key, part):
    inner = jax.random.fold_in(key, 1)
    noise = jnp.clip(jax.random.normal(inner, (VEC, D), jnp.float32), -4.0, 4.0)
    return vector_layout(noise).astype(jnp.bfloat16)


def draw_vectors_two(key, part):
    inner = jax.random.fold_in(key, 2)
    noise = jnp.clip(jax.random.normal(inner, (VEC, D), jnp.float32), -4.0, 4.0)
    return vector_layout(noise).astype(jnp.bfloat16)


def draw_buckets(key, part):
    steps = jax.random.randint(jax.random.fold_in(key, 3), (2, ROW - 1), 0, 2)
    rising = jnp.minimum(jnp.cumsum(steps, axis=1), NB // 2 - 1)
    spots = jnp.arange(ROW - 1)[None, :]
    rising = jnp.where(spots == ROW - 2, NB // 2 - 1, rising)
    middle = jnp.zeros((1,), jnp.int32)
    return jnp.concatenate([rising[0][::-1].astype(jnp.int32), middle, (rising[1] + NB // 2).astype(jnp.int32)]).astype(jnp.int32)


def plant(result, rng, least, top_value):
    longest = result.shape.index(max(result.shape))
    spots = []
    for shift in (0, 1):
        where = [jax.random.randint(jax.random.fold_in(rng, axis), (), 0, length) for axis, length in enumerate(result.shape)]
        where[longest] = (where[longest] + shift) % result.shape[longest]
        spots.append(tuple(where))
    return result.at[spots[0]].set(least).at[spots[1]].set(top_value)


def levels(own_key, dims, split, least, top_value):
    factor_of = 1.0
    for axis_at, blocks in split:
        heights = jax.random.uniform(jax.random.fold_in(jax.random.fold_in(own_key, 6), axis_at), (blocks,), jnp.float32, least / len(split), top_value / len(split))
        factor_of = factor_of * jnp.repeat(jnp.exp(heights), dims[axis_at] // blocks).reshape((-1,) + (1,) * (len(dims) - 1 - axis_at))
    return factor_of


def split_up(amount, total, bound, slope):
    portions = [(1 << 20) // math.isqrt(standing ** slope) + 1 for standing in range(2, amount + 1)]
    surplus, counts = total - bound - (amount - 1), [1] * (amount - 1)
    while surplus > 0:
        candidates = [i for i in range(amount - 1) if counts[i] < bound]
        whole, budget = sum([portions[i] for i in candidates]), surplus
        for i in candidates:
            extra = min(bound - counts[i], max(1, budget * portions[i] // whole), surplus)
            counts[i] = counts[i] + extra
            surplus = surplus - extra
    return np.array([bound] + counts)


def uneven_parts(rng, amount, total, reach, slope):
    if amount == 2:
        one = jax.random.randint(rng, (), max(1, total - reach), min(reach, total - 1) + 1)
        return jnp.stack([one, total - one])
    sizes = jnp.asarray(split_up(amount, total, reach, slope), jnp.int32)
    couples = (amount - 1) // 2
    source_of, taker = sizes[1:1 + 2 * couples:2], sizes[2:2 + 2 * couples:2]
    slack = jnp.minimum(source_of - 1, reach - taker)
    moved = jax.random.randint(jax.random.fold_in(rng, 1), (couples,), 0, 1 << 20) % (slack + 1)
    sizes = sizes.at[1:1 + 2 * couples:2].set(source_of - moved).at[2:2 + 2 * couples:2].set(taker + moved)
    return sizes[jax.random.permutation(jax.random.fold_in(rng, 2), amount)]


def gaussian(key, dims, width, limit, pieces=(), kind=jnp.bfloat16):
    loudness = levels(key, dims, pieces, -0.22, 0.18) if pieces else 1.0
    drawn = jax.random.normal(key, dims, jnp.float32) * width * loudness
    return jnp.minimum(jnp.maximum(drawn, -limit), limit).astype(kind)


def setup_inputs(seed: int = 0) -> dict:
    arg_keys = jax.random.split(jax.random.key(seed), 20)
    return {
        "content_stream": gaussian(arg_keys[0], (ROWS, ROW, D), 1.0, 6.0, ((0, 32),)),
        "query_stream": gaussian(arg_keys[1], (ROWS, ROW, D), 1.0, 6.0, ((0, 32),)),
        "segments": jax.vmap(lambda own: jnp.searchsorted(jnp.cumsum(uneven_parts(own, DOCS + 1, ROW, ROW * 3 // 8, 1)), jnp.arange(ROW), side="right"))(jax.random.split(arg_keys[2], ROWS)).reshape((ROWS, ROW)).astype(jnp.int32),
        "perm_order": jax.vmap(lambda own: jax.random.permutation(own, ROW))(jax.random.split(arg_keys[3], ROWS)).reshape((ROWS, ROW)).astype(jnp.int32),
        "predicted": plant((jax.random.randint(arg_keys[4], (ROWS, ROW), 0, 20) < 3).astype(jnp.int32), jax.random.fold_in(arg_keys[4], 1), 0, 1),
        "buckets": draw_buckets(jax.random.fold_in(arg_keys[19], 71), 0),
        "bias_table": gaussian(arg_keys[6], (NB, H), 1.0, 4.0),
        "project_one": gaussian(arg_keys[7], (D, 3 * D), D ** -0.5, 0.21875, ((0, 8), (1, 4))),
        "output_one": gaussian(arg_keys[8], (D, D), (D // 64) ** -0.5, 1.75, ((0, 8), (1, 4))),
        "expand_one": gaussian(arg_keys[9], (D, FF), D ** -0.5, 0.21875, ((0, 8), (1, 4))),
        "contract_one": gaussian(arg_keys[10], (FF, D), FF ** -0.5, 0.109375, ((0, 8), (1, 4))),
        "vectors_one": draw_vectors_one(jax.random.fold_in(arg_keys[19], 71), 0),
        "project_two": gaussian(arg_keys[12], (D, 3 * D), D ** -0.5, 0.21875, ((0, 8), (1, 4))),
        "output_two": gaussian(arg_keys[13], (D, D), (D // 64) ** -0.5, 1.75, ((0, 8), (1, 4))),
        "expand_two": gaussian(arg_keys[14], (D, FF), D ** -0.5, 0.21875, ((0, 8), (1, 4))),
        "contract_two": gaussian(arg_keys[15], (FF, D), FF ** -0.5, 0.109375, ((0, 8), (1, 4))),
        "vectors_two": draw_vectors_two(jax.random.fold_in(arg_keys[19], 71), 0),
        "content_cotangent": gaussian(arg_keys[17], (ROWS, ROW, D), 1.0, 6.0, ((0, 32),)),
        "query_cotangent": gaussian(arg_keys[18], (ROWS, ROW, D), 1.0, 6.0, ((0, 32),)),
    }


@jax.custom_vjp
def low(v):
    return lax.optimization_barrier(v.astype(jnp.bfloat16)).astype(jnp.float32)

@jax.custom_vjp
def low_back(v):
    return v

def low_keep(v):
    return (low(v), None)

def low_pass(kept, grad):
    return (grad,)

def back_keep(v):
    return (v, None)

def back_low(kept, grad):
    return (low(grad),)
low.defvjp(low_keep, low_pass)
low_back.defvjp(back_keep, back_low)
highest = lax.Precision.HIGHEST

def layer_norm(values, gain, shift):
    centered = values - lax.optimization_barrier(jnp.mean(values, axis=-1, keepdims=True))
    spread = lax.optimization_barrier(jnp.mean(centered * centered, axis=-1, keepdims=True))
    return centered * lax.rsqrt(spread + 1e-05) * gain + shift

def rounded_both(value):
    return low_back(low(value))

def attend_row(bundle, position_bias):
    queries, keys, values, allowed = bundle
    scores = jnp.einsum('qhd,khd->hqk', queries, keys, precision=highest) * 0.125 + position_bias
    scores = low_back(scores)
    scores = jnp.where(allowed, scores, -1e+30)
    row_max = lax.optimization_barrier(jnp.max(scores, axis=-1, keepdims=True))
    lifted = jnp.where(allowed, jnp.exp(scores - row_max), 0.0)
    row_total = lax.optimization_barrier(jnp.sum(lifted, axis=-1, keepdims=True))
    row_total = jnp.where(row_total > 0, row_total, 1.0)
    chances = low(lifted / row_total)
    context = jnp.einsum('hqk,khd->qhd', chances, values, precision=highest)
    return rounded_both(context)

def run_layer(content_rows, query_rows, weights, position_bias, allowed_content, allowed_query):
    project, output, expand, contract, vectors = weights
    mixed = jnp.dot(content_rows, project, precision=highest)
    queries_content = rounded_both(mixed[:, :D] + vectors[0])
    keys = rounded_both(mixed[:, D:2 * D])
    values = rounded_both(mixed[:, 2 * D:] + vectors[1])
    queries_query = rounded_both(jnp.dot(query_rows, project[:, :D], precision=highest) + vectors[0])
    shape = (-1, ROW, H, HD)
    checked = jax.checkpoint(attend_row)

    def passed(queries, allowed):
        bundles = (queries.reshape(shape), keys.reshape(shape), values.reshape(shape), allowed)
        return lax.map(lambda bundle: checked(bundle, position_bias), bundles).reshape(-1, D)

    def branch(inputs, context):
        attended = low_back(jnp.dot(context, output, precision=highest) + vectors[2])
        normed = layer_norm(inputs + attended, vectors[3], vectors[4])
        hidden = low_back(jnp.dot(low(normed), expand, precision=highest) + vectors[8:].reshape(FF))
        activated = low(jax.nn.gelu(hidden, approximate=False))
        feed_out = low_back(jnp.dot(activated, contract, precision=highest) + vectors[5])
        return low(layer_norm(normed + feed_out, vectors[6], vectors[7]))
    content_next = branch(content_rows, passed(queries_content, allowed_content))
    query_next = branch(query_rows, passed(queries_query, allowed_query))
    return (content_next, query_next)

def group_pass(bundle, weights, position_bias):
    content_group, query_group, allowed_content, allowed_query = bundle
    content_rows = content_group.reshape(-1, D)
    query_rows = query_group.reshape(-1, D)
    for layer_index in range(2):
        content_rows, query_rows = run_layer(content_rows, query_rows, weights[5 * layer_index:5 * layer_index + 5], position_bias, allowed_content, allowed_query)
    return (content_rows.reshape(content_group.shape), query_rows.reshape(query_group.shape))

def reference(content_stream, query_stream, segments, perm_order, predicted, buckets, bias_table, project_one, output_one, expand_one, contract_one, vectors_one, project_two, output_two, expand_two, contract_two, vectors_two, content_cotangent, query_cotangent):
    same_doc = (segments[:, :, None] == segments[:, None, :]) & (segments[:, None, :] != DOCS)
    visible = predicted[:, None, :] == 0
    allowed_content = same_doc & (visible | (perm_order[:, None, :] <= perm_order[:, :, None]))
    allowed_query = same_doc & (visible | (perm_order[:, None, :] < perm_order[:, :, None]))
    spots = jnp.arange(ROW, dtype=jnp.int32)
    bucket_index = buckets[(spots[None, :] - spots[:, None] + ROW - 1).astype(jnp.int32)]
    checked_group = jax.checkpoint(group_pass)

    def forward(content_rows, query_rows, table, *weights):
        position_bias = jnp.transpose(table[bucket_index], (2, 0, 1))
        bundles = (content_rows.reshape(-1, 8, ROW, D), query_rows.reshape(-1, 8, ROW, D), allowed_content.reshape(-1, 8, ROW, ROW), allowed_query.reshape(-1, 8, ROW, ROW))
        content_out, query_out = lax.map(lambda bundle: checked_group(bundle, weights, position_bias), bundles)
        return (content_out.reshape(ROWS, ROW, D), query_out.reshape(ROWS, ROW, D))
    weights = (project_one, output_one, expand_one, contract_one, vectors_one, project_two, output_two, expand_two, contract_two, vectors_two)
    primals = [content_stream.astype(jnp.float32), query_stream.astype(jnp.float32), bias_table.astype(jnp.float32)] + [weight.astype(jnp.float32) for weight in weights]
    results, backward = jax.vjp(forward, *primals)
    grads = backward((content_cotangent.astype(jnp.float32), query_cotangent.astype(jnp.float32)))
    return (results[0].astype(jnp.bfloat16), results[1].astype(jnp.bfloat16), grads[0], grads[1], grads[2], grads[3], grads[4], grads[5], grads[6], grads[7], grads[8], grads[9], grads[10], grads[11], grads[12])
```

```python
import functools
import jax
import jax.numpy as jnp
from jax import lax
from jax.experimental import pallas as pl
from jax.experimental.pallas import tpu as pltpu
from jax.sharding import PartitionSpec as P

F32 = jnp.float32
BF = jnp.bfloat16
LOG2E = 1.4426950408889634
NEG = -1e30
FLOOR = -1e29
VM = 60 * 1024 * 1024
NT = (((1,), (1,)), ((), ()))
TN = (((0,), (0,)), ((), ()))


def nt(a, b):
    return lax.dot_general(a, b, NT, preferred_element_type=F32)


def tn(a, b):
    return lax.dot_general(a, b, TN, preferred_element_type=F32)


def nn(a, b):
    return jnp.dot(a, b, preferred_element_type=F32)


def whole(shape):
    return pl.BlockSpec(shape, lambda *_: (0,) * len(shape))


def params():
    return pltpu.CompilerParams(vmem_limit_bytes=VM)


def prep_kernel(base, base_t, marks, bias, bias_t, mask, mask_t):
    h = pl.program_id(0)
    n = bias.shape[1]
    for src, dst in ((base, bias), (base_t, bias_t)):
        row = jnp.broadcast_to(src[0], (n, 2 * n))
        dst[0] = pltpu.roll(row, 0, 1, stride=1, stride_axis=0)[:, :n]

    @pl.when(h == 0)
    def _():
        rows = marks[...]
        seg_r, perm_r, pred_r = rows[0:1], rows[1:2], rows[2:3]
        for lo in range(0, n, 128):
            at = slice(lo, lo + 128)

            def col(k):
                piece = jnp.broadcast_to(rows[k : k + 1, at], (128, 128))
                return piece.T[:, :1]

            seg_c, perm_c, pred_c = col(0), col(1), col(2)
            same = (seg_c == seg_r) & (seg_r != 6.0)
            shown = pred_r == 0.0
            mask[0, at, :] = jnp.where(same & (shown | (perm_r <= perm_c)), 0.0, NEG)
            mask[1, at, :] = jnp.where(same & (shown | (perm_r < perm_c)), 0.0, NEG)
            same = (seg_c == seg_r) & (seg_c != 6.0)
            shown = pred_c == 0.0
            mask_t[at, :n] = jnp.where(same & (shown | (perm_c <= perm_r)), 0.0, NEG)
            mask_t[at, n:] = jnp.where(same & (shown | (perm_c < perm_r)), 0.0, NEG)


def prep(base, base_t, marks):
    heads, n2 = base.shape
    n = n2 // 2
    return pl.pallas_call(
        prep_kernel,
        grid=(heads,),
        in_specs=[
            pl.BlockSpec((1, 1, n2), lambda h: (h, 0, 0)),
            pl.BlockSpec((1, 1, n2), lambda h: (h, 0, 0)),
            whole(marks.shape),
        ],
        out_specs=[
            pl.BlockSpec((1, n, n), lambda h: (h, 0, 0)),
            pl.BlockSpec((1, n, n), lambda h: (h, 0, 0)),
            whole((2, n, n)),
            whole((n, 2 * n)),
        ],
        out_shape=[
            jax.ShapeDtypeStruct((heads, n, n), F32),
            jax.ShapeDtypeStruct((heads, n, n), F32),
            jax.ShapeDtypeStruct((2, n, n), F32),
            jax.ShapeDtypeStruct((n, 2 * n), F32),
        ],
        compiler_params=params(),
        name="prep",
    )(base.reshape(heads, 1, n2), base_t.reshape(heads, 1, n2), marks)


def bias_bases(buckets, bias_table, n):
    selector = (buckets[:, None] == jnp.arange(bias_table.shape[0], dtype=jnp.int32)[None, :]).astype(F32)
    per_offset = jnp.dot(selector, bias_table.astype(F32), precision=lax.Precision.HIGHEST).T * LOG2E
    heads = per_offset.shape[0]
    zero = jnp.zeros((heads, 1), F32)
    base = jnp.concatenate([per_offset[:, n - 1 :], zero, per_offset[:, : n - 1]], axis=1)
    flipped = per_offset[:, ::-1]
    base_t = jnp.concatenate([flipped[:, n - 1 :], zero, flipped[:, : n - 1]], axis=1)
    return selector, base, base_t


def attn_fwd_kernel(rows_at, x, y, pw, vec, bias, mask, q_o, k_o, v_o, ctx_o, lse_o, pf, lse_s):
    p = pl.program_id(0)
    n, d = x.shape
    pairs = d // 128

    @pl.when(p == 0)
    def _():
        pf[...] = jnp.concatenate([pw[r] for r in range(pw.shape[0])], axis=1)
        bq, bv = vec[0:1], vec[1:2]
        xv = x[...]
        qc = nn(xv, pf[:, :d]) + bq
        qq = nn(y[...], pf[:, :d]) + bq
        kk = nn(xv, pf[:, d : 2 * d])
        vv = nn(xv, pf[:, 2 * d :]) + bv
        for c in range(pairs):
            at = slice(128 * c, 128 * c + 128)
            q_o[c, :n] = qc[:, at].astype(BF)
            q_o[c, n:] = qq[:, at].astype(BF)
            k_o[c] = kk[:, at].astype(BF)
            v_o[c] = vv[:, at].astype(BF)
        lse_s[...] = jnp.zeros_like(lse_s)

    k = k_o[p]
    v = v_o[p]
    low = lax.broadcasted_iota(jnp.int32, (1, 128), 1) < 64
    lane = lax.broadcasted_iota(jnp.int32, (1, 128), 1)
    vx = jnp.concatenate([v, jnp.ones_like(v)], axis=1)
    k0 = jnp.where(low, k, 0)
    k1 = jnp.where(low, 0, k)
    for s in range(2):
        for lo in range(0, n, rows_at):
            at = slice(lo, lo + rows_at)
            to = slice(s * n + lo, s * n + lo + rows_at)
            q = q_o[p, to]
            outs = []
            for hh, kh in ((0, k0), (1, k1)):
                sc = nt(q, kh) * (0.125 * LOG2E) + (bias[hh, at] + mask[s, at])
                m = jnp.maximum(jnp.max(sc, axis=-1, keepdims=True), FLOOR)
                e = jnp.exp2(sc - m).astype(BF)
                r = nn(e, vx)
                tot = r[:, 128:]
                tot = jnp.where(tot > 0, tot, 1.0)
                lse = m + jnp.log2(tot)
                lse_s[to] = jnp.where(lane == 2 * p + hh, lse, lse_s[to])
                outs.append(r[:, :128] / tot)
            ctx_o[0, to] = jnp.where(low, outs[0], outs[1]).astype(BF)

    @pl.when(p == pairs - 1)
    def _():
        for lo in range(0, 2 * n, 128):
            lse_o[:, lo : lo + 128] = lse_s[lo : lo + 128].T[: lse_o.shape[0]]


def attn_fwd(x, y, pw, vec, bias, mask, rows_at=256):
    n, d = x.shape
    pairs = d // 128
    return pl.pallas_call(
        functools.partial(attn_fwd_kernel, rows_at),
        grid=(pairs,),
        in_specs=[
            whole(x.shape), whole(y.shape), whole(pw.shape), whole(vec.shape),
            pl.BlockSpec((2, n, n), lambda p: (p, 0, 0)),
            whole(mask.shape),
        ],
        out_specs=[
            whole((pairs, 2 * n, 128)), whole((pairs, n, 128)), whole((pairs, n, 128)),
            pl.BlockSpec((1, 2 * n, 128), lambda p: (p, 0, 0)),
            whole((16, 2 * n)),
        ],
        out_shape=[
            jax.ShapeDtypeStruct((pairs, 2 * n, 128), BF),
            jax.ShapeDtypeStruct((pairs, n, 128), BF),
            jax.ShapeDtypeStruct((pairs, n, 128), BF),
            jax.ShapeDtypeStruct((pairs, 2 * n, 128), BF),
            jax.ShapeDtypeStruct((16, 2 * n), F32),
        ],
        scratch_shapes=[
            pltpu.VMEM((d, 3 * d), BF),
            pltpu.VMEM((2 * n, 128), F32),
        ],
        compiler_params=params(),
        name="attn_fwd",
    )(x, y, pw, vec, bias, mask)


def gelu_parts(z):
    e = jnp.exp2(z * z * (-0.5 * LOG2E))
    den = 1.0 + (0.3275911 * 0.7071067811865476) * jnp.abs(z)
    t = pl.reciprocal(den, approx=True)
    t = t * (2.0 - den * t)
    poly = t * (0.127414796 + t * (-0.142248368 + t * (0.7107068705 + t * (-0.7265760135 + t * 0.5307027145))))
    tail = poly * e
    phi = jnp.where(z < 0, tail, 1.0 - tail)
    return z * phi, phi + z * (e * 0.3989422804014327)


def moments(v):
    centered = v - jnp.mean(v, axis=-1, keepdims=True)
    rs = lax.rsqrt(jnp.mean(centered * centered, axis=-1, keepdims=True) + 1e-05)
    return centered * rs, rs


def post_fwd_kernel(blocks, x, y, ctx, ow, ew, ct, vec, rc_o, rq_o, xh1_o, nl_o, act_o, gp_o, xh2_o, rs_o, of):
    t = pl.program_id(0)
    d = x.shape[1]
    ff = ew.shape[1]

    @pl.when(t == 0)
    def _():
        of[...] = jnp.concatenate([ow[r] for r in range(ow.shape[0])], axis=1)

    z = jnp.where(t < blocks, x[...].astype(F32), y[...].astype(F32))
    cx = jnp.concatenate([ctx[c] for c in range(ctx.shape[0])], axis=1)
    first = z + (nn(cx, of[...]) + vec[2:3])
    xh1, rs1 = moments(first)
    normed = xh1 * vec[3:4] + vec[4:5]
    nl = normed.astype(BF)
    xh1_o[...] = xh1.astype(BF)
    nl_o[...] = nl
    second = normed + vec[5:6]
    for f in range(ff // d):
        at = slice(f * d, f * d + d)
        h = nn(nl, ew[:, at]) + vec[8 + f : 9 + f]
        act, gp = gelu_parts(h)
        act = act.astype(BF)
        act_o[:, at] = act
        gp_o[:, at] = gp.astype(BF)
        second = second + nt(act, ct[:, at])
    xh2, rs2 = moments(second)
    xh2_o[...] = xh2.astype(BF)
    lane = lax.broadcasted_iota(jnp.int32, (1, 128), 1)
    rs_o[...] = jnp.where(lane < 64, rs1, rs2)
    res = (xh2 * vec[6:7] + vec[7:8]).astype(BF)

    @pl.when(t < blocks)
    def _():
        rc_o[...] = res

    @pl.when(t >= blocks)
    def _():
        rq_o[...] = res


def post_fwd(x, y, ctx, ow, ew, ct, vec, tb=256):
    n, d = x.shape
    ff = ew.shape[1]
    pairs = ctx.shape[0]
    blocks = n // tb
    first = lambda t: (jnp.minimum(t, blocks - 1), 0)
    later = lambda t: (jnp.maximum(t - blocks, 0), 0)
    row = lambda t: (t, 0)
    return pl.pallas_call(
        functools.partial(post_fwd_kernel, blocks),
        grid=(2 * blocks,),
        in_specs=[
            pl.BlockSpec((tb, d), first), pl.BlockSpec((tb, d), later),
            pl.BlockSpec((pairs, tb, 128), lambda t: (0, t, 0)),
            whole(ow.shape), whole(ew.shape), whole(ct.shape), whole(vec.shape),
        ],
        out_specs=[
            pl.BlockSpec((tb, d), first), pl.BlockSpec((tb, d), later),
            pl.BlockSpec((tb, d), row), pl.BlockSpec((tb, d), row),
            pl.BlockSpec((tb, ff), row), pl.BlockSpec((tb, ff), row),
            pl.BlockSpec((tb, d), row), pl.BlockSpec((tb, 128), row),
        ],
        out_shape=[
            jax.ShapeDtypeStruct((n, d), BF), jax.ShapeDtypeStruct((n, d), BF),
            jax.ShapeDtypeStruct((2 * n, d), BF), jax.ShapeDtypeStruct((2 * n, d), BF),
            jax.ShapeDtypeStruct((2 * n, ff), BF), jax.ShapeDtypeStruct((2 * n, ff), BF),
            jax.ShapeDtypeStruct((2 * n, d), BF), jax.ShapeDtypeStruct((2 * n, 128), F32),
        ],
        scratch_shapes=[pltpu.VMEM((d, d), BF)],
        compiler_params=params(),
        name="post_fwd",
    )(x, y, ctx, ow, ew, ct, vec)


def norm_back(g, xh, rs, gain):
    a = g * gain
    return rs * (a - jnp.mean(a, axis=-1, keepdims=True) - xh * jnp.mean(a * xh, axis=-1, keepdims=True))


def rowsum(v):
    return jnp.sum(v, axis=0, keepdims=True)


def post_bwd_kernel(blocks, gc, gq, ctx, xh1, nl, gp, xh2, rs, act, ow, ew, ct, vec,
                    first_o, gctx_o, delta_o, vg_o, do_o, de_o, dc_o,
                    of, gh_s, nl_t, gf_t, cx_t, ga_s):
    t = pl.program_id(0)
    tb, d = gc.shape
    ff = ew.shape[1]

    @pl.when(t == 0)
    def _():
        of[...] = jnp.concatenate([ow[r] for r in range(ow.shape[0])], axis=1)
        vg_o[...] = jnp.zeros_like(vg_o)

    @pl.when(t < 2 * blocks)
    def _():
        g = jnp.where(t < blocks, gc[...].astype(F32), gq[...].astype(F32))
        rs1, rs2 = rs[:, :1], rs[:, 64:65]
        xh = xh2[...].astype(F32)
        vg_o[6:7] += rowsum(g * xh)
        vg_o[7:8] += rowsum(g)
        gs = norm_back(g, xh, rs2, vec[6:7])
        gf = gs.astype(BF)
        vg_o[5:6] += rowsum(gf.astype(F32))
        gn = gs
        spot = pl.ds(pl.multiple_of(t * tb, tb), tb)
        for f in range(ff // d):
            at = slice(f * d, f * d + d)
            gh = (nn(gf, ct[:, at]) * gp[:, at].astype(F32)).astype(BF)
            gh_s[spot, at] = gh
            vg_o[8 + f : 9 + f] += rowsum(gh.astype(F32))
            gn = gn + nt(gh, ew[:, at])
        xh = xh1[...].astype(F32)
        vg_o[3:4] += rowsum(gn * xh)
        vg_o[4:5] += rowsum(gn)
        first = norm_back(gn, xh, rs1, vec[3:4])
        first_o[...] = first
        ga = first.astype(BF)
        vg_o[2:3] += rowsum(ga.astype(F32))
        ga_s[spot] = ga
        gx = nt(ga, of[...]).astype(BF)
        cx = jnp.concatenate([ctx[c] for c in range(ctx.shape[0])], axis=1)
        for c in range(ctx.shape[0]):
            gctx_o[c] = gx[:, 128 * c : 128 * c + 128]
        prod = gx.astype(F32) * cx.astype(F32)
        high = prod.astype(BF)
        rest = (prod - high.astype(F32)).astype(BF)
        heads = lax.broadcasted_iota(jnp.int32, (16, d), 0)
        spots = lax.broadcasted_iota(jnp.int32, (16, d), 1)
        pick = jnp.where((spots >= heads * 64) & (spots < heads * 64 + 64), 1.0, 0.0).astype(BF)
        delta_o[...] = nt(pick, high) + nt(pick, rest)
        nl_t[:, spot] = nl[...].T
        gf_t[:, spot] = gf.T
        cx_t[:, spot] = cx.T

    @pl.when(t == 2 * blocks)
    def _():
        do = nn(cx_t[...], ga_s[...])
        w = do_o.shape[2]
        for r in range(do_o.shape[0]):
            do_o[r] = do[:, r * w : r * w + w].astype(BF)

    for f in range(ff // d):
        @pl.when(t == 2 * blocks + f)
        def _():
            de_o[...] = nn(nl_t[...], gh_s[:, f * d : f * d + d]).astype(BF)
            dc_o[...] = nn(gf_t[...], act[...]).astype(BF)


def post_bwd(gc, gq, ctx, xh1, nl, gp, xh2, rs, act, ow, ew, ct, vec, tb=256):
    n, d = gc.shape
    ff = ew.shape[1]
    pairs = ctx.shape[0]
    blocks = n // tb
    last = 2 * blocks - 1
    tok = lambda t: (jnp.minimum(t, last), 0)
    tok3 = lambda t: (0, jnp.minimum(t, last), 0)
    col = lambda t: (0, jnp.maximum(t - last - 1, 0))
    return pl.pallas_call(
        functools.partial(post_bwd_kernel, blocks),
        grid=(2 * blocks + ff // d,),
        in_specs=[
            pl.BlockSpec((tb, d), lambda t: (jnp.minimum(t, blocks - 1), 0)),
            pl.BlockSpec((tb, d), lambda t: (jnp.clip(t - blocks, 0, blocks - 1), 0)),
            pl.BlockSpec((pairs, tb, 128), tok3),
            pl.BlockSpec((tb, d), tok), pl.BlockSpec((tb, d), tok), pl.BlockSpec((tb, ff), tok),
            pl.BlockSpec((tb, d), tok), pl.BlockSpec((tb, 128), tok),
            pl.BlockSpec((2 * n, d), col),
            whole(ow.shape), whole(ew.shape), whole(ct.shape), whole(vec.shape),
        ],
        out_specs=[
            pl.BlockSpec((tb, d), tok), pl.BlockSpec((pairs, tb, 128), tok3),
            pl.BlockSpec((16, tb), lambda t: (0, jnp.minimum(t, last))),
            whole((16, d)), whole(ow.shape),
            pl.BlockSpec((d, d), col), pl.BlockSpec((d, d), col),
        ],
        out_shape=[
            jax.ShapeDtypeStruct((2 * n, d), F32),
            jax.ShapeDtypeStruct((pairs, 2 * n, 128), BF),
            jax.ShapeDtypeStruct((16, 2 * n), F32),
            jax.ShapeDtypeStruct((16, d), F32),
            jax.ShapeDtypeStruct(ow.shape, BF),
            jax.ShapeDtypeStruct((d, ff), BF),
            jax.ShapeDtypeStruct((d, ff), BF),
        ],
        scratch_shapes=[
            pltpu.VMEM((d, d), BF), pltpu.VMEM((2 * n, ff), BF),
            pltpu.VMEM((d, 2 * n), BF), pltpu.VMEM((d, 2 * n), BF), pltpu.VMEM((d, 2 * n), BF),
            pltpu.VMEM((2 * n, d), BF),
        ],
        compiler_params=params(),
        name="post_bwd",
    )(gc, gq, ctx, xh1, nl, gp, xh2, rs, act, ow, ew, ct, vec)


def attn_bwd_kernel(rows_at, q, k, v, go, lse, delta, bias_t, mask_t, x, y, first, pw,
                    gx_o, gy_o, dp_o, bg_o, t8_o, pf, dq_s, dk_s, dv_s, diag, x_t):
    p = pl.program_id(0)
    n, d = x.shape
    pairs = d // 128
    wide = diag.shape[2]

    @pl.when(p == 0)
    def _():
        pf[...] = jnp.concatenate([pw[r] for r in range(pw.shape[0])], axis=1)
        x_t[:, :n] = x[...].T
        x_t[:, n:] = y[...].T

    @pl.when(p < pairs)
    def _():
        low = lax.broadcasted_iota(jnp.int32, (1, 128), 1) < 64
        qa, ga = q[0], go[0]
        qm = (jnp.where(low, qa, 0), jnp.where(low, 0, qa))
        gm = (jnp.where(low, ga, 0), jnp.where(low, 0, ga))
        dq = jnp.zeros((2 * n, 128), F32)
        diag[...] = jnp.zeros_like(diag)
        for lo in range(0, n, rows_at):
            at = slice(lo, lo + rows_at)
            ka, va = k[0, at], v[0, at]
            dk = jnp.zeros((rows_at, 128), F32)
            dv = jnp.zeros((rows_at, 128), F32)
            for hh in range(2):
                km = jnp.where(low, ka, 0) if hh == 0 else jnp.where(low, 0, ka)
                vm = jnp.where(low, va, 0) if hh == 0 else jnp.where(low, 0, va)
                lrow = lse[pl.ds(2 * p + hh, 1)]
                drow = delta[pl.ds(2 * p + hh, 1)]
                bias = bias_t[hh, at]
                both = jnp.concatenate([bias, bias], axis=1) + mask_t[at]
                sc = nt(km, qa) * (0.125 * LOG2E) + both
                pr = jnp.exp2(sc - lrow)
                ds = pr * (nt(vm, ga) - drow)
                dsb = ds.astype(BF)
                dv = dv + nn(pr.astype(BF), gm[hh])
                dk = dk + nn(dsb, qm[hh])
                dq = dq + tn(dsb, km)
                for b in range(0, rows_at, 128):
                    off = 384 - (lo + b)
                    diag[hh, :, off : off + n] += ds[b : b + 128, :n] + ds[b : b + 128, n:]
            dk_s[p, at] = (dk * 0.125).astype(BF)
            dv_s[p, at] = dv.astype(BF)
        dq_s[p] = (dq * 0.125).astype(BF)
        for hh in range(2):
            total = jnp.zeros((8, 2 * n), F32)
            for g in range(16):
                piece = jnp.concatenate([diag[hh, 8 * g : 8 * g + 8], jnp.zeros((8, 2 * n - wide), F32)], axis=1)
                total = total + (pltpu.roll(piece, 2 * n - 8 * g, 1) if g else piece)
            t8_o[hh] = total

    @pl.when(p == pairs)
    def _():
        cat = lambda ref, at: jnp.concatenate([ref[c, at] for c in range(pairs)], axis=1)
        gqc, gqq = cat(dq_s, slice(0, n)), cat(dq_s, slice(n, 2 * n))
        gk, gv = cat(dk_s, slice(0, n)), cat(dv_s, slice(0, n))
        gx_o[...] = first[:n] + nt(gqc, pf[:, :d]) + nt(gk, pf[:, d : 2 * d]) + nt(gv, pf[:, 2 * d :])
        gy_o[...] = first[n:] + nt(gqq, pf[:, :d])
        bg_o[...] = jnp.zeros_like(bg_o)
        bg_o[0:1] = rowsum(gqc.astype(F32)) + rowsum(gqq.astype(F32))
        bg_o[1:2] = rowsum(gv.astype(F32))
        xt = x_t[:, :n]
        grads = jnp.concatenate([
            nn(x_t[...], jnp.concatenate([gqc, gqq], axis=0)).astype(BF),
            nn(xt, gk).astype(BF), nn(xt, gv).astype(BF)], axis=1)
        w = dp_o.shape[2]
        for r in range(dp_o.shape[0]):
            dp_o[r] = grads[:, r * w : r * w + w]


def attn_bwd(q, k, v, go, lse, delta, bias_t, mask_t, x, y, first, pw, rows_at=256):
    n, d = x.shape
    pairs = d // 128
    pair = lambda p: (jnp.minimum(p, pairs - 1), 0, 0)
    return pl.pallas_call(
        functools.partial(attn_bwd_kernel, rows_at),
        grid=(pairs + 1,),
        in_specs=[
            pl.BlockSpec((1, 2 * n, 128), pair), pl.BlockSpec((1, n, 128), pair),
            pl.BlockSpec((1, n, 128), pair), pl.BlockSpec((1, 2 * n, 128), pair),
            whole(lse.shape), whole(delta.shape),
            pl.BlockSpec((2, n, n), pair), whole(mask_t.shape),
            whole(x.shape), whole(y.shape), whole(first.shape), whole(pw.shape),
        ],
        out_specs=[
            whole((n, d)), whole((n, d)), whole(pw.shape), whole((8, d)),
            pl.BlockSpec((2, 8, 2 * n), pair),
        ],
        out_shape=[
            jax.ShapeDtypeStruct((n, d), F32), jax.ShapeDtypeStruct((n, d), F32),
            jax.ShapeDtypeStruct(pw.shape, BF), jax.ShapeDtypeStruct((8, d), F32),
            jax.ShapeDtypeStruct((2 * pairs, 8, 2 * n), F32),
        ],
        scratch_shapes=[
            pltpu.VMEM((d, 3 * d), BF), pltpu.VMEM((pairs, 2 * n, 128), BF),
            pltpu.VMEM((pairs, n, 128), BF), pltpu.VMEM((pairs, n, 128), BF),
            pltpu.VMEM((2, 128, n + 384), F32), pltpu.VMEM((d, 2 * n), BF),
        ],
        compiler_params=params(),
        name="attn_bwd",
    )(q, k, v, go, lse, delta, bias_t, mask_t, x, y, first, pw)


def offset_sums(t8):
    heads, eight, n2 = t8.shape
    n = n2 // 2
    total = sum(jnp.roll(t8[:, r], -(384 + r), axis=1) for r in range(eight))
    return jnp.concatenate([total[:, 1:n][:, ::-1], total[:, :1], total[:, n + 1 :][:, ::-1]], axis=1)


def gather_layer(project, output, expand, contract, vectors):
    rows = lambda a, dim: lax.all_gather(a, "dp", axis=dim, tiled=True)
    pw = lax.all_gather(rows(project, 0), "rep", axis=0)
    ow = lax.all_gather(rows(output, 0), "rep", axis=0)
    ew = lax.all_gather(rows(expand, 0), "rep", axis=1, tiled=True)
    ct = lax.all_gather(rows(contract.T, 1), "rep", axis=0, tiled=True)
    vec = lax.all_gather(rows(vectors, 1), "rep", axis=0, tiled=True).astype(F32)
    return pw, ow, ew, ct, vec


def scatter_sum(a, rep_dim, dp_dim):
    a = lax.psum_scatter(a, "rep", scatter_dimension=rep_dim, tiled=True)
    return lax.psum_scatter(a, "dp", scatter_dimension=dp_dim, tiled=True).astype(F32)


def scatter_layer(dp, do, de, dc, vec):
    return (
        scatter_sum(dp, 0, 1)[0],
        scatter_sum(do, 0, 1)[0],
        scatter_sum(de, 1, 0),
        scatter_sum(dc, 0, 1).T,
        scatter_sum(vec, 0, 1),
    )


def shards(
    content_stream, query_stream, segments, perm_order, predicted, buckets, bias_table,
    project_one, output_one, expand_one, contract_one, vectors_one,
    project_two, output_two, expand_two, contract_two, vectors_two,
    content_cotangent, query_cotangent,
):
    shape = content_stream.shape
    n, d = shape[1:]
    flat = lambda a: a.reshape(n, d)
    selector, base, base_t = bias_bases(buckets, bias_table, n)
    marks = jnp.concatenate([segments, perm_order, predicted, jnp.zeros((5, n), jnp.int32)]).astype(F32)
    bias, bias_t, mask, mask_t = prep(base, base_t, marks)
    layers = (
        gather_layer(project_one, output_one, expand_one, contract_one, vectors_one),
        gather_layer(project_two, output_two, expand_two, contract_two, vectors_two),
    )
    x, y = flat(content_stream), flat(query_stream)
    kept = []
    for pw, ow, ew, ct, vec in layers:
        q, k, v, ctx, lse = attn_fwd(x, y, pw, vec, bias, mask)
        nx, ny, xh1, nl, act, gp, xh2, rs = post_fwd(x, y, ctx, ow, ew, ct, vec)
        kept.append((x, y, q, k, v, ctx, lse, xh1, nl, act, gp, xh2, rs))
        x, y = nx, ny
    gx, gy = flat(content_cotangent), flat(query_cotangent)
    grads, sums = [], []
    for (pw, ow, ew, ct, vec), saved in zip(layers[::-1], kept[::-1]):
        ix, iy, q, k, v, ctx, lse, xh1, nl, act, gp, xh2, rs = saved
        first, gctx, delta, vg, do, de, dc = post_bwd(gx, gy, ctx, xh1, nl, gp, xh2, rs, act, ow, ew, ct, vec)
        gx, gy, dp, bg, t8 = attn_bwd(q, k, v, gctx, lse, delta, bias_t, mask_t, ix, iy, first, pw)
        vg = jnp.concatenate([bg[:2], vg[2:12]], axis=0)
        grads.append(scatter_layer(dp, do, de, dc, vg))
        sums.append(t8)
    distances = offset_sums(sums[0] + sums[1])
    table = jnp.dot(selector.T, distances.T, precision=lax.Precision.HIGHEST)
    table = lax.psum(table, ("dp", "rep"))
    return (
        x.reshape(shape), y.reshape(shape), gx.reshape(shape), gy.reshape(shape), table,
        *grads[1], *grads[0],
    )


def solution(mesh):
    rows3, rows2 = P(("dp", "rep"), None, None), P(("dp", "rep"), None)
    weights = (P("dp", "rep"),) * 4 + (P("rep", "dp"),)
    return jax.shard_map(
        shards,
        mesh=mesh,
        in_specs=(rows3, rows3, rows2, rows2, rows2, P(), P(), *weights, *weights, rows3, rows3),
        out_specs=(rows3, rows3, rows3, rows3, P(), *weights, *weights),
        check_vma=False,
    )
```

```python
import functools
import jax
import jax.numpy as jnp
from jax import lax
from jax.experimental import pallas as pl
from jax.experimental.pallas import tpu as pltpu
from jax.sharding import PartitionSpec as P

F32 = jnp.float32
BF = jnp.bfloat16
LOG2E = 1.4426950408889634
NEG = -1e30
FLOOR = -1e29
VM = 60 * 1024 * 1024
NT = (((1,), (1,)), ((), ()))
TN = (((0,), (0,)), ((), ()))


def nt(a, b):
    return lax.dot_general(a, b, NT, preferred_element_type=F32)


def tn(a, b):
    return lax.dot_general(a, b, TN, preferred_element_type=F32)


def nn(a, b):
    return jnp.dot(a, b, preferred_element_type=F32)


def whole(shape):
    return pl.BlockSpec(shape, lambda *_: (0,) * len(shape))


def params(number=None):
    if number is None:
        return pltpu.CompilerParams(vmem_limit_bytes=VM)
    return pltpu.CompilerParams(vmem_limit_bytes=VM, collective_id=number, has_side_effects=True)


MESH = pl.DeviceIdType.MESH
ANY = pl.BlockSpec(memory_space=pl.ANY)
SEMS = 18


class Place:
    def __init__(self):
        self.dp = lax.axis_index("dp")
        self.rep = lax.axis_index("rep")
        self.z, self.x = self.dp // 2, self.dp % 2
        self.y, self.c = self.rep // 2, self.rep % 2
        self.dx, self.dy, self.dc = 1 - 2 * self.x, 2 - 4 * self.y, 1 - 2 * self.c
        self.across_x = (self.dp + self.dx, self.rep)
        self.across_y = (self.dp, self.rep + self.dy)
        self.other_core = (self.dp, self.rep + self.dc)

    def plane(self, k):
        return ((self.z + k) % 4, self.x)

    def to_plane(self, k):
        return (((self.z + k) % 4) * 2 + self.x, self.rep)

    def from_plane(self, k):
        return ((self.z + 4 - k) % 4) * 2 + self.x

    def greet(self):
        barrier = pltpu.get_barrier_semaphore()
        peers = [self.to_plane(k) for k in (1, 2, 3)] + [self.across_x, self.across_y, self.other_core]
        for peer in peers:
            pl.semaphore_signal(barrier, inc=1, device_id=peer, device_id_type=MESH)
        pl.semaphore_wait(barrier, len(peers))


def remote(src, dst, send, recv, peer):
    return pltpu.make_async_remote_copy(
        src_ref=src, dst_ref=dst, send_sem=send, recv_sem=recv, device_id=peer, device_id_type=MESH
    )


def block_of(full, rep, dp, rows, cols):
    if len(full.shape) == 3:
        return full.at[rep, pl.ds(pl.multiple_of(dp * rows, rows), rows)]
    return full.at[pl.ds(pl.multiple_of(rep * rows, rows), rows), pl.ds(pl.multiple_of(dp * cols, cols), cols)]


def half_of(full, rep, rows):
    if len(full.shape) == 3:
        return full.at[rep]
    return full.at[pl.ds(pl.multiple_of(rep * rows, rows), rows)]


def gather_ticks(shard, full, send, recv):
    me = Place()
    rows, cols = shard.shape
    blk = lambda rep, dp: block_of(full, rep, dp, rows, cols)
    rep_y = me.rep + me.dy
    src = lambda k: shard if k == 0 else blk(me.rep, me.from_plane(k))
    own = lambda k: blk(me.rep, me.from_plane(k))
    z_copy = lambda k: remote(shard, own(0), send.at[k - 1], recv.at[k - 1], me.to_plane(k))
    z_land = lambda k: remote(own(k), own(k), send.at[k - 1], recv.at[k - 1], me.to_plane(k))
    x_copy = lambda k: remote(src(k), own(k), send.at[3 + k], recv.at[3 + k], me.across_x)
    y_copy = lambda k: remote(src(k), own(k), send.at[7 + k], recv.at[7 + k], me.across_y)
    x_spot = lambda k: blk(me.rep, me.from_plane(k) + me.dx)
    y_spot = lambda k: blk(rep_y, me.from_plane(k))
    d_spot = lambda k: blk(rep_y, me.from_plane(k) + me.dx)
    x_land = lambda k: remote(x_spot(k), x_spot(k), send.at[3 + k], recv.at[3 + k], me.across_x)
    y_land = lambda k: remote(y_spot(k), y_spot(k), send.at[7 + k], recv.at[7 + k], me.across_y)
    d_land = lambda k: remote(d_spot(k), d_spot(k), send.at[11 + k], recv.at[11 + k], me.across_x)

    def d_copy(k):
        spot = blk(me.rep + (1 - me.c) * me.dy, me.from_plane(k) + me.c * me.dx)
        peer = (me.dp + (1 - me.c) * me.dx, me.rep + me.c * me.dy)
        return remote(spot, spot, send.at[11 + k], recv.at[11 + k], peer)

    mine = (half_of(full, me.rep, rows), half_of(full, rep_y, rows))
    theirs = (half_of(full, me.rep + me.dc, rows), half_of(full, rep_y + me.dc, rows))
    c_copy = lambda j: remote(mine[j], mine[j], send.at[15 + j], recv.at[15 + j], me.other_core)
    c_land = lambda j: remote(theirs[j], theirs[j], send.at[15 + j], recv.at[15 + j], me.other_core)
    place = lambda: pltpu.make_async_copy(shard, own(0), send.at[17])

    def begin():
        x_copy(0).start()
        y_copy(0).start()
        for k in (1, 3, 2):
            z_copy(k).start()
        place().start()

    def spread(k):
        z_land(k).wait_recv()
        x_copy(k).start()
        y_copy(k).start()

    def forward(k):
        x_land(k).wait_recv()
        y_land(k).wait_recv()
        d_copy(k).start()

    def swap():
        place().wait()
        for k in range(4):
            d_land(k).wait_recv()
        for j in range(2):
            c_copy(j).start()

    def end():
        for j in range(2):
            c_land(j).wait_recv()
        for k in range(4):
            if k:
                z_copy(k).wait_send()
            x_copy(k).wait_send()
            y_copy(k).wait_send()
            d_copy(k).wait_send()
        for j in range(2):
            c_copy(j).wait_send()

    def both(a, b):
        def run():
            spread(a)
            forward(b)
        return run

    return begin, [both(1, 0), both(3, 1), both(2, 3), lambda: forward(2), swap], end


class Gather:
    def __init__(self, shards):
        self.shards = list(shards)
        self.count = len(self.shards)

    def shapes(self):
        out = []
        for name, a in self.shards:
            rows, cols = a.shape
            shape = (4 * rows, 8 * cols) if name == "contract" else (4, 8 * rows, cols)
            out.append(jax.ShapeDtypeStruct(shape, a.dtype))
        return out

    def arrays(self):
        return [a for _, a in self.shards]

    def scratch(self):
        return [pltpu.SemaphoreType.DMA((max(self.count, 1), SEMS))] * 2 if self.count else []

    def plan(self, shards, fulls, sems):
        if not self.count:
            return (lambda: None), [], (lambda: None)
        parts = [gather_ticks(s, f, sems[0].at[i], sems[1].at[i]) for i, (s, f) in enumerate(zip(shards, fulls))]

        def begin():
            Place().greet()
            for part in parts:
                part[0]()

        def end():
            for part in parts:
                part[2]()

        return begin, [tick for part in parts for tick in part[1]], end


def scatter_ticks(g, parts, out, send, recv):
    held, other, diag, near, far, planes = parts
    me = Place()
    first = (me.dp + (1 - me.c) * me.dx, me.rep + me.c * me.dy)
    second = (me.dp + me.c * me.dx, me.rep + (1 - me.c) * me.dy)
    flip_y, flip_x = 1 - 2 * me.y, me.dx
    at_first = (me.y + me.c * flip_y, me.x + (1 - me.c) * flip_x)
    at_second = (me.y + (1 - me.c) * flip_y, me.x + me.c * flip_x)
    at_diag = (me.y + flip_y, me.x + flip_x)
    c_copy = lambda j: remote(g.at[2 * j + 1 - me.c], other.at[j], send.at[j], recv.at[j], me.other_core)
    load = lambda j: pltpu.make_async_copy(g.at[2 * j + me.c], held.at[j], send.at[2 + j])
    region = lambda at: held.at[at[0], :, at[1]]
    diag_copy = remote(region(at_diag), diag, send.at[4], recv.at[4], first)
    near_copy = remote(region(at_first), near, send.at[5], recv.at[5], first)
    far_copy = remote(region(at_second), far, send.at[6], recv.at[6], second)
    z_copy = lambda k: remote(
        held.at[me.y, (me.z + k) % 4, me.x], planes.at[k - 1], send.at[6 + k], recv.at[6 + k], me.to_plane(k)
    )

    def add(spot, *terms):
        total = held[spot].astype(F32)
        for ref, i in terms:
            total = total + ref[i].astype(F32)
        held[spot] = total.astype(held.dtype)

    def begin():
        for j in range(2):
            c_copy(j).start()
            load(j).start()

    def fold(j):
        def run():
            c_copy(j).wait_recv()
            load(j).wait()

            @pl.loop(0, 4)
            def _(zz):
                for xx in range(2):
                    add((j, zz, xx), (other, (j, zz, xx)))

            if j == 1:
                diag_copy.start()
                near_copy.start()
        return run

    def pass_on():
        diag_copy.wait_recv()

        @pl.loop(0, 4)
        def _(zz):
            add((at_second[0], zz, at_second[1]), (diag, zz))

        far_copy.start()

    def planes_out():
        near_copy.wait_recv()
        far_copy.wait_recv()

        @pl.loop(0, 4)
        def _(zz):
            add((me.y, zz, me.x), (near, zz), (far, zz))

        for k in (1, 3, 2):
            z_copy(k).start()

    def finish():
        total = held[me.y, me.z, me.x].astype(F32)
        for k in (1, 2, 3):
            z_copy(k).wait_recv()
            total = total + planes[k - 1].astype(F32)
        out[...] = total

    def end():
        for j in range(2):
            c_copy(j).wait_send()
        diag_copy.wait_send()
        near_copy.wait_send()
        far_copy.wait_send()
        for k in (1, 2, 3):
            z_copy(k).wait_send()

    return begin, [fold(0), fold(1), pass_on, planes_out, finish], end


class Scatter:
    def __init__(self, grads):
        self.grads = list(grads)
        self.count = len(self.grads)

    def out_shapes(self):
        return [jax.ShapeDtypeStruct(g.shape[3:], F32) for g in self.grads]

    def scratch(self):
        out = []
        for g in self.grads:
            a, b = g.shape[3:]
            for shape in ((2, 4, 2, a, b), (2, 4, 2, a, b), (4, a, b), (4, a, b), (4, a, b), (3, a, b)):
                out.append(pltpu.VMEM(shape, g.dtype))
        if self.count:
            out += [pltpu.SemaphoreType.DMA((self.count, 10))] * 2
        return out

    def plan(self, grads, outs, scratch):
        if not self.count:
            return (lambda: None), [], (lambda: None)
        send, recv = scratch[-2:]
        parts = [
            scatter_ticks(g, scratch[6 * i : 6 * i + 6], o, send.at[i], recv.at[i])
            for i, (g, o) in enumerate(zip(grads, outs))
        ]

        def begin():
            Place().greet()
            for part in parts:
                part[0]()

        def end():
            for part in parts:
                part[2]()

        order = sorted(
            ((i * 2 + s, i, s) for i in range(len(parts)) for s in range(5))
        )
        return begin, [parts[i][1][s] for _, i, s in order], end


def run_at(step, sub, subs, steps, first, ticks):
    points = steps * subs - first
    for s in range(steps):
        chosen = [t for i, t in enumerate(ticks) if first + min(i * points // max(len(ticks), 1), points - 1) == s * subs + sub]
        if chosen:
            @pl.when(step == s)
            def _():
                for t in chosen:
                    t()


def call(name, body, steps, ticked, subs, first, inputs, outputs, scratch, comm, number):
    gathers = isinstance(comm, Gather)
    extra_in = comm.arrays() if gathers else comm.grads
    extra_out = comm.shapes() if gathers else comm.out_shapes()
    count = comm.count

    def kernel(*refs):
        cut, at = [], 0
        for size in (len(inputs), count, len(outputs), count, len(scratch)):
            cut.append(refs[at : at + size])
            at += size
        ins, c_in, outs, c_out, own = cut
        step = pl.program_id(0)
        begin, ticks, end = comm.plan(c_in, c_out, refs[at:])
        if count:
            pl.when(step == 0)(begin)
        body(step, lambda sub: run_at(step, sub, subs, ticked, first, ticks), ins, outs, own)
        if count:
            pl.when(step == steps - 1)(end)

    return pl.pallas_call(
        kernel,
        grid=(steps,),
        in_specs=[spec for _, spec in inputs] + [ANY] * count,
        out_specs=[spec for _, spec in outputs] + [ANY if gathers else whole(s.shape) for s in extra_out],
        out_shape=[shape for shape, _ in outputs] + extra_out,
        scratch_shapes=scratch + comm.scratch(),
        compiler_params=params(number if count else None),
        name=name,
    )(*[a for a, _ in inputs], *extra_in)


def full(a):
    return a, whole(a.shape)


def shape_of(*dims, dtype=BF):
    return jax.ShapeDtypeStruct(dims, dtype)


def prep_body(step, tick, ins, outs, own):
    base, base_t, marks = ins
    bias, bias_t, mask, mask_t = outs
    n = bias.shape[1]
    tick(0)
    for src, dst in ((base, bias), (base_t, bias_t)):
        row = jnp.broadcast_to(src[0], (n, 2 * n))
        dst[0] = pltpu.roll(row, 0, 1, stride=1, stride_axis=0)[:, :n]

    @pl.when(step == 0)
    def _():
        rows = marks[...]
        seg_r, perm_r, pred_r = rows[0:1], rows[1:2], rows[2:3]
        for lo in range(0, n, 128):
            at = slice(lo, lo + 128)

            def col(k):
                piece = jnp.broadcast_to(rows[k : k + 1, at], (128, 128))
                return piece.T[:, :1]

            seg_c, perm_c, pred_c = col(0), col(1), col(2)
            same = (seg_c == seg_r) & (seg_r != 6.0)
            shown = pred_r == 0.0
            mask[0, at, :] = jnp.where(same & (shown | (perm_r <= perm_c)), 0.0, NEG)
            mask[1, at, :] = jnp.where(same & (shown | (perm_r < perm_c)), 0.0, NEG)
            same = (seg_c == seg_r) & (seg_c != 6.0)
            shown = pred_c == 0.0
            mask_t[at, :n] = jnp.where(same & (shown | (perm_c <= perm_r)), 0.0, NEG)
            mask_t[at, n:] = jnp.where(same & (shown | (perm_c < perm_r)), 0.0, NEG)


def prep(base, base_t, marks, comm, number):
    heads, n2 = base.shape
    n = n2 // 2
    row = pl.BlockSpec((1, 1, n2), lambda h: (h, 0, 0))
    grid = pl.BlockSpec((1, n, n), lambda h: (h, 0, 0))
    return call(
        "prep", prep_body, heads, heads, 1, 1,
        [(base.reshape(heads, 1, n2), row), (base_t.reshape(heads, 1, n2), row), full(marks)],
        [
            (shape_of(heads, n, n, dtype=F32), grid), (shape_of(heads, n, n, dtype=F32), grid),
            (shape_of(2, n, n, dtype=F32), whole((2, n, n))), (shape_of(n, n2, dtype=F32), whole((n, n2))),
        ],
        [], comm, number,
    )


def bias_bases(buckets, bias_table, n):
    selector = (buckets[:, None] == jnp.arange(bias_table.shape[0], dtype=jnp.int32)[None, :]).astype(F32)
    per_offset = jnp.dot(selector, bias_table.astype(F32), precision=lax.Precision.HIGHEST).T * LOG2E
    heads = per_offset.shape[0]
    zero = jnp.zeros((heads, 1), F32)
    base = jnp.concatenate([per_offset[:, n - 1 :], zero, per_offset[:, : n - 1]], axis=1)
    flipped = per_offset[:, ::-1]
    base_t = jnp.concatenate([flipped[:, n - 1 :], zero, flipped[:, : n - 1]], axis=1)
    return selector, base, base_t


def attn_fwd_body(step, tick, ins, outs, own):
    x, y, pw, vec, bias, mask = ins
    q_o, k_o, v_o, ctx_o, lse_o = outs
    pf, lse_s = own
    n, d = x.shape
    pairs = d // 128
    rows_at = n // 2
    p = step

    @pl.when(p == 0)
    def _():
        pf[...] = jnp.concatenate([pw[r] for r in range(pw.shape[0])], axis=1)
        bq, bv = vec[0:1], vec[1:2]
        xv = x[...]
        qc = nn(xv, pf[:, :d]) + bq
        qq = nn(y[...], pf[:, :d]) + bq
        kk = nn(xv, pf[:, d : 2 * d])
        vv = nn(xv, pf[:, 2 * d :]) + bv
        for c in range(pairs):
            at = slice(128 * c, 128 * c + 128)
            q_o[c, :n] = qc[:, at].astype(BF)
            q_o[c, n:] = qq[:, at].astype(BF)
            k_o[c] = kk[:, at].astype(BF)
            v_o[c] = vv[:, at].astype(BF)
        lse_s[...] = jnp.zeros_like(lse_s)

    k = k_o[p]
    v = v_o[p]
    lane = lax.broadcasted_iota(jnp.int32, (1, 128), 1)
    low = lane < 64
    vx = jnp.concatenate([v, jnp.ones_like(v)], axis=1)
    k0 = jnp.where(low, k, 0)
    k1 = jnp.where(low, 0, k)
    for s in range(2):
        for lo in range(0, n, rows_at):
            tick(2 * s + lo // rows_at)
            at = slice(lo, lo + rows_at)
            to = slice(s * n + lo, s * n + lo + rows_at)
            q = q_o[p, to]
            parts = []
            for hh, kh in ((0, k0), (1, k1)):
                sc = nt(q, kh) * (0.125 * LOG2E) + (bias[hh, at] + mask[s, at])
                m = jnp.maximum(jnp.max(sc, axis=-1, keepdims=True), FLOOR)
                e = jnp.exp2(sc - m).astype(BF)
                r = nn(e, vx)
                tot = r[:, 128:]
                tot = jnp.where(tot > 0, tot, 1.0)
                lse = m + jnp.log2(tot)
                lse_s[to] = jnp.where(lane == 2 * p + hh, lse, lse_s[to])
                parts.append(r[:, :128] / tot)
            ctx_o[0, to] = jnp.where(low, parts[0], parts[1]).astype(BF)

    @pl.when(p == pairs - 1)
    def _():
        for lo in range(0, 2 * n, 128):
            lse_o[:, lo : lo + 128] = lse_s[lo : lo + 128].T[: lse_o.shape[0]]


def attn_fwd(x, y, pw, vec, bias, mask, comm, number):
    n, d = x.shape
    pairs = d // 128
    return call(
        "attn_fwd", attn_fwd_body, pairs, pairs, 4, 2,
        [full(x), full(y), full(pw), full(vec), (bias, pl.BlockSpec((2, n, n), lambda p: (p, 0, 0))), full(mask)],
        [
            (shape_of(pairs, 2 * n, 128), whole((pairs, 2 * n, 128))),
            (shape_of(pairs, n, 128), whole((pairs, n, 128))),
            (shape_of(pairs, n, 128), whole((pairs, n, 128))),
            (shape_of(pairs, 2 * n, 128), pl.BlockSpec((1, 2 * n, 128), lambda p: (p, 0, 0))),
            (shape_of(16, 2 * n, dtype=F32), whole((16, 2 * n))),
        ],
        [pltpu.VMEM((d, 3 * d), BF), pltpu.VMEM((2 * n, 128), F32)],
        comm, number,
    )


def gelu_parts(z):
    e = jnp.exp2(z * z * (-0.5 * LOG2E))
    den = 1.0 + (0.3275911 * 0.7071067811865476) * jnp.abs(z)
    t = pl.reciprocal(den, approx=True)
    t = t * (2.0 - den * t)
    poly = t * (0.127414796 + t * (-0.142248368 + t * (0.7107068705 + t * (-0.7265760135 + t * 0.5307027145))))
    tail = poly * e
    phi = jnp.where(z < 0, tail, 1.0 - tail)
    return z * phi, phi + z * (e * 0.3989422804014327)


def moments(v):
    centered = v - jnp.mean(v, axis=-1, keepdims=True)
    rs = lax.rsqrt(jnp.mean(centered * centered, axis=-1, keepdims=True) + 1e-05)
    return centered * rs, rs


def post_fwd_body(step, tick, ins, outs, own):
    x, y, ctx, ow, ew, ct, vec = ins
    rc_o, rq_o, xh1_o, nl_o, act_o, gp_o, xh2_o, rs_o = outs
    (of,) = own
    t = step
    d = x.shape[1]
    fw = ew.shape[2]
    blocks = ew.shape[0] // 2

    @pl.when(t == 0)
    def _():
        of[...] = jnp.concatenate([ow[r] for r in range(ow.shape[0])], axis=1)

    z = jnp.where(t < blocks, x[...].astype(F32), y[...].astype(F32))
    cx = jnp.concatenate([ctx[c] for c in range(ctx.shape[0])], axis=1)
    first = z + (nn(cx, of[...]) + vec[2:3])
    xh1, rs1 = moments(first)
    normed = xh1 * vec[3:4] + vec[4:5]
    nl = normed.astype(BF)
    xh1_o[...] = xh1.astype(BF)
    nl_o[...] = nl
    second = normed + vec[5:6]
    for f in range(ew.shape[0]):
        tick(f)
        at = slice(f * fw, f * fw + fw)
        h = nn(nl, ew[f]) + vec[8 + f : 9 + f]
        act, gp = gelu_parts(h)
        act = act.astype(BF)
        act_o[:, at] = act
        gp_o[:, at] = gp.astype(BF)
        second = second + nt(act, ct[:, at])
    xh2, rs2 = moments(second)
    xh2_o[...] = xh2.astype(BF)
    lane = lax.broadcasted_iota(jnp.int32, (1, 128), 1)
    rs_o[...] = jnp.where(lane < 64, rs1, rs2)
    res = (xh2 * vec[6:7] + vec[7:8]).astype(BF)

    @pl.when(t < blocks)
    def _():
        rc_o[...] = res

    @pl.when(t >= blocks)
    def _():
        rq_o[...] = res


def post_fwd(x, y, ctx, ow, ew, ct, vec, comm, number):
    n, d = x.shape
    ff = ct.shape[1]
    pairs = ctx.shape[0]
    blocks = ew.shape[0] // 2
    tb = n // blocks
    early = pl.BlockSpec((tb, d), lambda t: (jnp.minimum(t, blocks - 1), 0))
    late = pl.BlockSpec((tb, d), lambda t: (jnp.maximum(t - blocks, 0), 0))
    row = lambda width: pl.BlockSpec((tb, width), lambda t: (t, 0))
    return call(
        "post_fwd", post_fwd_body, 2 * blocks, 2 * blocks, ew.shape[0], 1,
        [
            (x, early), (y, late), (ctx, pl.BlockSpec((pairs, tb, 128), lambda t: (0, t, 0))),
            full(ow), full(ew), full(ct), full(vec),
        ],
        [
            (shape_of(n, d), early), (shape_of(n, d), late), (shape_of(2 * n, d), row(d)), (shape_of(2 * n, d), row(d)),
            (shape_of(2 * n, ff), row(ff)), (shape_of(2 * n, ff), row(ff)), (shape_of(2 * n, d), row(d)),
            (shape_of(2 * n, 128, dtype=F32), row(128)),
        ],
        [pltpu.VMEM((d, d), BF)],
        comm, number,
    )


def norm_back(g, xh, rs, gain):
    a = g * gain
    return rs * (a - jnp.mean(a, axis=-1, keepdims=True) - xh * jnp.mean(a * xh, axis=-1, keepdims=True))


def rowsum(v):
    return jnp.sum(v, axis=0, keepdims=True)


def post_bwd_body(step, tick, ins, outs, own):
    gc, gq, ctx, xh1, nl, gp, xh2, rs, act, ow, ew, ct, vec = ins
    first_o, gctx_o, vg_o, do_o, de_o, dc_o = outs
    of, gh_s, nl_t, gf_t, cx_t, ga_s = own
    t = step
    tb, d = gc.shape
    chunks, fw = ew.shape[0], ew.shape[2]
    blocks = chunks // 2

    @pl.when(t == 0)
    def _():
        of[...] = jnp.concatenate([ow[r] for r in range(ow.shape[0])], axis=1)
        vg_o[...] = jnp.zeros_like(vg_o)

    tick(0)

    @pl.when(t < 2 * blocks)
    def _():
        g = jnp.where(t < blocks, gc[...].astype(F32), gq[...].astype(F32))
        rs1, rs2 = rs[:, :1], rs[:, 64:65]
        xh = xh2[...].astype(F32)
        vg_o[6:7] += rowsum(g * xh)
        vg_o[7:8] += rowsum(g)
        gs = norm_back(g, xh, rs2, vec[6:7])
        gf = gs.astype(BF)
        vg_o[5:6] += rowsum(gf.astype(F32))
        gn = gs
        spot = pl.ds(pl.multiple_of(t * tb, tb), tb)
        for f in range(chunks):
            at = slice(f * fw, f * fw + fw)
            gh = (nn(gf, ct[:, at]) * gp[:, at].astype(F32)).astype(BF)
            gh_s[f, spot] = gh
            vg_o[8 + f : 9 + f] += rowsum(gh.astype(F32))
            gn = gn + nt(gh, ew[f])
        xh = xh1[...].astype(F32)
        vg_o[3:4] += rowsum(gn * xh)
        vg_o[4:5] += rowsum(gn)
        first = norm_back(gn, xh, rs1, vec[3:4])
        first_o[...] = first
        ga = first.astype(BF)
        vg_o[2:3] += rowsum(ga.astype(F32))
        ga_s[spot] = ga
        gx = nt(ga, of[...]).astype(BF)
        cx = jnp.concatenate([ctx[c] for c in range(ctx.shape[0])], axis=1)
        for c in range(ctx.shape[0]):
            gctx_o[c] = gx[:, 128 * c : 128 * c + 128]
        nl_t[:, spot] = nl[...].T
        gf_t[:, spot] = gf.T
        cx_t[:, spot] = cx.T

    @pl.when(t == 2 * blocks)
    def _():
        do = nn(cx_t[...], ga_s[...])
        w = do_o.shape[2]
        for r in range(do_o.shape[0]):
            do_o[r] = do[:, r * w : r * w + w].astype(BF)

    @pl.when(t >= 2 * blocks)
    def _():
        de_o[0] = nn(nl_t[...], gh_s[t - 2 * blocks]).astype(BF)
        dc = nn(gf_t[...], act[...]).astype(BF)
        if len(dc_o.shape) == 2:
            dc_o[...] = dc
        else:
            reps, across, a, b = dc_o.shape
            for r in range(reps):
                for x in range(across):
                    dc_o[r, x] = dc[a * r : a * r + a, b * x : b * x + b]


def post_bwd(gc, gq, ctx, xh1, nl, gp, xh2, rs, act, ow, ew, ct, vec, comm, number, split):
    n, d = gc.shape
    chunks, fw = ew.shape[0], ew.shape[2]
    ff = chunks * fw
    pairs = ctx.shape[0]
    blocks = chunks // 2
    tb = n // blocks
    last = 2 * blocks - 1
    tok = lambda width: pl.BlockSpec((tb, width), lambda t: (jnp.minimum(t, last), 0))
    tok3 = pl.BlockSpec((pairs, tb, 128), lambda t: (0, jnp.minimum(t, last), 0))
    part = lambda t: jnp.maximum(t - last - 1, 0)
    if split:
        reps, owners = split
        across = owners // chunks
        dc = (
            shape_of(reps, owners, d // reps, ff // owners),
            pl.BlockSpec((reps, across, d // reps, ff // owners), lambda t: (0, part(t), 0, 0)),
        )
    else:
        dc = shape_of(d, ff), pl.BlockSpec((d, fw), lambda t: (0, part(t)))
    return call(
        "post_bwd", post_bwd_body, 2 * blocks + chunks, 2 * blocks + chunks, 1, 1,
        [
            (gc, pl.BlockSpec((tb, d), lambda t: (jnp.minimum(t, blocks - 1), 0))),
            (gq, pl.BlockSpec((tb, d), lambda t: (jnp.clip(t - blocks, 0, blocks - 1), 0))),
            (ctx, tok3), (xh1, tok(d)), (nl, tok(d)), (gp, tok(ff)), (xh2, tok(d)), (rs, tok(128)),
            (act, pl.BlockSpec((2 * n, fw), lambda t: (0, part(t)))),
            full(ow), full(ew), full(ct), full(vec),
        ],
        [
            (shape_of(2 * n, d, dtype=F32), tok(d)), (shape_of(pairs, 2 * n, 128), tok3),
            (shape_of(16, d, dtype=F32), whole((16, d))), (shape_of(*ow.shape), whole(ow.shape)),
            (shape_of(chunks, d, fw), pl.BlockSpec((1, d, fw), lambda t: (part(t), 0, 0))), dc,
        ],
        [
            pltpu.VMEM((d, d), BF), pltpu.VMEM((chunks, 2 * n, fw), BF),
            pltpu.VMEM((d, 2 * n), BF), pltpu.VMEM((d, 2 * n), BF), pltpu.VMEM((d, 2 * n), BF),
            pltpu.VMEM((2 * n, d), BF),
        ],
        comm, number,
    )


def attn_bwd_body(step, tick, ins, outs, own):
    q, k, v, go, lse, bias_t, mask_t, x, y, first, pw = ins
    gx_o, gy_o, dp_o, bg_o, t8_o = outs
    pf, dq_s, dk_s, dv_s, diag, x_t, dk_a, dv_a = own
    p = step
    n, d = x.shape
    pairs = d // 128
    wide = diag.shape[2]
    cols = n // 2

    @pl.when(p == 0)
    def _():
        pf[...] = jnp.concatenate([pw[r] for r in range(pw.shape[0])], axis=1)
        x_t[:, :n] = x[...].T
        x_t[:, n:] = y[...].T

    @pl.when(p < pairs)
    def _():
        low = lax.broadcasted_iota(jnp.int32, (1, 128), 1) < 64
        only = lambda a, hh: jnp.where(low, a, 0) if hh == 0 else jnp.where(low, 0, a)
        diag[...] = jnp.zeros_like(diag)
        ka, va = k[0], v[0]
        for i, lo in enumerate(range(0, 2 * n, cols)):
            tick(i)
            at = slice(lo, lo + cols)
            i0 = lo % n
            qa, ga = q[0, at], go[0, at]
            dq = dk = dv = None
            for hh in range(2):
                km, vm = only(ka, hh), only(va, hh)
                lrow = lse[pl.ds(2 * p + hh, 1), at]
                sc = nt(km, qa) * (0.125 * LOG2E) + (bias_t[hh, :, i0 : i0 + cols] + mask_t[:, at])
                pr = jnp.exp2(sc - lrow)
                gp = nt(vm, ga)
                ds = pr * (gp - rowsum(pr * gp))
                dsb = ds.astype(BF)
                dv_h = nn(pr.astype(BF), only(ga, hh))
                dk_h = nn(dsb, only(qa, hh))
                dq_h = tn(dsb, km)
                dq, dk, dv = (dq_h, dk_h, dv_h) if hh == 0 else (dq + dq_h, dk + dk_h, dv + dv_h)
                for b in range(n // 128):
                    off = n - 128 - 128 * b + i0
                    diag[hh, :, off : off + cols] += ds[128 * b : 128 * b + 128]
            dq_s[p, at] = (dq * 0.125).astype(BF)
            if i == 0:
                dk_a[...] = dk
                dv_a[...] = dv
            else:
                dk_a[...] += dk
                dv_a[...] += dv
        dk_s[p] = (dk_a[...] * 0.125).astype(BF)
        dv_s[p] = dv_a[...].astype(BF)
        for hh in range(2):
            total = jnp.zeros((8, 2 * n), F32)
            for g in range(16):
                piece = jnp.concatenate([diag[hh, 8 * g : 8 * g + 8], jnp.zeros((8, 2 * n - wide), F32)], axis=1)
                total = total + (pltpu.roll(piece, 2 * n - 8 * g, 1) if g else piece)
            t8_o[hh] = total

    @pl.when(p == pairs)
    def _():
        cat = lambda ref, at: jnp.concatenate([ref[c, at] for c in range(pairs)], axis=1)
        gqc, gqq = cat(dq_s, slice(0, n)), cat(dq_s, slice(n, 2 * n))
        gk, gv = cat(dk_s, slice(0, n)), cat(dv_s, slice(0, n))
        gx_o[...] = first[:n] + nt(gqc, pf[:, :d]) + nt(gk, pf[:, d : 2 * d]) + nt(gv, pf[:, 2 * d :])
        gy_o[...] = first[n:] + nt(gqq, pf[:, :d])
        bg_o[...] = jnp.zeros_like(bg_o)
        bg_o[0:1] = rowsum(gqc.astype(F32)) + rowsum(gqq.astype(F32))
        bg_o[1:2] = rowsum(gv.astype(F32))
        xt = x_t[:, :n]
        grads = jnp.concatenate([
            nn(x_t[...], jnp.concatenate([gqc, gqq], axis=0)).astype(BF),
            nn(xt, gk).astype(BF), nn(xt, gv).astype(BF)], axis=1)
        w = dp_o.shape[2]
        for r in range(dp_o.shape[0]):
            dp_o[r] = grads[:, r * w : r * w + w]


def attn_bwd(q, k, v, go, lse, bias_t, mask_t, x, y, first, pw, comm, number):
    n, d = x.shape
    pairs = d // 128
    pair = lambda *block: pl.BlockSpec(block, lambda p: (jnp.minimum(p, pairs - 1), 0, 0))
    return call(
        "attn_bwd", attn_bwd_body, pairs + 1, pairs, 4, 2,
        [
            (q, pair(1, 2 * n, 128)), (k, pair(1, n, 128)), (v, pair(1, n, 128)), (go, pair(1, 2 * n, 128)),
            full(lse), (bias_t, pair(2, n, n)), full(mask_t), full(x), full(y), full(first), full(pw),
        ],
        [
            (shape_of(n, d, dtype=F32), whole((n, d))), (shape_of(n, d, dtype=F32), whole((n, d))),
            (shape_of(*pw.shape), whole(pw.shape)), (shape_of(8, d, dtype=F32), whole((8, d))),
            (shape_of(2 * pairs, 8, 2 * n, dtype=F32), pair(2, 8, 2 * n)),
        ],
        [
            pltpu.VMEM((d, 3 * d), BF), pltpu.VMEM((pairs, 2 * n, 128), BF),
            pltpu.VMEM((pairs, n, 128), BF), pltpu.VMEM((pairs, n, 128), BF),
            pltpu.VMEM((2, 128, 2 * n - 128), F32), pltpu.VMEM((d, 2 * n), BF),
            pltpu.VMEM((n, 128), F32), pltpu.VMEM((n, 128), F32),
        ],
        comm, number,
    )


def offset_sums(t8, n):
    total = sum(jnp.roll(t8[:, r], -(n - 128 + r), axis=1) for r in range(t8.shape[1]))
    return jnp.concatenate([total[:, 1:n][:, ::-1], total[:, :1], total[:, n + 1 :][:, ::-1]], axis=1)


def tail_kernel(comm, *refs):
    count = comm.count
    ins, outs, scratch = refs[:count], refs[count : 2 * count], refs[2 * count :]
    begin, ticks, end = comm.plan(ins, outs, scratch)
    begin()
    for tick in ticks:
        tick()
    end()


def tail(comm, number):
    return pl.pallas_call(
        functools.partial(tail_kernel, comm),
        in_specs=[ANY] * comm.count,
        out_specs=[pl.BlockSpec(memory_space=pltpu.VMEM)] * comm.count,
        out_shape=comm.out_shapes(),
        scratch_shapes=comm.scratch(),
        compiler_params=params(number),
        name="tail",
    )(*comm.grads)


NAMES = ("project", "output", "expand", "contract")


def vector_block(vectors):
    rows, cols = vectors.shape
    return jnp.pad(vectors, ((0, 8 - rows), (0, 128 - cols)))


def vectors_whole(gathered, lo, rows, cols):
    part = gathered.reshape(4, 8, 16, 128)[:, :, lo : lo + rows, :cols]
    return part.transpose(0, 2, 1, 3).reshape(4 * rows, 8 * cols).astype(F32)


def plain_gather(project, output, expand, contract, vectors):
    rows = lambda a, dim: lax.all_gather(a, "dp", axis=dim, tiled=True)
    pw = lax.all_gather(rows(project, 0), "rep", axis=0)
    ow = lax.all_gather(rows(output, 0), "rep", axis=0)
    ew = lax.all_gather(rows(expand, 0), "rep", axis=0)
    ct = lax.all_gather(rows(contract, 1), "rep", axis=0, tiled=True)
    vec = lax.all_gather(rows(vectors, 1), "rep", axis=0, tiled=True).astype(F32)
    return pw, ow, ew, ct, vec


def scatter_sum(a, rep_dim, dp_dim):
    a = lax.psum_scatter(a, "rep", scatter_dimension=rep_dim, tiled=True)
    return lax.psum_scatter(a, "dp", scatter_dimension=dp_dim, tiled=True).astype(F32)


def shards(
    square,
    content_stream, query_stream, segments, perm_order, predicted, buckets, bias_table,
    project_one, output_one, expand_one, contract_one, vectors_one,
    project_two, output_two, expand_two, contract_two, vectors_two,
    content_cotangent, query_cotangent,
):
    shape = content_stream.shape
    n, d = shape[1:]
    flat = lambda a: a.reshape(n, d)
    selector, base, base_t = bias_bases(buckets, bias_table, n)
    marks = jnp.concatenate([segments, perm_order, predicted, jnp.zeros((5, n), jnp.int32)]).astype(F32)
    one = (project_one, output_one, expand_one, contract_one.T, vectors_one)
    two = (project_two, output_two, expand_two, contract_two.T, vectors_two)
    none = Gather([])
    pick = lambda weights, names: Gather([(k, weights[NAMES.index(k)]) for k in names])
    x, y = flat(content_stream), flat(query_stream)
    ins = [(x, y)]
    if square:
        rows, cols = vectors_one.shape
        both = jnp.concatenate([vector_block(vectors_one), vector_block(vectors_two)], axis=0)
        bias, bias_t, mask, mask_t, pw, vecs = prep(
            base, base_t, marks, Gather([("project", project_one), ("vectors", both)]), 1
        )
        vec_one, vec_two = (vectors_whole(vecs, lo, rows, cols) for lo in (0, 8))
        *att_one, ow, ew, ct = attn_fwd(x, y, pw, vec_one, bias, mask, pick(one, NAMES[1:]), 2)
        full_one = (pw, ow, ew, ct, vec_one)
        *post_one, pw, ow = post_fwd(x, y, att_one[3], ow, ew, ct, vec_one, pick(two, NAMES[:2]), 3)
        x, y = post_one[:2]
        ins.append((x, y))
        *att_two, ew, ct = attn_fwd(x, y, pw, vec_two, bias, mask, pick(two, NAMES[2:]), 4)
        full_two = (pw, ow, ew, ct, vec_two)
        post_two = post_fwd(x, y, att_two[3], ow, ew, ct, vec_two, none, 0)
    else:
        bias, bias_t, mask, mask_t = prep(base, base_t, marks, none, 0)
        full_one, full_two = plain_gather(*one), plain_gather(*two)
        pw, ow, ew, ct, vec = full_one
        att_one = attn_fwd(x, y, pw, vec, bias, mask, none, 0)
        post_one = post_fwd(x, y, att_one[3], ow, ew, ct, vec, none, 0)
        x, y = post_one[:2]
        ins.append((x, y))
        pw, ow, ew, ct, vec = full_two
        att_two = attn_fwd(x, y, pw, vec, bias, mask, none, 0)
        post_two = post_fwd(x, y, att_two[3], ow, ew, ct, vec, none, 0)

    def back_post(gx, gy, weights, att, post, comm, number):
        pw, ow, ew, ct, vec = weights
        xh1, nl, act, gp, xh2, rs = post[2:]
        split = (4, 8) if square else None
        return post_bwd(gx, gy, att[3], xh1, nl, gp, xh2, rs, act, ow, ew, ct, vec, comm, number, split)

    def back_attn(gctx, first, weights, att, inputs, comm, number):
        q, k, v, ctx, lse = att
        return attn_bwd(q, k, v, gctx, lse, bias_t, mask_t, *inputs, first, weights[0], comm, number)

    empty = Scatter([])
    pieces = lambda a: a.reshape(4, 4, 2, a.shape[-2] if a.ndim == 4 else a.shape[1] // 8, a.shape[-1])
    sent = lambda *arrays: Scatter([pieces(a) for a in arrays]) if square else empty
    first, gctx, vg_two, do_two, de_two, dc_two, *_ = back_post(
        flat(content_cotangent), flat(query_cotangent), full_two, att_two, post_two, empty, 0
    )
    gx, gy, dp_two, bg_two, t8_two, *out_two = back_attn(
        gctx, first, full_two, att_two, ins[1], sent(do_two, de_two, dc_two), 5
    )
    first, gctx, vg_one, do_one, de_one, dc_one, *out_p2 = back_post(
        gx, gy, full_one, att_one, post_one, sent(dp_two), 6
    )
    gx, gy, dp_one, bg_one, t8_one, *out_one = back_attn(
        gctx, first, full_one, att_one, ins[0], sent(do_one, de_one, dc_one), 7
    )
    vg_one = jnp.concatenate([bg_one[:2], vg_one[2:12]], axis=0)
    vg_two = jnp.concatenate([bg_two[:2], vg_two[2:12]], axis=0)
    distances = offset_sums(t8_one + t8_two, n)
    table = jnp.dot(selector.T, distances.T, precision=lax.Precision.HIGHEST)
    table = lax.psum(table, ("dp", "rep"))
    if square:
        vgs = jnp.stack([vg_one, vg_two]).reshape(2, 4, rows, 8, cols).transpose(1, 3, 0, 2, 4)
        vgs = jnp.pad(vgs.reshape(4, 8, 2 * rows, cols), ((0, 0), (0, 0), (0, 8 - 2 * rows), (0, 128 - cols)))
        out_p1, vecs = tail(Scatter([pieces(dp_one), pieces(vgs)]), 8)
        grads_one = (out_p1, out_one[0], out_one[1], out_one[2].T, vecs[:rows, :cols])
        grads_two = (out_p2[0], out_two[0], out_two[1], out_two[2].T, vecs[rows : 2 * rows, :cols])
    else:
        spread = lambda dp, do, de, dc, vec: (
            scatter_sum(dp, 0, 1)[0], scatter_sum(do, 0, 1)[0], scatter_sum(de, 0, 1)[0],
            scatter_sum(dc, 0, 1).T, scatter_sum(vec, 0, 1),
        )
        grads_one = spread(dp_one, do_one, de_one, dc_one, vg_one)
        grads_two = spread(dp_two, do_two, de_two, dc_two, vg_two)
    return (
        post_two[0].reshape(shape), post_two[1].reshape(shape), gx.reshape(shape), gy.reshape(shape), table,
        *grads_one, *grads_two,
    )


def solution(mesh):
    rows3, rows2 = P(("dp", "rep"), None, None), P(("dp", "rep"), None)
    weights = (P("dp", "rep"),) * 4 + (P("rep", "dp"),)
    square = mesh.shape["dp"] == 8 and mesh.shape["rep"] == 4
    return jax.shard_map(
        functools.partial(shards, square),
        mesh=mesh,
        in_specs=(rows3, rows3, rows2, rows2, rows2, P(), P(), *weights, *weights, rows3, rows3),
        out_specs=(rows3, rows3, rows3, rows3, P(), *weights, *weights),
        check_vma=False,
    )
```

```python
import functools
import types
import jax
import jax.numpy as jnp
from jax import lax
from jax.experimental import pallas as pl
from jax.experimental.pallas import tpu as pltpu
from jax.sharding import PartitionSpec as P

F32 = jnp.float32
BF = jnp.bfloat16
LOG2E = 1.4426950408889634
NEG = -1e30
FLOOR = -1e29
VM = 60 * 1024 * 1024
NT = (((1,), (1,)), ((), ()))
TN = (((0,), (0,)), ((), ()))


def nt(a, b):
    return lax.dot_general(a, b, NT, preferred_element_type=F32)


def tn(a, b):
    return lax.dot_general(a, b, TN, preferred_element_type=F32)


def nn(a, b):
    return jnp.dot(a, b, preferred_element_type=F32)


def whole(shape):
    return pl.BlockSpec(shape, lambda *_: (0,) * len(shape))


def params(number=None):
    if number is None:
        return pltpu.CompilerParams(vmem_limit_bytes=VM)
    return pltpu.CompilerParams(vmem_limit_bytes=VM, collective_id=number, has_side_effects=True)


MESH = pl.DeviceIdType.MESH
ANY = pl.BlockSpec(memory_space=pl.ANY)
SEMS = 24


class Place:
    def __init__(self):
        self.dp = lax.axis_index("dp")
        self.rep = lax.axis_index("rep")
        self.z, self.x = self.dp // 2, self.dp % 2
        self.y, self.c = self.rep // 2, self.rep % 2
        self.dx, self.dy, self.dc = 1 - 2 * self.x, 2 - 4 * self.y, 1 - 2 * self.c
        self.across_x = (self.dp + self.dx, self.rep)
        self.across_y = (self.dp, self.rep + self.dy)
        self.other_core = (self.dp, self.rep + self.dc)

    def plane(self, k):
        return ((self.z + k) % 4, self.x)

    def to_plane(self, k):
        return (((self.z + k) % 4) * 2 + self.x, self.rep)

    def from_plane(self, k):
        return ((self.z + 4 - k) % 4) * 2 + self.x

    def greet(self):
        barrier = pltpu.get_barrier_semaphore()
        peers = [self.to_plane(k) for k in (1, 2, 3)] + [self.across_x, self.across_y, self.other_core]
        for peer in peers:
            pl.semaphore_signal(barrier, inc=1, device_id=peer, device_id_type=MESH)
        pl.semaphore_wait(barrier, len(peers))


def remote(src, dst, send, recv, peer):
    return pltpu.make_async_remote_copy(
        src_ref=src, dst_ref=dst, send_sem=send, recv_sem=recv, device_id=peer, device_id_type=MESH
    )


def block_of(full, rep, dp, rows, cols):
    if len(full.shape) == 3:
        return full.at[rep, pl.ds(pl.multiple_of(dp * rows, rows), rows)]
    return full.at[pl.ds(pl.multiple_of(rep * rows, rows), rows), pl.ds(pl.multiple_of(dp * cols, cols), cols)]


def plane_of(full, rep, z, rows, cols):
    if len(full.shape) == 3:
        return full.at[rep, pl.ds(pl.multiple_of(z * 2 * rows, 2 * rows), 2 * rows)]
    lanes = pl.ds(pl.multiple_of(z * 2 * cols, 2 * cols), 2 * cols)
    return full.at[pl.ds(pl.multiple_of(rep * rows, rows), rows), lanes]


def gather_steps(shard, full, send, recv):
    me = Place()
    rows, cols = shard.shape
    blk = lambda rep, dp: block_of(full, rep, dp, rows, cols)
    rep_y = me.rep + me.dy
    src = lambda k: shard if k == 0 else blk(me.rep, me.from_plane(k))
    own = lambda k: blk(me.rep, me.from_plane(k))
    z_copy = lambda k: remote(shard, own(0), send.at[k - 1], recv.at[k - 1], me.to_plane(k))
    z_land = lambda k: remote(own(k), own(k), send.at[k - 1], recv.at[k - 1], me.to_plane(k))
    x_copy = lambda k: remote(src(k), own(k), send.at[3 + k], recv.at[3 + k], me.across_x)
    y_copy = lambda k: remote(src(k), own(k), send.at[7 + k], recv.at[7 + k], me.across_y)
    x_spot = lambda k: blk(me.rep, me.from_plane(k) + me.dx)
    y_spot = lambda k: blk(rep_y, me.from_plane(k))
    d_spot = lambda k: blk(rep_y, me.from_plane(k) + me.dx)
    x_land = lambda k: remote(x_spot(k), x_spot(k), send.at[3 + k], recv.at[3 + k], me.across_x)
    y_land = lambda k: remote(y_spot(k), y_spot(k), send.at[7 + k], recv.at[7 + k], me.across_y)
    d_land = lambda k: remote(d_spot(k), d_spot(k), send.at[11 + k], recv.at[11 + k], me.across_x)

    def d_copy(k):
        spot = blk(me.rep + (1 - me.c) * me.dy, me.from_plane(k) + me.c * me.dx)
        peer = (me.dp + (1 - me.c) * me.dx, me.rep + me.c * me.dy)
        return remote(spot, spot, send.at[11 + k], recv.at[11 + k], peer)

    pair = lambda rep, k: plane_of(full, rep, (me.z + 4 - k) % 4, rows, cols)
    mine = lambda j, k: pair(rep_y if j else me.rep, k)
    theirs = lambda j, k: pair((rep_y if j else me.rep) + me.dc, k)
    c_copy = lambda j, k: remote(mine(j, k), mine(j, k), send.at[15 + 4 * j + k], recv.at[15 + 4 * j + k], me.other_core)
    c_land = lambda j, k: remote(
        theirs(j, k), theirs(j, k), send.at[15 + 4 * j + k], recv.at[15 + 4 * j + k], me.other_core
    )
    place = lambda k: pltpu.make_async_copy(shard, own(k), send.at[23 + k])

    def spread(k):
        z_land(k).wait_recv()
        x_copy(k).start()
        y_copy(k).start()

    def forward(k):
        x_land(k).wait_recv()
        y_land(k).wait_recv()
        d_copy(k).start()

    def swap(k):
        if k == 0:
            place(k).wait()
        d_land(k).wait_recv()
        for j in range(2):
            c_copy(j, k).start()

    def end():
        for k in range(4):
            for j in range(2):
                c_land(j, k).wait_recv()
                c_copy(j, k).wait_send()
            if k:
                z_copy(k).wait_send()
            x_copy(k).wait_send()
            y_copy(k).wait_send()
            d_copy(k).wait_send()

    def reach():
        for k in (1, 3, 2):
            z_copy(k).start()
        place(0).start()

    def near():
        x_copy(0).start()
        y_copy(0).start()

    return types.SimpleNamespace(reach=reach, near=near, spread=spread, forward=forward, swap=swap, end=end)


class Comms:
    def __init__(self, *parts):
        self.parts = parts
        self.arrays = [a for part in parts for a in part.arrays]
        self.outputs = [o for part in parts for o in part.outputs]
        self.scratch = [s for part in parts for s in part.scratch]

    def plan(self, ins, outs, scratch):
        plans, i, o, s = [], 0, 0, 0
        for part in self.parts:
            ni, no, ns = len(part.arrays), len(part.outputs), len(part.scratch)
            plans.append(part.plan(ins[i : i + ni], outs[o : o + no], scratch[s : s + ns]))
            i, o, s = i + ni, o + no, s + ns

        def begin():
            Place().greet()
            for plan in plans:
                plan[0]()

        def end():
            for plan in plans:
                plan[2]()

        return begin, sorted((entry for plan in plans for entry in plan[1]), key=lambda entry: entry[0]), end


def scatter_ticks(g, parts, out, inside, send, recv):
    held, other, diag, near, far, planes = parts
    me = Place()
    first = (me.dp + (1 - me.c) * me.dx, me.rep + me.c * me.dy)
    second = (me.dp + me.c * me.dx, me.rep + (1 - me.c) * me.dy)
    flip_y, flip_x = 1 - 2 * me.y, me.dx
    at_first = (me.y + me.c * flip_y, me.x + (1 - me.c) * flip_x)
    at_second = (me.y + (1 - me.c) * flip_y, me.x + me.c * flip_x)
    at_diag = (me.y + flip_y, me.x + flip_x)
    c_copy = lambda j: remote(g.at[2 * j + 1 - me.c], other.at[j], send.at[j], recv.at[j], me.other_core)
    load = lambda j: pltpu.make_async_copy(g.at[2 * j + me.c], held.at[j], send.at[2 + j])
    region = lambda at: held.at[at[0], :, at[1]]
    diag_copy = remote(region(at_diag), diag, send.at[4], recv.at[4], first)
    near_copy = remote(region(at_first), near, send.at[5], recv.at[5], first)
    far_copy = remote(region(at_second), far, send.at[6], recv.at[6], second)
    z_copy = lambda k: remote(
        held.at[me.y, (me.z + k) % 4, me.x], planes.at[k - 1], send.at[6 + k], recv.at[6 + k], me.to_plane(k)
    )

    def add(spot, *terms):
        total = held[spot].astype(F32)
        for ref, i in terms:
            total = total + ref[i].astype(F32)
        held[spot] = total.astype(held.dtype)

    def begin():
        for j in range(2):
            c_copy(j).start()
            load(j).start()

    def fold(j):
        def run():
            c_copy(j).wait_recv()
            load(j).wait()

            @pl.loop(0, 4)
            def _(zz):
                for xx in range(2):
                    add((j, zz, xx), (other, (j, zz, xx)))

            if j == 1:
                diag_copy.start()
                near_copy.start()
        return run

    def pass_on():
        diag_copy.wait_recv()

        @pl.loop(0, 4)
        def _(zz):
            add((at_second[0], zz, at_second[1]), (diag, zz))

        far_copy.start()

    def planes_out():
        near_copy.wait_recv()
        far_copy.wait_recv()

        @pl.loop(0, 4)
        def _(zz):
            add((me.y, zz, me.x), (near, zz), (far, zz))

        if inside:
            for k in (1, 3, 2):
                z_copy(k).start()
        else:
            for k in range(4):
                out[k] = held[me.y, (me.z + k) % 4, me.x]

    def finish():
        if inside:
            total = held[me.y, me.z, me.x].astype(F32)
            for k in (1, 2, 3):
                z_copy(k).wait_recv()
                total = total + planes[k - 1].astype(F32)
            out[...] = total

    def end():
        for j in range(2):
            c_copy(j).wait_send()
        diag_copy.wait_send()
        near_copy.wait_send()
        far_copy.wait_send()
        if inside:
            for k in (1, 2, 3):
                z_copy(k).wait_send()

    return begin, [fold(0), fold(1), pass_on, planes_out, finish], end


class Scatter:
    def __init__(self, grads, inside=False):
        self.arrays, self.inside = list(grads), inside
        self.outputs, self.scratch = [], []
        for g in grads:
            a, b = g.shape[3:]
            out = jax.ShapeDtypeStruct((a, b), F32) if inside else jax.ShapeDtypeStruct((4, a, b), g.dtype)
            self.outputs.append((out, whole(out.shape)))
            planes = (3, a, b) if inside else (1, 8, 128)
            for shape in ((2, 4, 2, a, b), (2, 4, 2, a, b), (4, a, b), (4, a, b), (4, a, b), planes):
                self.scratch.append(pltpu.VMEM(shape, g.dtype))
        self.scratch += [pltpu.SemaphoreType.DMA((len(self.arrays), 10))] * 2

    def plan(self, grads, outs, scratch):
        send, recv = scratch[-2:]
        parts = [
            scatter_ticks(g, scratch[6 * i : 6 * i + 6], outs[i], self.inside, send.at[i], recv.at[i])
            for i, g in enumerate(grads)
        ]

        def begin():
            for part in parts:
                part[0]()

        def end():
            for part in parts:
                part[2]()

        timed = []
        for i, part in enumerate(parts):
            times = (3 + 4 * i, 5 + 4 * i, 12 + 13 * i, 29 + 17 * i, 100 + i)
            timed += list(zip(times, part[1]))
        return begin, timed, end


class PlaneScatter:
    def __init__(self, blocks):
        self.arrays = list(blocks)
        self.outputs, self.scratch = [], []
        for b in blocks:
            out = jax.ShapeDtypeStruct(b.shape[1:], F32)
            self.outputs.append((out, whole(out.shape)))
            self.scratch += [pltpu.VMEM(b.shape[1:], b.dtype), pltpu.VMEM((3, *b.shape[1:]), b.dtype)]
        self.scratch += [pltpu.SemaphoreType.DMA((len(self.arrays), 4)), pltpu.SemaphoreType.DMA((len(self.arrays), 3))]

    def plan(self, blocks, outs, scratch):
        me = Place()
        send, recv = scratch[-2:]
        each = []
        for i, b in enumerate(blocks):
            own, landed = scratch[2 * i : 2 * i + 2]
            copies = [remote(b.at[k], landed.at[k - 1], send.at[i, k], recv.at[i, k - 1], me.to_plane(k)) for k in (1, 3, 2)]
            each.append((pltpu.make_async_copy(b.at[0], own, send.at[i, 0]), copies, own, landed, outs[i]))

        def begin():
            for load, copies, *_ in each:
                load.start()
                for copy in copies:
                    copy.start()

        def end():
            for load, copies, own, landed, out in each:
                load.wait()
                for copy in copies:
                    copy.wait()
                total = own[...].astype(F32)
                for k in range(3):
                    total = total + landed[k].astype(F32)
                out[...] = total

        return begin, [], end


def run_at(step, sub, subs, steps, pace, timed):
    for s in range(steps):
        point = s * subs + sub
        chosen = [tick for t, tick in timed if round(t / pace) == point]
        if chosen:
            @pl.when(step == s)
            def _():
                for tick in chosen:
                    tick()


def run_rest(subs, steps, pace, timed):
    for t, tick in timed:
        if round(t / pace) >= subs * steps:
            tick()


def call(name, body, steps, ticked, subs, pace, inputs, outputs, scratch, comm, number):
    given = [] if comm is None else comm.arrays
    made = [] if comm is None else comm.outputs

    def kernel(*refs):
        cut, at = [], 0
        for size in (len(inputs), len(given), len(outputs), len(made), len(scratch)):
            cut.append(refs[at : at + size])
            at += size
        ins, c_in, outs, c_out, own = cut
        step = pl.program_id(0)
        if comm is None:
            body(step, lambda sub: None, ins, outs, own)
            return
        begin, timed, end = comm.plan(c_in, c_out, refs[at:])
        pl.when(step == 0)(begin)
        body(step, lambda sub: run_at(step, sub, subs, ticked, pace, timed), ins, outs, own)

        @pl.when(step == steps - 1)
        def _():
            run_rest(subs, ticked, pace, timed)
            end()

    return pl.pallas_call(
        kernel,
        grid=(steps,),
        in_specs=[spec for _, spec in inputs] + [ANY] * len(given),
        out_specs=[spec for _, spec in outputs] + [spec for _, spec in made],
        out_shape=[shape for shape, _ in outputs] + [shape for shape, _ in made],
        scratch_shapes=scratch + ([] if comm is None else comm.scratch),
        compiler_params=params(None if comm is None else number),
        name=name,
    )(*[a for a, _ in inputs], *given)


def full(a):
    return a, whole(a.shape)


def shape_of(*dims, dtype=BF):
    return jax.ShapeDtypeStruct(dims, dtype)


def gelu_parts(z):
    e = jnp.exp2(z * z * (-0.5 * LOG2E))
    den = 1.0 + (0.3275911 * 0.7071067811865476) * jnp.abs(z)
    t = pl.reciprocal(den, approx=True)
    t = t * (2.0 - den * t)
    poly = t * (0.127414796 + t * (-0.142248368 + t * (0.7107068705 + t * (-0.7265760135 + t * 0.5307027145))))
    tail = poly * e
    phi = jnp.where(z < 0, tail, 1.0 - tail)
    return z * phi, phi + z * (e * 0.3989422804014327)


def moments(v):
    centered = v - jnp.mean(v, axis=-1, keepdims=True)
    rs = lax.rsqrt(jnp.mean(centered * centered, axis=-1, keepdims=True) + 1e-05)
    return centered * rs, rs


def bias_bases(buckets, bias_table, n):
    selector = (buckets[:, None] == jnp.arange(bias_table.shape[0], dtype=jnp.int32)[None, :]).astype(F32)
    per_offset = jnp.dot(selector, bias_table.astype(F32), precision=lax.Precision.HIGHEST).T
    heads = per_offset.shape[0]
    zero = jnp.zeros((heads, 1), F32)
    base = jnp.concatenate([per_offset[:, n - 1 :], zero, per_offset[:, : n - 1]], axis=1)
    flipped = per_offset[:, ::-1]
    base_t = jnp.concatenate([flipped[:, n - 1 :], zero, flipped[:, : n - 1]], axis=1) * LOG2E
    return selector, base, base_t


def build_bias(h, base, base_t, bias, bias_t):
    n = bias.shape[1]
    for src, dst, at in ((base, bias, h), (base_t, bias_t, 0)):
        row = jnp.broadcast_to(src[h], (n, 2 * n))
        dst[at] = pltpu.roll(row, 0, 1, stride=1, stride_axis=0)[:, :n].astype(dst.dtype)


def build_masks(marks, mask, mask_t):
    n = mask.shape[1]
    rows = marks[...]
    seg_r, perm_r, pred_r = rows[0:1], rows[1:2], rows[2:3]
    for lo in range(0, n, 128):
        at = slice(lo, lo + 128)

        def col(k):
            piece = jnp.broadcast_to(rows[k : k + 1, at], (128, 128))
            return piece.T[:, :1]

        seg_c, perm_c, pred_c = col(0), col(1), col(2)
        same = (seg_c == seg_r) & (seg_r != 6.0)
        shown = pred_r == 0.0
        mask[0, at, :] = jnp.where(same & (shown | (perm_r <= perm_c)), 0.0, NEG)
        mask[1, at, :] = jnp.where(same & (shown | (perm_r < perm_c)), 0.0, NEG)
        same = (seg_c == seg_r) & (seg_c != 6.0)
        shown = pred_c == 0.0
        mask_t[at, :n] = jnp.where(same & (shown | (perm_c <= perm_r)), 0.0, NEG)
        mask_t[at, n:] = jnp.where(same & (shown | (perm_c < perm_r)), 0.0, NEG)


def project_streams(raw, xy, vec, layer, q_o, k_o, v_o, pf, of):
    n, d = xy.shape[1:]
    pairs = d // 128
    w = pf.shape[1] // raw.shape[0]
    pf[...] = jnp.concatenate([raw[r, :, :w] for r in range(raw.shape[0])], axis=1)
    of[...] = jnp.concatenate([raw[r, :, w:] for r in range(raw.shape[0])], axis=1)
    bq, bv = vec[layer, 0:1], vec[layer, 1:2]
    x = xy[0]
    qc = nn(x, pf[:, :d]) + bq
    qq = nn(xy[1], pf[:, :d]) + bq
    kk = nn(x, pf[:, d : 2 * d])
    vv = nn(x, pf[:, 2 * d :]) + bv
    for c in range(pairs):
        at = slice(128 * c, 128 * c + 128)
        q_o[c, :n] = qc[:, at].astype(BF)
        q_o[c, n:] = qq[:, at].astype(BF)
        k_o[c] = kk[:, at].astype(BF)
        v_o[c] = vv[:, at].astype(BF)


def attend_pair(p, tick, bias, mask, q_o, k_o, v_o, ctx_o, lse_s):
    n = mask.shape[1]
    rows_at = n // 2
    k, v = k_o[p], v_o[p]
    lane = lax.broadcasted_iota(jnp.int32, (1, 128), 1)
    low = lane < 64
    vx = jnp.concatenate([v, jnp.ones_like(v)], axis=1)
    k0 = jnp.where(low, k, 0)
    k1 = jnp.where(low, 0, k)
    for s in range(2):
        for lo in range(0, n, rows_at):
            tick(2 * s + lo // rows_at)
            at = slice(lo, lo + rows_at)
            to = slice(s * n + lo, s * n + lo + rows_at)
            q = q_o[p, to]
            parts = []
            for hh, kh in ((0, k0), (1, k1)):
                sc = (nt(q, kh) * 0.125 + bias[2 * p + hh, at].astype(F32)) * LOG2E + mask[s, at]
                m = jnp.maximum(jnp.max(sc, axis=-1, keepdims=True), FLOOR)
                e = jnp.exp2(sc - m).astype(BF)
                r = nn(e, vx)
                tot = r[:, 128:]
                tot = jnp.where(tot > 0, tot, 1.0)
                lse = m + jnp.log2(tot)
                lse_s[to] = jnp.where(lane == 2 * p + hh, lse, lse_s[to])
                parts.append(r[:, :128] / tot)
            ctx_o[p, to] = jnp.where(low, parts[0], parts[1]).astype(BF)


def forward_kernel(
    square, vec_shape, heads,
    x_in, y_in, marks, base, base_t, *refs,
):
    weights, refs = refs[:7], refs[7:]
    (bias_t, mask_t, q_o, k_o, v_o, ctx_h, lse_o, pf_h, of_h, xh1_o, nl_o, act_o, gp_o, xh2_o, rs1_o, rs2_o,
     mid_o, rc_o, rq_o, vec_o) = refs[:20]
    refs = refs[20:]
    if square:
        fulls, refs = refs[:7], refs[7:]
        vec_land, send, recv = refs[-3:]
    else:
        fulls = weights
    bias, mask, xy, raw, cts, act_s, second_s, lse_s, pf, of, ctx_o, load_sem = refs[:12]
    n, d = x_in.shape
    pairs = d // 128
    chunks, _, fw = raw.shape
    blocks = n // xh1_o.shape[0]
    tb = n // blocks
    step = pl.program_id(0)
    span = pairs + 4 * blocks
    layer = (step >= heads + span).astype(jnp.int32)
    spot = step - heads - layer * span
    starts = []
    for l in range(2):
        lo = heads + l * span
        starts += [lo, lo + pairs, lo + pairs + 2 * blocks]
    sizes = [pairs, 2 * blocks, 2 * blocks] * 2

    points = {}

    def put(at, sub, *actions):
        points.setdefault((at, sub), []).extend(actions)

    if square:
        items = [gather_steps(w, f, send.at[i], recv.at[i]) for i, (w, f) in enumerate(zip(weights, fulls))]
        vec_item, items = items[0], items[1:]
        do = lambda action, *ks: [functools.partial(action, k) for k in ks]

        def open_all():
            Place().greet()
            vec_item.near()
            vec_item.reach()
            items[0].near()
            items[0].reach()

        put(0, 0, open_all)
        put(2, 0, *do(vec_item.spread, 1, 3, 2), *do(vec_item.forward, 0))
        put(4, 0, *do(vec_item.forward, 1, 2, 3), *do(items[0].spread, 1))
        put(6, 0, *do(vec_item.swap, 0, 1, 2, 3), *do(items[0].forward, 0))
        put(8, 0, *do(items[0].spread, 3))
        put(9, 0, *do(items[0].forward, 1), *do(items[0].swap, 0))
        put(10, 0, *do(items[0].spread, 2), items[1].reach)
        put(11, 0, *do(items[0].forward, 3), *do(items[0].swap, 1))
        first = [*do(items[0].forward, 2), items[1].near, *do(items[0].swap, 3, 2), vec_item.end, items[0].end]
        for j in range(1, 6):
            lo, count = starts[j - 1], sizes[j - 1] * 4
            item = items[j]
            after = items[j + 1] if j < 5 else None
            plan = [
                (0.0, do(item.spread, 1, 3, 2)), (0.1, [after.reach] if after else []), (0.2, do(item.forward, 0)),
                (0.4, do(item.forward, 1)), (0.55, do(item.forward, 2) + do(item.swap, 0)),
                (0.65, [after.near] if after else []), (0.8, do(item.forward, 3) + do(item.swap, 1)),
                (0.93, do(item.swap, 2)),
            ]
            for part, actions in plan:
                point = int(part * count)
                put(lo + point // 4, point % 4, *actions)
        finish = [first] + [[functools.partial(items[j].swap, 3), items[j].end] for j in range(1, 6)]
    else:
        finish = [[] for _ in range(6)]

    def tick(sub):
        for (at, which), actions in points.items():
            if which == sub and actions:
                @pl.when(step == at)
                def _():
                    for action in actions:
                        action()

    def arrive(j, dst, then=None):
        @pl.when(step == starts[j])
        def _():
            for action in finish[j]:
                action()
            copy = pltpu.make_async_copy(fulls[1 + j], dst, load_sem.at[0])
            copy.start()
            if then:
                then()
            copy.wait()

    def vectors():
        if not square:
            copy = pltpu.make_async_copy(weights[0], vec_o, load_sem.at[1])
            copy.start()
            copy.wait()
            return
        copy = pltpu.make_async_copy(fulls[0], vec_land, load_sem.at[1])
        copy.start()
        copy.wait()
        rows, cols = vec_shape
        vec_o[...] = jnp.zeros_like(vec_o)
        for l in range(2):
            for r in range(4):
                pieces = [vec_land[r, 16 * i + 8 * l : 16 * i + 8 * l + rows, :cols] for i in range(d // cols)]
                vec_o[l, rows * r : rows * r + rows] = jnp.concatenate(pieces, axis=1).astype(F32)

    keep = lambda ref, out, sem: pltpu.make_async_copy(ref, out.at[layer], load_sem.at[sem])

    @pl.when(step < heads)
    def _():
        tick_prep = tick
        tick_prep(0)
        build_bias(step, base, base_t, bias, bias_t)

    @pl.when(step == 0)
    def _():
        build_masks(marks, mask, mask_t)
        xy[0] = x_in[...]
        xy[1] = y_in[...]
        lse_s[...] = jnp.zeros_like(lse_s)

    arrive(0, raw, vectors)
    arrive(3, raw)

    @pl.when((spot >= 0) & (spot < pairs))
    def _():
        @pl.when(spot == 0)
        def _():
            project_streams(raw, xy, vec_o, layer, q_o, k_o, v_o, pf, of)
            keep(pf, pf_h, 2).start()
            keep(of, of_h, 3).start()

        attend_pair(spot, tick, bias, mask, q_o, k_o, v_o, ctx_o, lse_s)

        @pl.when(spot == pairs - 1)
        def _():
            for lo in range(0, 2 * n, 128):
                lse_o[:, lo : lo + 128] = lse_s[lo : lo + 128].T[: lse_o.shape[0]]
            keep(ctx_o, ctx_h, 4).start()
            keep(pf, pf_h, 2).wait()
            keep(of, of_h, 3).wait()

    arrive(1, raw)
    arrive(4, raw)

    @pl.when((spot >= pairs) & (spot < pairs + 2 * blocks))
    def _():
        t = spot - pairs
        rows = pl.ds(pl.multiple_of(t * tb, tb), tb)
        inner = pl.ds(pl.multiple_of(t % blocks * tb, tb), tb)
        vec = vec_o.at[layer]
        z = xy[t // blocks, inner].astype(F32)
        cx = jnp.concatenate([ctx_o[c, rows] for c in range(pairs)], axis=1)
        xh1, rs1 = moments(z + (nn(cx, of[...]) + vec[2:3]))
        normed = xh1 * vec[3:4] + vec[4:5]
        nl = normed.astype(BF)
        xh1_o[...] = xh1.astype(BF)
        nl_o[...] = nl
        rs1_o[...] = jnp.broadcast_to(rs1, rs1_o.shape)
        second_s[rows] = normed + vec[5:6]
        for f in range(chunks):
            tick(f)
            at = slice(f * fw, f * fw + fw)
            act, gp = gelu_parts(nn(nl, raw[f]) + vec[8 + f : 9 + f])
            act = act.astype(BF)
            act_o[:, at] = act
            act_s[rows, at] = act
            gp_o[:, at] = gp.astype(BF)

    arrive(2, cts)
    arrive(5, cts)

    @pl.when(spot >= pairs + 2 * blocks)
    def _():
        t = spot - pairs - 2 * blocks
        rows = pl.ds(pl.multiple_of(t * tb, tb), tb)
        inner = pl.ds(pl.multiple_of(t % blocks * tb, tb), tb)
        vec = vec_o.at[layer]
        second = second_s[rows]
        for f in range(chunks):
            tick(f)
            at = slice(f * fw, f * fw + fw)
            second = second + nt(act_s[rows, at], cts[:, at])
        xh2, rs2 = moments(second)
        xh2_o[...] = xh2.astype(BF)
        rs2_o[...] = jnp.broadcast_to(rs2, rs2_o.shape)
        res = (xh2 * vec[6:7] + vec[7:8]).astype(BF)

        @pl.when(t == 0)
        def _():
            keep(ctx_o, ctx_h, 4).wait()

        @pl.when(layer == 0)
        def _():
            mid_o[...] = res
            xy[t // blocks, inner] = res

        @pl.when((layer == 1) & (t < blocks))
        def _():
            rc_o[...] = res

        @pl.when((layer == 1) & (t >= blocks))
        def _():
            rq_o[...] = res


def forward(x, y, marks, base, base_t, weights, square, vec_shape, heads):
    n, d = x.shape
    pairs = d // 128
    reps = 4
    if square:
        rows = [(4, 8 * a.shape[0], a.shape[1]) for a in weights]
        rows[3] = rows[6] = (4 * weights[3].shape[0], 8 * weights[3].shape[1])
        made = [(shape_of(*s), ANY) for s in rows]
        fw = weights[2].shape[1]
    else:
        made = []
        fw = weights[2].shape[2]
    ff = reps * fw
    blocks = 2
    tb = n // blocks
    span = pairs + 4 * blocks
    layer = lambda s: jnp.where(s >= heads + span, 1, 0)
    tok = lambda s: jnp.clip(s - heads - layer(s) * span - pairs, 0, 2 * blocks - 1)
    down = lambda s: jnp.clip(s - heads - layer(s) * span - pairs - 2 * blocks, 0, 2 * blocks - 1)
    per_layer = lambda *dims: (shape_of(2, *dims), pl.BlockSpec((None, *dims), lambda s: (layer(s), *(0,) * len(dims))))
    f32_layer = lambda *dims: (shape_of(2, *dims, dtype=F32), pl.BlockSpec((None, *dims), lambda s: (layer(s), *(0,) * len(dims))))
    blocked = lambda width, at, dtype=BF: (
        shape_of(2, 2 * n, width, dtype=dtype), pl.BlockSpec((None, tb, width), lambda s: (layer(s), at(s), 0))
    )
    end = heads + 2 * span
    outputs = [
        (shape_of(heads, n, n, dtype=F32), pl.BlockSpec((1, n, n), lambda s: (jnp.minimum(s, heads - 1), 0, 0))),
        (shape_of(n, 2 * n, dtype=F32), whole((n, 2 * n))),
        per_layer(pairs, 2 * n, 128), per_layer(pairs, n, 128), per_layer(pairs, n, 128), (shape_of(2, pairs, 2 * n, 128), ANY),
        f32_layer(16, 2 * n), (shape_of(2, d, 3 * d), ANY), (shape_of(2, d, d), ANY),
        blocked(d, tok), blocked(d, tok), blocked(ff, tok), blocked(ff, tok), blocked(d, down),
        blocked(128, tok, F32), blocked(128, down, F32),
        (shape_of(2 * n, d), pl.BlockSpec((tb, d), lambda s: (jnp.where(layer(s) == 0, down(s), 2 * blocks - 1), 0))),
        (shape_of(n, d), pl.BlockSpec((tb, d), lambda s: (jnp.clip(s - (end - 2 * blocks), 0, blocks - 1), 0))),
        (shape_of(n, d), pl.BlockSpec((tb, d), lambda s: (jnp.clip(s - (end - blocks), 0, blocks - 1), 0))),
        (shape_of(2, 16, d, dtype=F32), whole((2, 16, d))),
    ]
    scratch = [
        pltpu.VMEM((heads, n, n), BF), pltpu.VMEM((2, n, n), F32), pltpu.VMEM((2, n, d), BF),
        pltpu.VMEM((reps, d, fw), BF), pltpu.VMEM((d, ff), BF), pltpu.VMEM((2 * n, ff), BF),
        pltpu.VMEM((2 * n, d), F32), pltpu.VMEM((2 * n, 128), F32),
        pltpu.VMEM((d, 3 * d), BF), pltpu.VMEM((d, d), BF), pltpu.VMEM((pairs, 2 * n, 128), BF),
        pltpu.SemaphoreType.DMA((5,)),
    ]
    if square:
        scratch += [pltpu.VMEM(made[0][0].shape, BF)] + [pltpu.SemaphoreType.DMA((7, SEMS))] * 2
    outs = pl.pallas_call(
        functools.partial(forward_kernel, square, vec_shape, heads),
        grid=(end,),
        in_specs=[whole(a.shape) for a in (x, y, marks)] + [whole((heads, 1, 2 * n))] * 2 + [ANY] * 7,
        out_specs=[spec for _, spec in outputs + made],
        out_shape=[shape for shape, _ in outputs + made],
        scratch_shapes=scratch,
        compiler_params=params(1 if square else None),
        name="forward",
    )(x, y, marks, base.reshape(heads, 1, 2 * n), base_t.reshape(heads, 1, 2 * n), *weights)
    (bias_t, mask_t, q, k, v, ctx, lse, pf, of, xh1, nl, act, gp, xh2, rs1, rs2, mid, rc, rq, vec) = outs[:20]
    fulls = outs[20:] if square else weights
    return types.SimpleNamespace(
        bias_t=bias_t, mask_t=mask_t, att=(q, k, v, lse, pf), post=(ctx, xh1, nl, gp, xh2, rs1, rs2, act, of),
        mid=mid, content=rc, query=rq, vec=vec, fulls=fulls[1:],
    )


def norm_back(g, xh, rs, gain):
    a = g * gain
    return rs * (a - jnp.mean(a, axis=-1, keepdims=True) - xh * jnp.mean(a * xh, axis=-1, keepdims=True))


def rowsum(v):
    return jnp.sum(v, axis=0, keepdims=True)


def post_bwd_body(step, tick, ins, outs, own):
    gc, gq, ctx, xh1, nl, gp, xh2, rs1, rs2, act, of, ew, ct, vec = ins
    first_o, gctx_o, vg_o, do_o, de_o, dc_o = outs
    gh_s, nl_t, gf_t, cx_t, ga_s = own
    t = step
    tb, d = gc.shape
    chunks, fw = ew.shape[0], ew.shape[2]
    blocks = chunks // 2

    @pl.when(t == 0)
    def _():
        vg_o[...] = jnp.zeros_like(vg_o)

    @pl.when(t < 2 * blocks)
    def _():
        g = jnp.where(t < blocks, gc[...].astype(F32), gq[...].astype(F32))
        xh = xh2[...].astype(F32)
        vg_o[6:7] += rowsum(g * xh)
        vg_o[7:8] += rowsum(g)
        gs = norm_back(g, xh, rs2[:, :1], vec[6:7])
        gf = gs.astype(BF)
        vg_o[5:6] += rowsum(gf.astype(F32))
        gn = gs
        spot = pl.ds(pl.multiple_of(t * tb, tb), tb)
        for f in range(chunks):
            tick(f)
            at = slice(f * fw, f * fw + fw)
            gh = (nn(gf, ct[:, at]) * gp[:, at].astype(F32)).astype(BF)
            gh_s[f, spot] = gh
            vg_o[8 + f : 9 + f] += rowsum(gh.astype(F32))
            gn = gn + nt(gh, ew[f])
        xh = xh1[...].astype(F32)
        vg_o[3:4] += rowsum(gn * xh)
        vg_o[4:5] += rowsum(gn)
        first = norm_back(gn, xh, rs1[:, :1], vec[3:4])
        first_o[...] = first
        ga = first.astype(BF)
        vg_o[2:3] += rowsum(ga.astype(F32))
        ga_s[spot] = ga
        gx = nt(ga, of[...]).astype(BF)
        cx = jnp.concatenate([ctx[c] for c in range(ctx.shape[0])], axis=1)
        for c in range(ctx.shape[0]):
            gctx_o[c] = gx[:, 128 * c : 128 * c + 128]
        nl_t[:, spot] = nl[...].T
        gf_t[:, spot] = gf.T
        cx_t[:, spot] = cx.T

    @pl.when(t == 2 * blocks)
    def _():
        do_o[...] = nn(cx_t[...], ga_s[...]).astype(BF)

    @pl.when(t >= 2 * blocks)
    def _():
        de_o[0] = nn(nl_t[...], gh_s[t - 2 * blocks]).astype(BF)
        dc = nn(gf_t[...], act[...]).astype(BF)
        if len(dc_o.shape) == 2:
            dc_o[...] = dc
        else:
            reps, across, a, b = dc_o.shape
            for r in range(reps):
                for x in range(across):
                    dc_o[r, x] = dc[a * r : a * r + a, b * x : b * x + b]


def post_bwd(layer, gc, gq, kept, ew, ct, vec, comm, number, split):
    ctx, xh1, nl, gp, xh2, rs1, rs2, act, of = kept
    n, d = gc.shape
    chunks, fw = ew.shape[0], ew.shape[2]
    ff = chunks * fw
    pairs = ctx.shape[1]
    blocks = chunks // 2
    tb = n // blocks
    last = 2 * blocks - 1
    tok = lambda width: pl.BlockSpec((tb, width), lambda t: (jnp.minimum(t, last), 0))
    tok3 = pl.BlockSpec((pairs, tb, 128), lambda t: (0, jnp.minimum(t, last), 0))
    kept_tok = lambda width: pl.BlockSpec((None, tb, width), lambda t: (layer, jnp.minimum(t, last), 0))
    of_layer = lambda a: (a, pl.BlockSpec((None, *a.shape[1:]), lambda t: (layer, 0, 0)))
    part = lambda t: jnp.maximum(t - last - 1, 0)
    if split:
        reps, owners = split
        across = owners // chunks
        dc = (
            shape_of(reps, owners, d // reps, ff // owners),
            pl.BlockSpec((reps, across, d // reps, ff // owners), lambda t: (0, part(t), 0, 0)),
        )
    else:
        dc = shape_of(d, ff), pl.BlockSpec((d, fw), lambda t: (0, part(t)))
    return call(
        "post_bwd", post_bwd_body, 2 * blocks + chunks, 2 * blocks, chunks, 1.7,
        [
            (gc, pl.BlockSpec((tb, d), lambda t: (jnp.minimum(t, blocks - 1), 0))),
            (gq, pl.BlockSpec((tb, d), lambda t: (jnp.clip(t - blocks, 0, blocks - 1), 0))),
            (ctx, pl.BlockSpec((None, pairs, tb, 128), lambda t: (layer, 0, jnp.minimum(t, last), 0))),
            (xh1, kept_tok(d)), (nl, kept_tok(d)), (gp, kept_tok(ff)), (xh2, kept_tok(d)),
            (rs1, kept_tok(128)), (rs2, kept_tok(128)),
            (act, pl.BlockSpec((None, 2 * n, fw), lambda t: (layer, 0, part(t)))),
            of_layer(of), full(ew), full(ct), of_layer(vec),
        ],
        [
            (shape_of(2 * n, d, dtype=F32), tok(d)), (shape_of(pairs, 2 * n, 128), tok3),
            (shape_of(16, d, dtype=F32), whole((16, d))), (shape_of(d, d), whole((d, d))),
            (shape_of(chunks, d, fw), pl.BlockSpec((1, d, fw), lambda t: (part(t), 0, 0))), dc,
        ],
        [
            pltpu.VMEM((chunks, 2 * n, fw), BF),
            pltpu.VMEM((d, 2 * n), BF), pltpu.VMEM((d, 2 * n), BF), pltpu.VMEM((d, 2 * n), BF),
            pltpu.VMEM((2 * n, d), BF),
        ],
        comm, number,
    )


def attn_bwd_body(step, tick, ins, outs, own):
    q, k, v, go, lse, bias_t, mask_t, x, y, first, pf, do = ins
    gx_o, gy_o, dp_o, bg_o, t8_o = outs
    dq_s, dk_s, dv_s, diag, x_t, dk_a, dv_a = own
    p = step
    n, d = x.shape
    pairs = d // 128
    wide = diag.shape[2]
    cols = n // 2

    @pl.when(p == 0)
    def _():
        x_t[:, :n] = x[...].T
        x_t[:, n:] = y[...].T

    @pl.when(p < pairs)
    def _():
        low = lax.broadcasted_iota(jnp.int32, (1, 128), 1) < 64
        only = lambda a, hh: jnp.where(low, a, 0) if hh == 0 else jnp.where(low, 0, a)
        diag[...] = jnp.zeros_like(diag)
        ka, va = k[0], v[0]
        for i, lo in enumerate(range(0, 2 * n, cols)):
            tick(i)
            at = slice(lo, lo + cols)
            i0 = lo % n
            qa, ga = q[0, at], go[0, at]
            dq = dk = dv = None
            for hh in range(2):
                km, vm = only(ka, hh), only(va, hh)
                lrow = lse[pl.ds(2 * p + hh, 1), at]
                sc = nt(km, qa) * (0.125 * LOG2E) + (bias_t[hh, :, i0 : i0 + cols] + mask_t[:, at])
                pr = jnp.exp2(sc - lrow)
                gp = nt(vm, ga)
                ds = pr * (gp - rowsum(pr * gp))
                dsb = ds.astype(BF)
                dv_h = nn(pr.astype(BF), only(ga, hh))
                dk_h = nn(dsb, only(qa, hh))
                dq_h = tn(dsb, km)
                dq, dk, dv = (dq_h, dk_h, dv_h) if hh == 0 else (dq + dq_h, dk + dk_h, dv + dv_h)
                for b in range(n // 128):
                    off = n - 128 - 128 * b + i0
                    diag[hh, :, off : off + cols] += ds[128 * b : 128 * b + 128]
            dq_s[p, at] = (dq * 0.125).astype(BF)
            if i == 0:
                dk_a[...] = dk
                dv_a[...] = dv
            else:
                dk_a[...] += dk
                dv_a[...] += dv
        dk_s[p] = (dk_a[...] * 0.125).astype(BF)
        dv_s[p] = dv_a[...].astype(BF)
        for hh in range(2):
            total = jnp.zeros((8, 2 * n), F32)
            for g in range(16):
                piece = jnp.concatenate([diag[hh, 8 * g : 8 * g + 8], jnp.zeros((8, 2 * n - wide), F32)], axis=1)
                total = total + (pltpu.roll(piece, 2 * n - 8 * g, 1) if g else piece)
            t8_o[hh] = total

    @pl.when(p == pairs)
    def _():
        cat = lambda ref, at: jnp.concatenate([ref[c, at] for c in range(pairs)], axis=1)
        gqc, gqq = cat(dq_s, slice(0, n)), cat(dq_s, slice(n, 2 * n))
        gk, gv = cat(dk_s, slice(0, n)), cat(dv_s, slice(0, n))
        gx_o[...] = first[:n] + nt(gqc, pf[:, :d]) + nt(gk, pf[:, d : 2 * d]) + nt(gv, pf[:, 2 * d :])
        gy_o[...] = first[n:] + nt(gqq, pf[:, :d])
        bg_o[...] = jnp.zeros_like(bg_o)
        bg_o[0:1] = rowsum(gqc.astype(F32)) + rowsum(gqq.astype(F32))
        bg_o[1:2] = rowsum(gv.astype(F32))
        xt = x_t[:, :n]
        grads = jnp.concatenate([
            nn(x_t[...], jnp.concatenate([gqc, gqq], axis=0)).astype(BF),
            nn(xt, gk).astype(BF), nn(xt, gv).astype(BF)], axis=1)
        reps = dp_o.shape[0]
        w, u = 3 * d // reps, d // reps
        for r in range(reps):
            both = [grads[:, r * w : r * w + w], do[:, r * u : r * u + u]]
            dp_o[r] = jnp.concatenate(both, axis=1)


def attn_bwd(layer, kept, go, bias_t, mask_t, x, y, first, do, reps, comm, number):
    q, k, v, lse, pf = kept
    n, d = first.shape[0] // 2, first.shape[1]
    packed = (reps, d, 4 * d // reps)
    pairs = d // 128
    pair = lambda *block: pl.BlockSpec(block, lambda p: (jnp.minimum(p, pairs - 1), 0, 0))
    kept_pair = lambda rows: pl.BlockSpec((None, 1, rows, 128), lambda p: (layer, jnp.minimum(p, pairs - 1), 0, 0))
    of_layer = lambda a: (a, pl.BlockSpec((None, *a.shape[1:]), lambda t: (layer, 0, 0)))
    return call(
        "attn_bwd", attn_bwd_body, pairs + 1, pairs, 4, 1.5,
        [
            (q, kept_pair(2 * n)), (k, kept_pair(n)), (v, kept_pair(n)), (go, pair(1, 2 * n, 128)),
            of_layer(lse), (bias_t, pair(2, n, n)), full(mask_t), x, y, full(first), of_layer(pf), full(do),
        ],
        [
            (shape_of(n, d, dtype=F32), whole((n, d))), (shape_of(n, d, dtype=F32), whole((n, d))),
            (shape_of(*packed), whole(packed)), (shape_of(8, d, dtype=F32), whole((8, d))),
            (shape_of(2 * pairs, 8, 2 * n, dtype=F32), pair(2, 8, 2 * n)),
        ],
        [
            pltpu.VMEM((pairs, 2 * n, 128), BF),
            pltpu.VMEM((pairs, n, 128), BF), pltpu.VMEM((pairs, n, 128), BF),
            pltpu.VMEM((2, 128, 2 * n - 128), F32), pltpu.VMEM((d, 2 * n), BF),
            pltpu.VMEM((n, 128), F32), pltpu.VMEM((n, 128), F32),
        ],
        comm, number,
    )


def offset_sums(t8, n):
    total = sum(jnp.roll(t8[:, r], -(n - 128 + r), axis=1) for r in range(t8.shape[1]))
    return jnp.concatenate([total[:, 1:n][:, ::-1], total[:, :1], total[:, n + 1 :][:, ::-1]], axis=1)


def turn(v, shift):
    return pltpu.roll(v, v.shape[1] - shift, 1)


def table_sums(first, second, places, n):
    heads, eight, wide = first.shape
    v = turn((first[...] + second[...]).reshape(heads * eight, wide), n - 128)
    row = lax.broadcasted_iota(jnp.int32, (heads * eight, 1), 0) % eight
    for bit in (1, 2, 4):
        v = jnp.where(row // bit % 2 == 1, turn(v, bit), v)
    sums = jnp.sum(v.reshape(heads, eight, wide), axis=1)
    pick = jnp.where(lax.broadcasted_iota(jnp.int32, (32, wide), 0) == places[...], 1.0, 0.0).astype(BF)
    out = 0.0
    for _ in range(3):
        piece = sums.astype(BF)
        out = out + nt(pick, piece)
        sums = sums - piece.astype(F32)
    return out


def table_ticks(own, table, held, landed, planes, send, recv):
    me = Place()
    peers = (me.other_core, me.across_x, me.across_y)
    step = lambda s: remote(held.at[s], landed.at[s], send.at[s], recv.at[s], peers[s])
    z_copy = lambda k: remote(held.at[3], planes.at[me.z], send.at[2 + k], recv.at[2 + k], me.to_plane(k))
    z_land = lambda k: remote(held.at[3], planes.at[me.from_plane(k) // 2], send.at[2 + k], recv.at[2 + k], me.to_plane(k))

    def begin():
        held[0] = own()
        step(0).start()

    def next_step(s):
        def run():
            step(s).wait_recv()
            held[s + 1] = held[s] + landed[s]
            if s < 2:
                step(s + 1).start()
            else:
                planes[me.z] = held[3]
                for k in (1, 2, 3):
                    z_copy(k).start()
        return run

    def end():
        for k in (1, 2, 3):
            z_land(k).wait_recv()
        table[...] = (planes[0] + planes[1]) + (planes[2] + planes[3])
        for s in range(3):
            step(s).wait_send()
        for k in (1, 2, 3):
            z_copy(k).wait_send()

    return begin, [next_step(s) for s in range(3)], end


class Table:
    def __init__(self, t8_one, t8_two, places):
        vmem = pl.BlockSpec(memory_space=pltpu.VMEM)
        self.arrays = []
        self.inputs = [(t8_one, vmem), (t8_two, vmem), (places, vmem)]
        self.outputs = [(shape_of(32, 128, dtype=F32), vmem)]
        self.scratch = [
            pltpu.VMEM((4, 32, 128), F32), pltpu.VMEM((3, 32, 128), F32), pltpu.VMEM((4, 32, 128), F32),
            pltpu.SemaphoreType.DMA((6,)), pltpu.SemaphoreType.DMA((6,)),
        ]

    def plan(self, ins, outs, scratch):
        t8_one, t8_two, places = self.refs
        heads, _, wide = t8_one.shape

        def own():
            sums = table_sums(t8_one, t8_two, places, wide // 2)
            return jnp.concatenate([sums, jnp.zeros((sums.shape[0], 128 - heads), F32)], axis=1)

        begin, ticks, end = table_ticks(own, outs[0], *scratch)
        return begin, [(6 + 5 * i, tick) for i, tick in enumerate(ticks)], end


def tail_kernel(table, comm, *refs):
    table.refs = refs[:3]
    at = 3 + len(comm.arrays)
    to = at + len(comm.outputs)
    begin, timed, end = comm.plan(refs[3:at], refs[at:to], refs[to:])
    begin()
    for _, tick in timed:
        tick()
    end()


def tail(table, comm, number):
    return pl.pallas_call(
        functools.partial(tail_kernel, table, comm),
        in_specs=[spec for _, spec in table.inputs] + [ANY] * len(comm.arrays),
        out_specs=[spec for _, spec in comm.outputs],
        out_shape=[shape for shape, _ in comm.outputs],
        scratch_shapes=comm.scratch,
        compiler_params=params(number),
        name="tail",
    )(*[a for a, _ in table.inputs], *comm.arrays)


def vector_block(vectors):
    rows, cols = vectors.shape
    return jnp.pad(vectors, ((0, 8 - rows), (0, 128 - cols)))


def plain_gather(both, expand, contract, vectors):
    rows = lambda a, dim: lax.all_gather(a, "dp", axis=dim, tiled=True)
    po = lax.all_gather(rows(both, 0), "rep", axis=0)
    ew = lax.all_gather(rows(expand, 0), "rep", axis=0)
    ct = lax.all_gather(rows(contract, 1), "rep", axis=0, tiled=True)
    vec = lax.all_gather(rows(vectors, 1), "rep", axis=0, tiled=True).astype(F32)
    return po, ew, ct, vec


def scatter_sum(a, rep_dim, dp_dim):
    a = lax.psum_scatter(a, "rep", scatter_dimension=rep_dim, tiled=True)
    return lax.psum_scatter(a, "dp", scatter_dimension=dp_dim, tiled=True).astype(F32)


def shards(
    square,
    content_stream, query_stream, segments, perm_order, predicted, buckets, bias_table,
    project_one, output_one, expand_one, contract_one, vectors_one,
    project_two, output_two, expand_two, contract_two, vectors_two,
    content_cotangent, query_cotangent,
):
    shape = content_stream.shape
    n, d = shape[1:]
    reps = 3 * d // project_one.shape[1]
    flat = lambda a: a.reshape(n, d)
    selector, base, base_t = bias_bases(buckets, bias_table, n)
    marks = jnp.concatenate([segments, perm_order, predicted, jnp.zeros((5, n), jnp.int32)]).astype(F32)
    one = (jnp.concatenate([project_one, output_one], axis=1), expand_one, contract_one.T, vectors_one)
    two = (jnp.concatenate([project_two, output_two], axis=1), expand_two, contract_two.T, vectors_two)
    rows, cols = vectors_one.shape
    if square:
        both = jnp.concatenate([vector_block(vectors_one), vector_block(vectors_two)], axis=0)
        weights = [both, *one[:3], *two[:3]]
    else:
        full_one, full_two = plain_gather(*one), plain_gather(*two)
        both = jnp.pad(jnp.stack([full_one[3], full_two[3]]), ((0, 0), (0, 16 - 4 * rows), (0, 0)))
        weights = [both, *full_one[:3], *full_two[:3]]
    kept = forward(
        flat(content_stream), flat(query_stream), marks, base, base_t, weights, square, (rows, cols), bias_table.shape[1]
    )
    bias_t, mask_t = kept.bias_t, kept.mask_t
    ew, ct = (kept.fulls[1], kept.fulls[4]), (kept.fulls[2], kept.fulls[5])
    x, y = kept.content, kept.query
    half = lambda i: pl.BlockSpec((n, d), lambda t: (i, 0))
    ins = [
        ((flat(content_stream), half(0)), (flat(query_stream), half(0))),
        ((kept.mid, half(0)), (kept.mid, half(1))),
    ]

    def back_post(layer, gx, gy, comm, number):
        split = (4, 8) if square else None
        return post_bwd(layer, gx, gy, kept.post, ew[layer], ct[layer], kept.vec, comm, number, split)

    def back_attn(layer, gctx, first, do, comm, number):
        return attn_bwd(layer, kept.att, gctx, bias_t, mask_t, *ins[layer], first, do, reps, comm, number)

    pieces = lambda a: a.reshape(4, 4, 2, a.shape[-2] if a.ndim == 4 else a.shape[1] // 8, a.shape[-1])
    sent = lambda grads, blocks: Comms(Scatter([pieces(a) for a in grads]), *[PlaneScatter(b) for b in blocks]) if square else None
    first, gctx, vg_two, do, de_two, dc_two = back_post(
        1, flat(content_cotangent), flat(query_cotangent), None, 0
    )
    gx, gy, dp_two, bg_two, t8_two, *out_two = back_attn(1, gctx, first, do, sent([dc_two, de_two], []), 5)
    first, gctx, vg_one, do, de_one, dc_one, *out_mid = back_post(0, gx, gy, sent([dp_two], [out_two]), 6)
    gx, gy, dp_one, bg_one, t8_one, *out_one = back_attn(
        0, gctx, first, do, sent([dc_one, de_one], [out_mid[:1]]), 7
    )
    vg_one = jnp.concatenate([bg_one[:2], vg_one[2:12]], axis=0)
    vg_two = jnp.concatenate([bg_two[:2], vg_two[2:12]], axis=0)
    cut = project_one.shape[1]
    if square:
        vgs = jnp.stack([vg_one, vg_two]).reshape(2, 4, rows, 8, cols).transpose(1, 3, 0, 2, 4)
        vgs = jnp.pad(vgs.reshape(4, 8, 2 * rows, cols), ((0, 0), (0, 0), (0, 8 - 2 * rows), (0, 128 - cols)))
        turned = buckets[::-1]
        places = jnp.concatenate([turned[n - 1 :], -jnp.ones((1,), jnp.int32), turned[: n - 1]])[None]
        table = Table(t8_one, t8_two, places)
        out_p1, vecs, table, *ce_one = tail(
            table, Comms(Scatter([pieces(dp_one), pieces(vgs)], True), table, PlaneScatter(out_one[:2])), 8
        )
        table = table[:, : bias_table.shape[1]]
        grads = lambda po, c, e, lo: (po[:, :cut], po[:, cut:], e, c.T, vecs[lo : lo + rows, :cols])
        grads_one, grads_two = grads(out_p1, *ce_one, 0), grads(out_one[2], *out_mid[1:], rows)
    else:
        distances = offset_sums(t8_one + t8_two, n)
        table = jnp.dot(selector.T, distances.T, precision=lax.Precision.HIGHEST)
        table = lax.psum(table, ("dp", "rep"))

        def spread(dp, de, dc, vec):
            po = scatter_sum(dp, 0, 1)[0]
            return po[:, :cut], po[:, cut:], scatter_sum(de, 0, 1)[0], scatter_sum(dc, 0, 1).T, scatter_sum(vec, 0, 1)

        grads_one = spread(dp_one, de_one, dc_one, vg_one)
        grads_two = spread(dp_two, de_two, dc_two, vg_two)
    return (
        x.reshape(shape), y.reshape(shape), gx.reshape(shape), gy.reshape(shape), table,
        *grads_one, *grads_two,
    )


def solution(mesh):
    rows3, rows2 = P(("dp", "rep"), None, None), P(("dp", "rep"), None)
    weights = (P("dp", "rep"),) * 4 + (P("rep", "dp"),)
    square = mesh.shape["dp"] == 8 and mesh.shape["rep"] == 4
    return jax.shard_map(
        functools.partial(shards, square),
        mesh=mesh,
        in_specs=(rows3, rows3, rows2, rows2, rows2, P(), P(), *weights, *weights, rows3, rows3),
        out_specs=(rows3, rows3, rows3, rows3, P(), *weights, *weights),
        check_vma=False,
    )
```

```python
import functools
import types
import jax
import jax.numpy as jnp
from jax import lax
from jax.experimental import pallas as pl
from jax.experimental.pallas import tpu as pltpu
from jax.sharding import PartitionSpec as P

F32 = jnp.float32
BF = jnp.bfloat16
LOG2E = 1.4426950408889634
NEG = -1e30
FLOOR = -1e29
VM = 60 * 1024 * 1024
NT = (((1,), (1,)), ((), ()))
TN = (((0,), (0,)), ((), ()))


def nt(a, b):
    return lax.dot_general(a, b, NT, preferred_element_type=F32)


def tn(a, b):
    return lax.dot_general(a, b, TN, preferred_element_type=F32)


def nn(a, b):
    return jnp.dot(a, b, preferred_element_type=F32)


def whole(shape):
    return pl.BlockSpec(shape, lambda *_: (0,) * len(shape))


def params(number=None):
    if number is None:
        return pltpu.CompilerParams(vmem_limit_bytes=VM)
    return pltpu.CompilerParams(vmem_limit_bytes=VM, collective_id=number, has_side_effects=True)


MESH = pl.DeviceIdType.MESH
ANY = pl.BlockSpec(memory_space=pl.ANY)
SEMS = 24


class Place:
    def __init__(self):
        self.dp = lax.axis_index("dp")
        self.rep = lax.axis_index("rep")
        self.z, self.x = self.dp // 2, self.dp % 2
        self.y, self.c = self.rep // 2, self.rep % 2
        self.dx, self.dy, self.dc = 1 - 2 * self.x, 2 - 4 * self.y, 1 - 2 * self.c
        self.across_x = (self.dp + self.dx, self.rep)
        self.across_y = (self.dp, self.rep + self.dy)
        self.other_core = (self.dp, self.rep + self.dc)

    def plane(self, k):
        return ((self.z + k) % 4, self.x)

    def to_plane(self, k):
        return (((self.z + k) % 4) * 2 + self.x, self.rep)

    def from_plane(self, k):
        return ((self.z + 4 - k) % 4) * 2 + self.x

    def greet(self):
        barrier = pltpu.get_barrier_semaphore()
        peers = [self.to_plane(k) for k in (1, 2, 3)] + [self.across_x, self.across_y, self.other_core]
        for peer in peers:
            pl.semaphore_signal(barrier, inc=1, device_id=peer, device_id_type=MESH)
        pl.semaphore_wait(barrier, len(peers))


def remote(src, dst, send, recv, peer):
    return pltpu.make_async_remote_copy(
        src_ref=src, dst_ref=dst, send_sem=send, recv_sem=recv, device_id=peer, device_id_type=MESH
    )


def block_of(full, rep, dp, rows, cols):
    if len(full.shape) == 3:
        return full.at[rep, pl.ds(pl.multiple_of(dp * rows, rows), rows)]
    return full.at[pl.ds(pl.multiple_of(rep * rows, rows), rows), pl.ds(pl.multiple_of(dp * cols, cols), cols)]


def plane_of(full, rep, z, rows, cols):
    if len(full.shape) == 3:
        return full.at[rep, pl.ds(pl.multiple_of(z * 2 * rows, 2 * rows), 2 * rows)]
    lanes = pl.ds(pl.multiple_of(z * 2 * cols, 2 * cols), 2 * cols)
    return full.at[pl.ds(pl.multiple_of(rep * rows, rows), rows), lanes]


def gather_steps(shard, full, send, recv):
    me = Place()
    rows, cols = shard.shape
    blk = lambda rep, dp: block_of(full, rep, dp, rows, cols)
    rep_y = me.rep + me.dy
    src = lambda k: shard if k == 0 else blk(me.rep, me.from_plane(k))
    own = lambda k: blk(me.rep, me.from_plane(k))
    z_copy = lambda k: remote(shard, own(0), send.at[k - 1], recv.at[k - 1], me.to_plane(k))
    z_land = lambda k: remote(own(k), own(k), send.at[k - 1], recv.at[k - 1], me.to_plane(k))
    x_copy = lambda k: remote(src(k), own(k), send.at[3 + k], recv.at[3 + k], me.across_x)
    y_copy = lambda k: remote(src(k), own(k), send.at[7 + k], recv.at[7 + k], me.across_y)
    x_spot = lambda k: blk(me.rep, me.from_plane(k) + me.dx)
    y_spot = lambda k: blk(rep_y, me.from_plane(k))
    d_spot = lambda k: blk(rep_y, me.from_plane(k) + me.dx)
    x_land = lambda k: remote(x_spot(k), x_spot(k), send.at[3 + k], recv.at[3 + k], me.across_x)
    y_land = lambda k: remote(y_spot(k), y_spot(k), send.at[7 + k], recv.at[7 + k], me.across_y)
    d_land = lambda k: remote(d_spot(k), d_spot(k), send.at[11 + k], recv.at[11 + k], me.across_x)

    def d_copy(k):
        spot = blk(me.rep + (1 - me.c) * me.dy, me.from_plane(k) + me.c * me.dx)
        peer = (me.dp + (1 - me.c) * me.dx, me.rep + me.c * me.dy)
        return remote(spot, spot, send.at[11 + k], recv.at[11 + k], peer)

    pair = lambda rep, k: plane_of(full, rep, (me.z + 4 - k) % 4, rows, cols)
    mine = lambda j, k: pair(rep_y if j else me.rep, k)
    theirs = lambda j, k: pair((rep_y if j else me.rep) + me.dc, k)
    c_copy = lambda j, k: remote(mine(j, k), mine(j, k), send.at[15 + 4 * j + k], recv.at[15 + 4 * j + k], me.other_core)
    c_land = lambda j, k: remote(
        theirs(j, k), theirs(j, k), send.at[15 + 4 * j + k], recv.at[15 + 4 * j + k], me.other_core
    )
    place = lambda k: pltpu.make_async_copy(shard, own(k), send.at[23 + k])

    def spread(k):
        z_land(k).wait_recv()
        x_copy(k).start()
        y_copy(k).start()

    def forward(k):
        x_land(k).wait_recv()
        y_land(k).wait_recv()
        d_copy(k).start()

    def swap(k):
        if k == 0:
            place(k).wait()
        d_land(k).wait_recv()
        for j in range(2):
            c_copy(j, k).start()

    def end():
        for k in range(4):
            for j in range(2):
                c_land(j, k).wait_recv()
                c_copy(j, k).wait_send()
            if k:
                z_copy(k).wait_send()
            x_copy(k).wait_send()
            y_copy(k).wait_send()
            d_copy(k).wait_send()

    def reach():
        for k in (1, 3, 2):
            z_copy(k).start()
        place(0).start()

    def near():
        x_copy(0).start()
        y_copy(0).start()

    return types.SimpleNamespace(reach=reach, near=near, spread=spread, forward=forward, swap=swap, end=end)


class Comms:
    def __init__(self, *parts):
        self.parts = parts
        self.arrays = [a for part in parts for a in part.arrays]
        self.outputs = [o for part in parts for o in part.outputs]
        self.scratch = [s for part in parts for s in part.scratch]

    def plan(self, ins, outs, scratch):
        plans, i, o, s = [], 0, 0, 0
        for part in self.parts:
            ni, no, ns = len(part.arrays), len(part.outputs), len(part.scratch)
            plans.append(part.plan(ins[i : i + ni], outs[o : o + no], scratch[s : s + ns]))
            i, o, s = i + ni, o + no, s + ns

        def begin():
            Place().greet()
            for plan in plans:
                plan[0]()

        def end():
            for plan in plans:
                plan[2]()

        return begin, sorted((entry for plan in plans for entry in plan[1]), key=lambda entry: entry[0]), end


def scatter_ticks(g, parts, out, inside, send, recv):
    held, other, diag, near, far, planes = parts
    me = Place()
    first = (me.dp + (1 - me.c) * me.dx, me.rep + me.c * me.dy)
    second = (me.dp + me.c * me.dx, me.rep + (1 - me.c) * me.dy)
    flip_y, flip_x = 1 - 2 * me.y, me.dx
    at_first = (me.y + me.c * flip_y, me.x + (1 - me.c) * flip_x)
    at_second = (me.y + (1 - me.c) * flip_y, me.x + me.c * flip_x)
    at_diag = (me.y + flip_y, me.x + flip_x)
    c_copy = lambda j: remote(g.at[2 * j + 1 - me.c], other.at[j], send.at[j], recv.at[j], me.other_core)
    load = lambda j: pltpu.make_async_copy(g.at[2 * j + me.c], held.at[j], send.at[2 + j])
    region = lambda at: held.at[at[0], :, at[1]]
    diag_copy = remote(region(at_diag), diag, send.at[4], recv.at[4], first)
    near_copy = remote(region(at_first), near, send.at[5], recv.at[5], first)
    far_copy = remote(region(at_second), far, send.at[6], recv.at[6], second)
    z_copy = lambda k: remote(
        held.at[me.y, (me.z + k) % 4, me.x], planes.at[k - 1], send.at[6 + k], recv.at[6 + k], me.to_plane(k)
    )

    def add(spot, *terms):
        total = held[spot].astype(F32)
        for ref, i in terms:
            total = total + ref[i].astype(F32)
        held[spot] = total.astype(held.dtype)

    def begin():
        for j in range(2):
            c_copy(j).start()
            load(j).start()

    def fold(j):
        def run():
            c_copy(j).wait_recv()
            load(j).wait()

            @pl.loop(0, 4)
            def _(zz):
                for xx in range(2):
                    add((j, zz, xx), (other, (j, zz, xx)))

            if j == 1:
                diag_copy.start()
                near_copy.start()
        return run

    def pass_on():
        diag_copy.wait_recv()

        @pl.loop(0, 4)
        def _(zz):
            add((at_second[0], zz, at_second[1]), (diag, zz))

        far_copy.start()

    def planes_out():
        near_copy.wait_recv()
        far_copy.wait_recv()

        @pl.loop(0, 4)
        def _(zz):
            add((me.y, zz, me.x), (near, zz), (far, zz))

        if inside:
            for k in (1, 3, 2):
                z_copy(k).start()
        else:
            for k in range(4):
                out[k] = held[me.y, (me.z + k) % 4, me.x]

    def finish():
        if inside:
            total = held[me.y, me.z, me.x].astype(F32)
            for k in (1, 2, 3):
                z_copy(k).wait_recv()
                total = total + planes[k - 1].astype(F32)
            out[...] = total

    def end():
        for j in range(2):
            c_copy(j).wait_send()
        diag_copy.wait_send()
        near_copy.wait_send()
        far_copy.wait_send()
        if inside:
            for k in (1, 2, 3):
                z_copy(k).wait_send()

    return begin, [fold(0), fold(1), pass_on, planes_out, finish], end


class Scatter:
    def __init__(self, grads, inside=False):
        self.arrays, self.inside = list(grads), inside
        self.outputs, self.scratch = [], []
        for g in grads:
            a, b = g.shape[3:]
            out = jax.ShapeDtypeStruct((a, b), F32) if inside else jax.ShapeDtypeStruct((4, a, b), g.dtype)
            self.outputs.append((out, whole(out.shape)))
            planes = (3, a, b) if inside else (1, 8, 128)
            for shape in ((2, 4, 2, a, b), (2, 4, 2, a, b), (4, a, b), (4, a, b), (4, a, b), planes):
                self.scratch.append(pltpu.VMEM(shape, g.dtype))
        self.scratch += [pltpu.SemaphoreType.DMA((len(self.arrays), 10))] * 2

    def plan(self, grads, outs, scratch):
        send, recv = scratch[-2:]
        parts = [
            scatter_ticks(g, scratch[6 * i : 6 * i + 6], outs[i], self.inside, send.at[i], recv.at[i])
            for i, g in enumerate(grads)
        ]

        def begin():
            for part in parts:
                part[0]()

        def end():
            for part in parts:
                part[2]()

        timed = []
        for i, part in enumerate(parts):
            times = (3 + 4 * i, 5 + 4 * i, 12 + 13 * i, 29 + 17 * i, 100 + i)
            timed += list(zip(times, part[1]))
        return begin, timed, end


class PlaneScatter:
    def __init__(self, blocks):
        self.arrays = list(blocks)
        self.outputs, self.scratch = [], []
        for b in blocks:
            out = jax.ShapeDtypeStruct(b.shape[1:], F32)
            self.outputs.append((out, whole(out.shape)))
            self.scratch += [pltpu.VMEM(b.shape[1:], b.dtype), pltpu.VMEM((3, *b.shape[1:]), b.dtype)]
        self.scratch += [pltpu.SemaphoreType.DMA((len(self.arrays), 4)), pltpu.SemaphoreType.DMA((len(self.arrays), 3))]

    def plan(self, blocks, outs, scratch):
        me = Place()
        send, recv = scratch[-2:]
        each = []
        for i, b in enumerate(blocks):
            own, landed = scratch[2 * i : 2 * i + 2]
            copies = [remote(b.at[k], landed.at[k - 1], send.at[i, k], recv.at[i, k - 1], me.to_plane(k)) for k in (1, 3, 2)]
            each.append((pltpu.make_async_copy(b.at[0], own, send.at[i, 0]), copies, own, landed, outs[i]))

        def begin():
            for load, copies, *_ in each:
                load.start()
                for copy in copies:
                    copy.start()

        def end():
            for load, copies, own, landed, out in each:
                load.wait()
                for copy in copies:
                    copy.wait()
                total = own[...].astype(F32)
                for k in range(3):
                    total = total + landed[k].astype(F32)
                out[...] = total

        return begin, [], end


def run_at(step, sub, subs, steps, pace, timed):
    for s in range(steps):
        point = s * subs + sub
        chosen = [tick for t, tick in timed if round(t / pace) == point]
        if chosen:
            @pl.when(step == s)
            def _():
                for tick in chosen:
                    tick()


def run_rest(subs, steps, pace, timed):
    for t, tick in timed:
        if round(t / pace) >= subs * steps:
            tick()


def call(name, body, steps, ticked, subs, pace, inputs, outputs, scratch, comm, number):
    given = [] if comm is None else comm.arrays
    made = [] if comm is None else comm.outputs

    def kernel(*refs):
        cut, at = [], 0
        for size in (len(inputs), len(given), len(outputs), len(made), len(scratch)):
            cut.append(refs[at : at + size])
            at += size
        ins, c_in, outs, c_out, own = cut
        step = pl.program_id(0)
        if comm is None:
            after = body(step, lambda sub: None, ins, outs, own)
            if after:
                pl.when(step == steps - 1)(after)
            return
        begin, timed, end = comm.plan(c_in, c_out, refs[at:])
        pl.when(step == 0)(begin)
        after = body(step, lambda sub: run_at(step, sub, subs, ticked, pace, timed), ins, outs, own)

        @pl.when(step == steps - 1)
        def _():
            run_rest(subs, ticked, pace, timed)
            end()
            if after:
                after()

    return pl.pallas_call(
        kernel,
        grid=(steps,),
        in_specs=[spec for _, spec in inputs] + [ANY] * len(given),
        out_specs=[spec for _, spec in outputs] + [spec for _, spec in made],
        out_shape=[shape for shape, _ in outputs] + [shape for shape, _ in made],
        scratch_shapes=scratch + ([] if comm is None else comm.scratch),
        compiler_params=params(None if comm is None else number),
        name=name,
    )(*[a for a, _ in inputs], *given)


def full(a):
    return a, whole(a.shape)


def shape_of(*dims, dtype=BF):
    return jax.ShapeDtypeStruct(dims, dtype)


def gelu_parts(z):
    e = jnp.exp2(z * z * (-0.5 * LOG2E))
    den = 1.0 + (0.3275911 * 0.7071067811865476) * jnp.abs(z)
    t = pl.reciprocal(den, approx=True)
    t = t * (2.0 - den * t)
    poly = t * (0.127414796 + t * (-0.142248368 + t * (0.7107068705 + t * (-0.7265760135 + t * 0.5307027145))))
    tail = poly * e
    phi = jnp.where(z < 0, tail, 1.0 - tail)
    return z * phi, phi + z * (e * 0.3989422804014327)


def moments(v):
    centered = v - jnp.mean(v, axis=-1, keepdims=True)
    rs = lax.rsqrt(jnp.mean(centered * centered, axis=-1, keepdims=True) + 1e-05)
    return centered * rs, rs


def bias_bases(buckets, bias_table, n):
    selector = (buckets[:, None] == jnp.arange(bias_table.shape[0], dtype=jnp.int32)[None, :]).astype(F32)
    per_offset = jnp.dot(selector, bias_table.astype(F32), precision=lax.Precision.HIGHEST).T
    heads = per_offset.shape[0]
    zero = jnp.zeros((heads, 1), F32)
    base = jnp.concatenate([per_offset[:, n - 1 :], zero, per_offset[:, : n - 1]], axis=1)
    flipped = per_offset[:, ::-1]
    base_t = jnp.concatenate([flipped[:, n - 1 :], zero, flipped[:, : n - 1]], axis=1) * LOG2E
    return selector, base, base_t


def build_bias(h, base, base_t, bias, bias_t):
    n = bias.shape[1]
    for src, dst, at in ((base, bias, h), (base_t, bias_t, 0)):
        row = jnp.broadcast_to(src[h], (n, 2 * n))
        dst[at] = pltpu.roll(row, 0, 1, stride=1, stride_axis=0)[:, :n].astype(dst.dtype)


def build_masks(marks, mask, mask_t):
    n = mask.shape[1]
    rows = jnp.concatenate([ref[...] for ref in marks], axis=0).astype(F32)
    seg_r, perm_r, pred_r = rows[0:1], rows[1:2], rows[2:3]
    for lo in range(0, n, 128):
        at = slice(lo, lo + 128)

        def col(k):
            piece = jnp.broadcast_to(rows[k : k + 1, at], (128, 128))
            return piece.T[:, :1]

        seg_c, perm_c, pred_c = col(0), col(1), col(2)
        same = (seg_c == seg_r) & (seg_r != 6.0)
        shown = pred_r == 0.0
        mask[0, at, :] = jnp.where(same & (shown | (perm_r <= perm_c)), 0.0, NEG)
        mask[1, at, :] = jnp.where(same & (shown | (perm_r < perm_c)), 0.0, NEG)
        same = (seg_c == seg_r) & (seg_c != 6.0)
        shown = pred_c == 0.0
        mask_t[at, :n] = jnp.where(same & (shown | (perm_c <= perm_r)), 0.0, NEG)
        mask_t[at, n:] = jnp.where(same & (shown | (perm_c < perm_r)), 0.0, NEG)


def project_streams(raw, xy, vec, layer, q_o, k_o, v_o, pf, of):
    n, d = xy.shape[1:]
    pairs = d // 128
    w = pf.shape[1] // raw.shape[0]
    pf[...] = jnp.concatenate([raw[r, :, :w] for r in range(raw.shape[0])], axis=1)
    of[...] = jnp.concatenate([raw[r, :, w:] for r in range(raw.shape[0])], axis=1)
    bq, bv = vec[layer, 0:1], vec[layer, 1:2]
    x = xy[0]
    qc = nn(x, pf[:, :d]) + bq
    qq = nn(xy[1], pf[:, :d]) + bq
    kk = nn(x, pf[:, d : 2 * d])
    vv = nn(x, pf[:, 2 * d :]) + bv
    for c in range(pairs):
        at = slice(128 * c, 128 * c + 128)
        q_o[c, :n] = qc[:, at].astype(BF)
        q_o[c, n:] = qq[:, at].astype(BF)
        k_o[c] = kk[:, at].astype(BF)
        v_o[c] = vv[:, at].astype(BF)


def attend_pair(p, tick, bias, mask, q_o, k_o, v_o, ctx_o, lse_s):
    n = mask.shape[1]
    rows_at = n // 2
    k, v = k_o[p], v_o[p]
    lane = lax.broadcasted_iota(jnp.int32, (1, 128), 1)
    low = lane < 64
    vx = jnp.concatenate([v, jnp.ones_like(v)], axis=1)
    k0 = jnp.where(low, k, 0)
    k1 = jnp.where(low, 0, k)
    for s in range(2):
        for lo in range(0, n, rows_at):
            tick(2 * s + lo // rows_at)
            at = slice(lo, lo + rows_at)
            to = slice(s * n + lo, s * n + lo + rows_at)
            q = q_o[p, to]
            parts = []
            for hh, kh in ((0, k0), (1, k1)):
                sc = (nt(q, kh) * 0.125 + bias[2 * p + hh, at].astype(F32)) * LOG2E + mask[s, at]
                m = jnp.maximum(jnp.max(sc, axis=-1, keepdims=True), FLOOR)
                e = jnp.exp2(sc - m).astype(BF)
                r = nn(e, vx)
                tot = r[:, 128:]
                tot = jnp.where(tot > 0, tot, 1.0)
                lse = m + jnp.log2(tot)
                lse_s[to] = jnp.where(lane == 2 * p + hh, lse, lse_s[to])
                parts.append(r[:, :128] / tot)
            ctx_o[p, to] = jnp.where(low, parts[0], parts[1]).astype(BF)


TIMES = (0.1, 0.2, 0.3, 0.4, 0.45, 0.5, 0.55, 0.7, 0.8, 0.93)
DEPTH = 1


def forward_kernel(
    square, vec_shape, heads,
    x_in, y_in, seg, perm, pred, base, base_t, vec_one, vec_two, *refs,
):
    count = 6 if square else 7
    weights, refs = refs[:count], refs[count:]
    (bias_t, mask_t, q_o, k_o, v_o, ctx_h, lse_o, pf_h, of_h, xh1_o, nl_o, act_o, gp_o, xh2_o, rs1_o, rs2_o,
     ins_h, rc_o, rq_o, vec_o) = refs[:20]
    refs = refs[20:]
    if square:
        fulls, refs = refs[:7], refs[7:]
        vec_land, vec_src, send, recv = refs[-4:]
        weights = [vec_src, *weights]
    else:
        fulls = weights
    bias, mask, xy, raw, cts, act_s, second_s, lse_s, pf, of, ctx_o, load_sem = refs[:12]
    n, d = x_in.shape
    pairs = d // 128
    chunks, _, fw = raw.shape
    blocks = n // xh1_o.shape[0]
    tb = n // blocks
    step = pl.program_id(0)
    span = pairs + 4 * blocks
    layer = (step >= heads + span).astype(jnp.int32)
    spot = step - heads - layer * span
    starts = []
    for l in range(2):
        lo = heads + l * span
        starts += [lo, lo + pairs, lo + pairs + 2 * blocks]
    sizes = [pairs, 2 * blocks, 2 * blocks] * 2

    points = {}
    load = lambda j: pltpu.make_async_copy(fulls[1 + j], (raw, raw, cts)[j % 3], load_sem.at[0])

    def put(at, sub, *actions):
        points.setdefault((at, sub), []).extend(actions)

    if square:
        items = [gather_steps(w, f, send.at[i], recv.at[i]) for i, (w, f) in enumerate(zip(weights, fulls))]
        vec_item, items = items[0], items[1:]
        rows, cols = vec_shape
        do = lambda action, *ks: [functools.partial(action, k) for k in ks]

        def open_all():
            Place().greet()
            blocks = [jnp.pad(ref[...].astype(F32), ((0, 8 - rows), (0, 128 - cols))) for ref in (vec_one, vec_two)]
            vec_src[...] = jnp.concatenate(blocks, axis=0).astype(BF)
            vec_item.near()
            vec_item.reach()
            items[0].near()
            items[0].reach()

        put(0, 0, open_all)
        put(2, 0, *do(vec_item.spread, 1, 3, 2), *do(vec_item.forward, 0))
        put(4, 0, *do(vec_item.forward, 1, 2, 3), *do(items[0].spread, 1))
        put(6, 0, *do(vec_item.swap, 0, 1, 2, 3), *do(items[0].forward, 0))
        put(8, 0, *do(items[0].spread, 3))
        put(9, 0, *do(items[0].forward, 1), *do(items[0].swap, 0))
        put(10, 0, *do(items[0].spread, 2), items[1].reach)
        put(11, 0, *do(items[0].forward, 3), *do(items[0].swap, 1))
        def open_next(j):
            item = items[j] if j < 6 else None
            return [item.near, *do(item.spread, 1, 3, 2)] if item else []

        def reach(j):
            return [items[j].reach] if j < 6 else []

        first = [
            *do(items[0].forward, 2), *do(items[0].swap, 3), *open_next(1), *reach(2), *do(items[0].swap, 2),
            vec_item.end, items[0].end,
        ] + (open_next(2) + reach(3) if DEPTH == 2 else [])
        for j in range(1, 6):
            lo, count = starts[j - 1], sizes[j - 1] * 4
            item = items[j]
            t = TIMES
            plan = [
                (t[0], do(item.forward, 0)), (t[1], do(item.forward, 1)), (t[2], do(item.forward, 2)),
                (t[3], do(item.forward, 3)), (t[4], open_next(j + DEPTH)), (t[5], do(item.swap, 0)),
                (t[6], do(item.swap, 1) + reach(j + DEPTH + 1)), (t[7], do(item.swap, 2)), (t[8], do(item.swap, 3)),
                (t[9], [item.end, load(j).start]),
            ]
            for part, actions in plan:
                point = int(part * count)
                put(lo + point // 4, point % 4, *actions)

    def tick(sub):
        for (at, which), actions in points.items():
            if which == sub and actions:
                @pl.when(step == at)
                def _():
                    for action in actions:
                        action()

    def arrive(j, then=None):
        @pl.when(step == starts[j])
        def _():
            if square and j == 0:
                for action in first:
                    action()
            if not square or j == 0:
                load(j).start()
            if then:
                then()
            load(j).wait()

    def vectors():
        if not square:
            copy = pltpu.make_async_copy(weights[0], vec_o, load_sem.at[1])
            copy.start()
            copy.wait()
            return
        copy = pltpu.make_async_copy(fulls[0], vec_land, load_sem.at[1])
        copy.start()
        copy.wait()
        vec_o[...] = jnp.zeros_like(vec_o)
        for l in range(2):
            for r in range(4):
                pieces = [vec_land[r, 16 * i + 8 * l : 16 * i + 8 * l + rows, :cols] for i in range(d // cols)]
                vec_o[l, rows * r : rows * r + rows] = jnp.concatenate(pieces, axis=1).astype(F32)

    keep = lambda ref, out, sem: pltpu.make_async_copy(ref, out.at[layer], load_sem.at[sem])

    @pl.when(step < heads)
    def _():
        tick_prep = tick
        tick_prep(0)
        build_bias(step, base, base_t, bias, bias_t)

    @pl.when(step == 0)
    def _():
        build_masks((seg, perm, pred), mask, mask_t)
        xy[0] = x_in[...]
        xy[1] = y_in[...]
        keep(xy, ins_h, 5).start()
        keep(xy, ins_h, 5).wait()
        lse_s[...] = jnp.zeros_like(lse_s)

    arrive(0, vectors)
    arrive(3)

    @pl.when((spot >= 0) & (spot < pairs))
    def _():
        @pl.when(spot == 0)
        def _():
            project_streams(raw, xy, vec_o, layer, q_o, k_o, v_o, pf, of)
            keep(pf, pf_h, 2).start()
            keep(of, of_h, 3).start()

        attend_pair(spot, tick, bias, mask, q_o, k_o, v_o, ctx_o, lse_s)

        @pl.when(spot == pairs - 1)
        def _():
            for lo in range(0, 2 * n, 128):
                lse_o[:, lo : lo + 128] = lse_s[lo : lo + 128].T[: lse_o.shape[0]]
            keep(ctx_o, ctx_h, 4).start()
            keep(pf, pf_h, 2).wait()
            keep(of, of_h, 3).wait()

    arrive(1)
    arrive(4)

    @pl.when((spot >= pairs) & (spot < pairs + 2 * blocks))
    def _():
        t = spot - pairs
        rows = pl.ds(pl.multiple_of(t * tb, tb), tb)
        inner = pl.ds(pl.multiple_of(t % blocks * tb, tb), tb)
        vec = vec_o.at[layer]
        z = xy[t // blocks, inner].astype(F32)
        cx = jnp.concatenate([ctx_o[c, rows] for c in range(pairs)], axis=1)
        xh1, rs1 = moments(z + (nn(cx, of[...]) + vec[2:3]))
        normed = xh1 * vec[3:4] + vec[4:5]
        nl = normed.astype(BF)
        xh1_o[...] = xh1.astype(BF)
        nl_o[...] = nl
        rs1_o[...] = jnp.broadcast_to(rs1, rs1_o.shape)
        second_s[rows] = normed + vec[5:6]
        for f in range(chunks):
            tick(f)
            at = slice(f * fw, f * fw + fw)
            act, gp = gelu_parts(nn(nl, raw[f]) + vec[8 + f : 9 + f])
            act = act.astype(BF)
            act_o[:, at] = act
            act_s[rows, at] = act
            gp_o[:, at] = gp.astype(BF)

    arrive(2)
    arrive(5)

    @pl.when(spot >= pairs + 2 * blocks)
    def _():
        t = spot - pairs - 2 * blocks
        rows = pl.ds(pl.multiple_of(t * tb, tb), tb)
        inner = pl.ds(pl.multiple_of(t % blocks * tb, tb), tb)
        vec = vec_o.at[layer]
        second = second_s[rows]
        for f in range(chunks):
            tick(f)
            at = slice(f * fw, f * fw + fw)
            second = second + nt(act_s[rows, at], cts[:, at])
        xh2, rs2 = moments(second)
        xh2_o[...] = xh2.astype(BF)
        rs2_o[...] = jnp.broadcast_to(rs2, rs2_o.shape)
        res = (xh2 * vec[6:7] + vec[7:8]).astype(BF)

        @pl.when(t == 0)
        def _():
            keep(ctx_o, ctx_h, 4).wait()

        @pl.when(layer == 0)
        def _():
            xy[t // blocks, inner] = res

        @pl.when((layer == 0) & (t == 2 * blocks - 1))
        def _():
            copy = pltpu.make_async_copy(xy, ins_h.at[1], load_sem.at[5])
            copy.start()
            copy.wait()

        @pl.when((layer == 1) & (t < blocks))
        def _():
            rc_o[...] = res

        @pl.when((layer == 1) & (t >= blocks))
        def _():
            rq_o[...] = res


def forward(x, y, marks, base, base_t, vectors, weights, square, heads):
    n, d = x.shape
    pairs = d // 128
    reps = 4
    vec_shape = vectors[0].shape
    if square:
        rows = [(4, 8 * 16, 128)] + [(4, 8 * a.shape[0], a.shape[1]) for a in weights]
        rows[3] = rows[6] = (4 * weights[2].shape[0], 8 * weights[2].shape[1])
        made = [(shape_of(*s), ANY) for s in rows]
        fw = weights[1].shape[1]
    else:
        made = []
        fw = weights[2].shape[2]
    ff = reps * fw
    blocks = 2
    tb = n // blocks
    span = pairs + 4 * blocks
    layer = lambda s: jnp.where(s >= heads + span, 1, 0)
    tok = lambda s: jnp.clip(s - heads - layer(s) * span - pairs, 0, 2 * blocks - 1)
    down = lambda s: jnp.clip(s - heads - layer(s) * span - pairs - 2 * blocks, 0, 2 * blocks - 1)
    per_layer = lambda *dims: (shape_of(2, *dims), pl.BlockSpec((None, *dims), lambda s: (layer(s), *(0,) * len(dims))))
    f32_layer = lambda *dims: (shape_of(2, *dims, dtype=F32), pl.BlockSpec((None, *dims), lambda s: (layer(s), *(0,) * len(dims))))
    blocked = lambda width, at, dtype=BF: (
        shape_of(2, 2 * n, width, dtype=dtype), pl.BlockSpec((None, tb, width), lambda s: (layer(s), at(s), 0))
    )
    end = heads + 2 * span
    outputs = [
        (shape_of(heads, n, n, dtype=F32), pl.BlockSpec((1, n, n), lambda s: (jnp.minimum(s, heads - 1), 0, 0))),
        (shape_of(n, 2 * n, dtype=F32), whole((n, 2 * n))),
        per_layer(pairs, 2 * n, 128), per_layer(pairs, n, 128), per_layer(pairs, n, 128), (shape_of(2, pairs, 2 * n, 128), ANY),
        f32_layer(16, 2 * n), (shape_of(2, d, 3 * d), ANY), (shape_of(2, d, d), ANY),
        blocked(d, tok), blocked(d, tok), blocked(ff, tok), blocked(ff, tok), blocked(d, down),
        blocked(128, tok, F32), blocked(128, down, F32),
        (shape_of(2, 2, n, d), ANY),
        (shape_of(n, d), pl.BlockSpec((tb, d), lambda s: (jnp.clip(s - (end - 2 * blocks), 0, blocks - 1), 0))),
        (shape_of(n, d), pl.BlockSpec((tb, d), lambda s: (jnp.clip(s - (end - blocks), 0, blocks - 1), 0))),
        (shape_of(2, 16, d, dtype=F32), whole((2, 16, d))),
    ]
    scratch = [
        pltpu.VMEM((heads, n, n), BF), pltpu.VMEM((2, n, n), F32), pltpu.VMEM((2, n, d), BF),
        pltpu.VMEM((reps, d, fw), BF), pltpu.VMEM((d, ff), BF), pltpu.VMEM((2 * n, ff), BF),
        pltpu.VMEM((2 * n, d), F32), pltpu.VMEM((2 * n, 128), F32),
        pltpu.VMEM((d, 3 * d), BF), pltpu.VMEM((d, d), BF), pltpu.VMEM((pairs, 2 * n, 128), BF),
        pltpu.SemaphoreType.DMA((6,)),
    ]
    if square:
        scratch += [pltpu.VMEM(made[0][0].shape, BF), pltpu.VMEM((16, 128), BF)] + [pltpu.SemaphoreType.DMA((7, SEMS))] * 2
    outs = pl.pallas_call(
        functools.partial(forward_kernel, square, vec_shape, heads),
        grid=(end,),
        in_specs=[whole(a.shape) for a in (x, y, *marks)] + [whole((heads, 1, 2 * n))] * 2 + [whole(vec_shape)] * 2
        + [ANY] * len(weights),
        out_specs=[spec for _, spec in outputs + made],
        out_shape=[shape for shape, _ in outputs + made],
        scratch_shapes=scratch,
        compiler_params=params(1 if square else None),
        name="forward",
    )(x, y, *marks, base.reshape(heads, 1, 2 * n), base_t.reshape(heads, 1, 2 * n), *vectors, *weights)
    (bias_t, mask_t, q, k, v, ctx, lse, pf, of, xh1, nl, act, gp, xh2, rs1, rs2, both, rc, rq, vec) = outs[:20]
    fulls = outs[20:] if square else weights
    return types.SimpleNamespace(
        bias_t=bias_t, mask_t=mask_t, att=(q, k, v, lse, pf), post=(ctx, xh1, nl, gp, xh2, rs1, rs2, act, of),
        both=both, content=rc, query=rq, vec=vec, fulls=fulls[1:],
    )


def norm_back(g, xh, rs, gain):
    a = g * gain
    return rs * (a - jnp.mean(a, axis=-1, keepdims=True) - xh * jnp.mean(a * xh, axis=-1, keepdims=True))


def rowsum(v):
    return jnp.sum(v, axis=0, keepdims=True)


def post_bwd_body(step, tick, ins, outs, own):
    gc, gq, ctx, xh1, nl, gp, xh2, rs1, rs2, act, of, ew, ct, vec = ins
    first_o, gctx_o, vg_o, do_o, de_o, dc_o = outs
    gh_s, nl_t, gf_t, cx_t, ga_s = own
    t = step
    tb, d = gc.shape
    chunks, fw = ew.shape[0], ew.shape[2]
    blocks = chunks // 2

    @pl.when(t == 0)
    def _():
        vg_o[...] = jnp.zeros_like(vg_o)

    @pl.when(t < 2 * blocks)
    def _():
        g = jnp.where(t < blocks, gc[...].astype(F32), gq[...].astype(F32))
        xh = xh2[...].astype(F32)
        vg_o[6:7] += rowsum(g * xh)
        vg_o[7:8] += rowsum(g)
        gs = norm_back(g, xh, rs2[:, :1], vec[6:7])
        gf = gs.astype(BF)
        vg_o[5:6] += rowsum(gf.astype(F32))
        gn = gs
        spot = pl.ds(pl.multiple_of(t * tb, tb), tb)
        for f in range(chunks):
            tick(f)
            at = slice(f * fw, f * fw + fw)
            gh = (nn(gf, ct[:, at]) * gp[:, at].astype(F32)).astype(BF)
            gh_s[f, spot] = gh
            vg_o[8 + f : 9 + f] += rowsum(gh.astype(F32))
            gn = gn + nt(gh, ew[f])
        xh = xh1[...].astype(F32)
        vg_o[3:4] += rowsum(gn * xh)
        vg_o[4:5] += rowsum(gn)
        first = norm_back(gn, xh, rs1[:, :1], vec[3:4])
        first_o[...] = first
        ga = first.astype(BF)
        vg_o[2:3] += rowsum(ga.astype(F32))
        ga_s[spot] = ga
        gx = nt(ga, of[...]).astype(BF)
        cx = jnp.concatenate([ctx[c] for c in range(ctx.shape[0])], axis=1)
        for c in range(ctx.shape[0]):
            gctx_o[c] = gx[:, 128 * c : 128 * c + 128]
        nl_t[:, spot] = nl[...].T
        gf_t[:, spot] = gf.T
        cx_t[:, spot] = cx.T

    @pl.when(t == 2 * blocks)
    def _():
        do_o[...] = nn(cx_t[...], ga_s[...]).astype(BF)

    @pl.when(t >= 2 * blocks)
    def _():
        for i in range(chunks):
            tick(i)
        de_o[0] = nn(nl_t[...], gh_s[t - 2 * blocks]).astype(BF)
        dc = nn(gf_t[...], act[...]).astype(BF)
        if len(dc_o.shape) == 2:
            dc_o[...] = dc
        else:
            reps, across, a, b = dc_o.shape
            for r in range(reps):
                for x in range(across):
                    dc_o[r, x] = dc[a * r : a * r + a, b * x : b * x + b]


def post_bwd(layer, gc, gq, kept, ew, ct, vec, comm, number, split):
    ctx, xh1, nl, gp, xh2, rs1, rs2, act, of = kept
    n, d = gc.shape
    chunks, fw = ew.shape[0], ew.shape[2]
    ff = chunks * fw
    pairs = ctx.shape[1]
    blocks = chunks // 2
    tb = n // blocks
    last = 2 * blocks - 1
    tok = lambda width: pl.BlockSpec((tb, width), lambda t: (jnp.minimum(t, last), 0))
    tok3 = pl.BlockSpec((pairs, tb, 128), lambda t: (0, jnp.minimum(t, last), 0))
    kept_tok = lambda width: pl.BlockSpec((None, tb, width), lambda t: (layer, jnp.minimum(t, last), 0))
    of_layer = lambda a: (a, pl.BlockSpec((None, *a.shape[1:]), lambda t: (layer, 0, 0)))
    part = lambda t: jnp.maximum(t - last - 1, 0)
    if split:
        reps, owners = split
        across = owners // chunks
        dc = (
            shape_of(reps, owners, d // reps, ff // owners),
            pl.BlockSpec((reps, across, d // reps, ff // owners), lambda t: (0, part(t), 0, 0)),
        )
    else:
        dc = shape_of(d, ff), pl.BlockSpec((d, fw), lambda t: (0, part(t)))
    return call(
        "post_bwd", post_bwd_body, 2 * blocks + chunks, 2 * blocks + chunks, chunks, 1.7,
        [
            (gc, pl.BlockSpec((tb, d), lambda t: (jnp.minimum(t, blocks - 1), 0))),
            (gq, pl.BlockSpec((tb, d), lambda t: (jnp.clip(t - blocks, 0, blocks - 1), 0))),
            (ctx, pl.BlockSpec((None, pairs, tb, 128), lambda t: (layer, 0, jnp.minimum(t, last), 0))),
            (xh1, kept_tok(d)), (nl, kept_tok(d)), (gp, kept_tok(ff)), (xh2, kept_tok(d)),
            (rs1, kept_tok(128)), (rs2, kept_tok(128)),
            (act, pl.BlockSpec((None, 2 * n, fw), lambda t: (layer, 0, part(t)))),
            of_layer(of), full(ew), full(ct), of_layer(vec),
        ],
        [
            (shape_of(2 * n, d, dtype=F32), tok(d)), (shape_of(pairs, 2 * n, 128), tok3),
            (shape_of(16, d, dtype=F32), whole((16, d))), (shape_of(d, d), whole((d, d))),
            (shape_of(chunks, d, fw), pl.BlockSpec((1, d, fw), lambda t: (part(t), 0, 0))), dc,
        ],
        [
            pltpu.VMEM((chunks, 2 * n, fw), BF),
            pltpu.VMEM((d, 2 * n), BF), pltpu.VMEM((d, 2 * n), BF), pltpu.VMEM((d, 2 * n), BF),
            pltpu.VMEM((2 * n, d), BF),
        ],
        comm, number,
    )


def attn_bwd_body(layer, step, tick, ins, outs, own):
    q, k, v, go, lse, bias_t, mask_t, *late = ins
    gx_o, gy_o, dp_o, bg_o, t8_o = outs
    dq_s, dk_s, dv_s, diag, dk_a, dv_a, xy, first, pf, do, dp_s, sem = own
    p = step
    n, d = xy.shape[1:]
    pairs = d // 128
    wide = diag.shape[2]
    cols = n // 2

    both, first_h, pf_h, do_h = late
    loads = [
        pltpu.make_async_copy(both.at[layer], xy, sem.at[0]), pltpu.make_async_copy(first_h, first, sem.at[1]),
        pltpu.make_async_copy(pf_h.at[layer], pf, sem.at[2]), pltpu.make_async_copy(do_h, do, sem.at[3]),
    ]
    stores = [
        pltpu.make_async_copy(first.at[pl.ds(0, n)], gx_o, sem.at[4]),
        pltpu.make_async_copy(first.at[pl.ds(n, n)], gy_o, sem.at[5]), pltpu.make_async_copy(dp_s, dp_o, sem.at[6]),
    ]

    @pl.when(p == 0)
    def _():
        for copy in loads:
            copy.start()

    @pl.when(p < pairs)
    def _():
        low = lax.broadcasted_iota(jnp.int32, (1, 128), 1) < 64
        only = lambda a, hh: jnp.where(low, a, 0) if hh == 0 else jnp.where(low, 0, a)
        diag[...] = jnp.zeros_like(diag)
        ka, va = k[0], v[0]
        for i, lo in enumerate(range(0, 2 * n, cols)):
            tick(i)
            at = slice(lo, lo + cols)
            i0 = lo % n
            qa, ga = q[0, at], go[0, at]
            dq = dk = dv = None
            for hh in range(2):
                km, vm = only(ka, hh), only(va, hh)
                lrow = lse[pl.ds(2 * p + hh, 1), at]
                sc = nt(km, qa) * (0.125 * LOG2E) + (bias_t[hh, :, i0 : i0 + cols] + mask_t[:, at])
                pr = jnp.exp2(sc - lrow)
                gp = nt(vm, ga)
                ds = pr * (gp - rowsum(pr * gp))
                dsb = ds.astype(BF)
                dv_h = nn(pr.astype(BF), only(ga, hh))
                dk_h = nn(dsb, only(qa, hh))
                dq_h = tn(dsb, km)
                dq, dk, dv = (dq_h, dk_h, dv_h) if hh == 0 else (dq + dq_h, dk + dk_h, dv + dv_h)
                for b in range(n // 128):
                    off = n - 128 - 128 * b + i0
                    diag[hh, :, off : off + cols] += ds[128 * b : 128 * b + 128]
            dq_s[p, at] = (dq * 0.125).astype(BF)
            if i == 0:
                dk_a[...] = dk
                dv_a[...] = dv
            else:
                dk_a[...] += dk
                dv_a[...] += dv
        dk_s[p] = (dk_a[...] * 0.125).astype(BF)
        dv_s[p] = dv_a[...].astype(BF)
        for hh in range(2):
            total = jnp.zeros((8, 2 * n), F32)
            for g in range(16):
                piece = jnp.concatenate([diag[hh, 8 * g : 8 * g + 8], jnp.zeros((8, 2 * n - wide), F32)], axis=1)
                total = total + (pltpu.roll(piece, 2 * n - 8 * g, 1) if g else piece)
            t8_o[hh] = total

    @pl.when(p == pairs)
    def _():
        for copy in loads:
            copy.wait()
        cat = lambda ref, at: jnp.concatenate([ref[c, at] for c in range(pairs)], axis=1)
        gqc, gqq = cat(dq_s, slice(0, n)), cat(dq_s, slice(n, 2 * n))
        gk, gv = cat(dk_s, slice(0, n)), cat(dv_s, slice(0, n))
        first[:n] = first[:n] + nt(gqc, pf[:, :d]) + nt(gk, pf[:, d : 2 * d]) + nt(gv, pf[:, 2 * d :])
        first[n:] = first[n:] + nt(gqq, pf[:, :d])
        stores[0].start()
        stores[1].start()
        bg_o[...] = jnp.zeros_like(bg_o)
        bg_o[0:1] = rowsum(gqc.astype(F32)) + rowsum(gqq.astype(F32))
        bg_o[1:2] = rowsum(gv.astype(F32))
        xt, yt = xy[0].T, xy[1].T
        grads = jnp.concatenate([
            (nn(xt, gqc) + nn(yt, gqq)).astype(BF),
            nn(xt, gk).astype(BF), nn(xt, gv).astype(BF)], axis=1)
        reps = dp_s.shape[0]
        w, u = 3 * d // reps, d // reps
        for r in range(reps):
            sides = [grads[:, r * w : r * w + w], do[:, r * u : r * u + u]]
            dp_s[r] = jnp.concatenate(sides, axis=1)
        stores[2].start()

    def after():
        for copy in stores:
            copy.wait()

    return after


def attn_bwd(layer, kept, go, bias_t, mask_t, both, first, do, reps, comm, number):
    q, k, v, lse, pf = kept
    n, d = first.shape[0] // 2, first.shape[1]
    packed = (reps, d, 4 * d // reps)
    pairs = d // 128
    pair = lambda *block: pl.BlockSpec(block, lambda p: (jnp.minimum(p, pairs - 1), 0, 0))
    kept_pair = lambda rows: pl.BlockSpec((None, 1, rows, 128), lambda p: (layer, jnp.minimum(p, pairs - 1), 0, 0))
    of_layer = lambda a: (a, pl.BlockSpec((None, *a.shape[1:]), lambda t: (layer, 0, 0)))
    return call(
        "attn_bwd", functools.partial(attn_bwd_body, layer), pairs + 1, pairs, 4, 1.5,
        [
            (q, kept_pair(2 * n)), (k, kept_pair(n)), (v, kept_pair(n)), (go, pair(1, 2 * n, 128)),
            of_layer(lse), (bias_t, pair(2, n, n)), full(mask_t),
            (both, ANY), (first, ANY), (pf, ANY), (do, ANY),
        ],
        [
            (shape_of(n, d, dtype=F32), ANY), (shape_of(n, d, dtype=F32), ANY),
            (shape_of(*packed), ANY), (shape_of(8, d, dtype=F32), whole((8, d))),
            (shape_of(2 * pairs, 8, 2 * n, dtype=F32), pair(2, 8, 2 * n)),
        ],
        [
            pltpu.VMEM((pairs, 2 * n, 128), BF),
            pltpu.VMEM((pairs, n, 128), BF), pltpu.VMEM((pairs, n, 128), BF),
            pltpu.VMEM((2, 128, 2 * n - 128), F32), pltpu.VMEM((n, 128), F32), pltpu.VMEM((n, 128), F32),
            pltpu.VMEM((2, n, d), BF), pltpu.VMEM((2 * n, d), F32), pltpu.VMEM((d, 3 * d), BF), pltpu.VMEM((d, d), BF),
            pltpu.VMEM(packed, BF), pltpu.SemaphoreType.DMA((7,)),
        ],
        comm, number,
    )


def offset_sums(t8, n):
    total = sum(jnp.roll(t8[:, r], -(n - 128 + r), axis=1) for r in range(t8.shape[1]))
    return jnp.concatenate([total[:, 1:n][:, ::-1], total[:, :1], total[:, n + 1 :][:, ::-1]], axis=1)


def turn(v, shift):
    return pltpu.roll(v, v.shape[1] - shift, 1)


def table_sums(first, second, places, n):
    heads, eight, wide = first.shape
    v = turn((first[...] + second[...]).reshape(heads * eight, wide), n - 128)
    row = lax.broadcasted_iota(jnp.int32, (heads * eight, 1), 0) % eight
    for bit in (1, 2, 4):
        v = jnp.where(row // bit % 2 == 1, turn(v, bit), v)
    sums = jnp.sum(v.reshape(heads, eight, wide), axis=1)
    pick = jnp.where(lax.broadcasted_iota(jnp.int32, (32, wide), 0) == places[...], 1.0, 0.0).astype(BF)
    out = 0.0
    for _ in range(3):
        piece = sums.astype(BF)
        out = out + nt(pick, piece)
        sums = sums - piece.astype(F32)
    return out


def table_ticks(own, table, held, landed, planes, send, recv):
    me = Place()
    peers = (me.other_core, me.across_x, me.across_y)
    step = lambda s: remote(held.at[s], landed.at[s], send.at[s], recv.at[s], peers[s])
    z_copy = lambda k: remote(held.at[3], planes.at[me.z], send.at[2 + k], recv.at[2 + k], me.to_plane(k))
    z_land = lambda k: remote(held.at[3], planes.at[me.from_plane(k) // 2], send.at[2 + k], recv.at[2 + k], me.to_plane(k))

    def begin():
        held[0] = own()
        step(0).start()

    def next_step(s):
        def run():
            step(s).wait_recv()
            held[s + 1] = held[s] + landed[s]
            if s < 2:
                step(s + 1).start()
            else:
                planes[me.z] = held[3]
                for k in (1, 2, 3):
                    z_copy(k).start()
        return run

    def end():
        for k in (1, 2, 3):
            z_land(k).wait_recv()
        table[...] = (planes[0] + planes[1]) + (planes[2] + planes[3])
        for s in range(3):
            step(s).wait_send()
        for k in (1, 2, 3):
            z_copy(k).wait_send()

    return begin, [next_step(s) for s in range(3)], end


class Table:
    def __init__(self, t8_one, t8_two, places):
        vmem = pl.BlockSpec(memory_space=pltpu.VMEM)
        self.arrays = []
        self.inputs = [(t8_one, vmem), (t8_two, vmem), (places, vmem)]
        self.outputs = [(shape_of(32, 128, dtype=F32), vmem)]
        self.scratch = [
            pltpu.VMEM((4, 32, 128), F32), pltpu.VMEM((3, 32, 128), F32), pltpu.VMEM((4, 32, 128), F32),
            pltpu.SemaphoreType.DMA((6,)), pltpu.SemaphoreType.DMA((6,)),
        ]

    def plan(self, ins, outs, scratch):
        t8_one, t8_two, places = self.refs
        heads, _, wide = t8_one.shape

        def own():
            sums = table_sums(t8_one, t8_two, places, wide // 2)
            return jnp.concatenate([sums, jnp.zeros((sums.shape[0], 128 - heads), F32)], axis=1)

        begin, ticks, end = table_ticks(own, outs[0], *scratch)
        return begin, [(6 + 5 * i, tick) for i, tick in enumerate(ticks)], end


def tail_kernel(table, comm, *refs):
    table.refs = refs[:3]
    at = 3 + len(comm.arrays)
    to = at + len(comm.outputs)
    begin, timed, end = comm.plan(refs[3:at], refs[at:to], refs[to:])
    begin()
    for _, tick in timed:
        tick()
    end()


def tail(table, comm, number):
    return pl.pallas_call(
        functools.partial(tail_kernel, table, comm),
        in_specs=[spec for _, spec in table.inputs] + [ANY] * len(comm.arrays),
        out_specs=[spec for _, spec in comm.outputs],
        out_shape=[shape for shape, _ in comm.outputs],
        scratch_shapes=comm.scratch,
        compiler_params=params(number),
        name="tail",
    )(*[a for a, _ in table.inputs], *comm.arrays)


def closing_kernel(heads, table_in, vecs, po1, c1, po2, c2, *refs):
    moved, outs = refs[:6], refs[6:21]
    x, y, gx, gy, table, p1, o1, e1, w1, v1, p2, o2, e2, w2, v2 = outs
    for src, dst in zip(moved, (x, y, gx, gy, e1, e2)):
        dst[...] = src[...]
    table[...] = table_in[...].T[:heads]
    rows, cols = v1.shape
    cut = p1.shape[1]
    p1[...] = po1[:, :cut]
    o1[...] = po1[:, cut:]
    w1[...] = c1[...]
    v1[...] = vecs[:rows, :cols]
    p2[...] = po2[:, :cut]
    o2[...] = po2[:, cut:]
    w2[...] = c2[...]
    v2[...] = vecs[rows : 2 * rows, :cols]


def closing(shape, heads, vec_shape, cut, x, y, gx, gy, table, vecs, po1, e1, c1, po2, e2, c2):
    vmem = pl.BlockSpec(memory_space=pltpu.VMEM)
    f32 = lambda *dims: (shape_of(*dims, dtype=F32), vmem)
    grads = lambda po, e, c: [
        f32(po.shape[0], cut), f32(po.shape[0], po.shape[1] - cut), (shape_of(*e.shape, dtype=F32), vmem),
        f32(*c.shape), f32(*vec_shape),
    ]
    outputs = [(shape_of(*a.shape, dtype=a.dtype), vmem) for a in (x, y, gx, gy)] + [f32(heads, table.shape[0])]
    outputs += grads(po1, e1, c1) + grads(po2, e2, c2)
    outs = pl.pallas_call(
        functools.partial(closing_kernel, heads),
        in_specs=[vmem] * 12,
        out_specs=[spec for _, spec in outputs],
        out_shape=[out for out, _ in outputs],
        compiler_params=params(),
        name="closing",
    )(table, vecs, po1, c1, po2, c2, x, y, gx, gy, e1, e2)
    outs = [a.reshape(shape) for a in outs[:4]] + list(outs[4:])
    for i in (4, 8, 13):
        outs[i] = outs[i].T
    return tuple(outs)


def plain_gather(both, expand, contract, vectors):
    rows = lambda a, dim: lax.all_gather(a, "dp", axis=dim, tiled=True)
    po = lax.all_gather(rows(both, 0), "rep", axis=0)
    ew = lax.all_gather(rows(expand, 0), "rep", axis=0)
    ct = lax.all_gather(rows(contract, 1), "rep", axis=0, tiled=True)
    vec = lax.all_gather(rows(vectors, 1), "rep", axis=0, tiled=True).astype(F32)
    return po, ew, ct, vec


def scatter_sum(a, rep_dim, dp_dim):
    a = lax.psum_scatter(a, "rep", scatter_dimension=rep_dim, tiled=True)
    return lax.psum_scatter(a, "dp", scatter_dimension=dp_dim, tiled=True).astype(F32)


def shards(
    square,
    content_stream, query_stream, segments, perm_order, predicted, buckets, bias_table,
    project_one, output_one, expand_one, contract_one, vectors_one,
    project_two, output_two, expand_two, contract_two, vectors_two,
    content_cotangent, query_cotangent,
):
    shape = content_stream.shape
    n, d = shape[1:]
    reps = 3 * d // project_one.shape[1]
    flat = lambda a: a.reshape(n, d)
    selector, base, base_t = bias_bases(buckets, bias_table, n)
    one = (jnp.concatenate([project_one, output_one], axis=1), expand_one, contract_one.T, vectors_one)
    two = (jnp.concatenate([project_two, output_two], axis=1), expand_two, contract_two.T, vectors_two)
    rows, cols = vectors_one.shape
    if square:
        weights = [*one[:3], *two[:3]]
    else:
        full_one, full_two = plain_gather(*one), plain_gather(*two)
        both = jnp.pad(jnp.stack([full_one[3], full_two[3]]), ((0, 0), (0, 16 - 4 * rows), (0, 0)))
        weights = [both, *full_one[:3], *full_two[:3]]
    kept = forward(
        flat(content_stream), flat(query_stream), (segments, perm_order, predicted), base, base_t,
        (vectors_one, vectors_two), weights, square, bias_table.shape[1],
    )
    bias_t, mask_t = kept.bias_t, kept.mask_t
    ew, ct = (kept.fulls[1], kept.fulls[4]), (kept.fulls[2], kept.fulls[5])
    x, y = kept.content, kept.query
    def back_post(layer, gx, gy, comm, number):
        split = (4, 8) if square else None
        return post_bwd(layer, gx, gy, kept.post, ew[layer], ct[layer], kept.vec, comm, number, split)

    def back_attn(layer, gctx, first, do, comm, number):
        return attn_bwd(layer, kept.att, gctx, bias_t, mask_t, kept.both, first, do, reps, comm, number)

    pieces = lambda a: a.reshape(4, 4, 2, a.shape[-2] if a.ndim == 4 else a.shape[1] // 8, a.shape[-1])
    sent = lambda grads, blocks: Comms(Scatter([pieces(a) for a in grads]), *[PlaneScatter(b) for b in blocks]) if square else None
    first, gctx, vg_two, do, de_two, dc_two = back_post(
        1, flat(content_cotangent), flat(query_cotangent), None, 0
    )
    gx, gy, dp_two, bg_two, t8_two, *out_two = back_attn(1, gctx, first, do, sent([dc_two], []), 5)
    first, gctx, vg_one, do, de_one, dc_one, *out_mid = back_post(0, gx, gy, sent([de_two, dp_two], [out_two]), 6)
    gx, gy, dp_one, bg_one, t8_one, *out_one = back_attn(
        0, gctx, first, do, sent([dc_one, de_one], [out_mid[:2]]), 7
    )
    vg_one = jnp.concatenate([bg_one[:2], vg_one[2:12]], axis=0)
    vg_two = jnp.concatenate([bg_two[:2], vg_two[2:12]], axis=0)
    cut = project_one.shape[1]
    if square:
        vgs = jnp.stack([vg_one, vg_two]).reshape(2, 4, rows, 8, cols).transpose(1, 3, 0, 2, 4)
        vgs = jnp.pad(vgs.reshape(4, 8, 2 * rows, cols), ((0, 0), (0, 0), (0, 8 - 2 * rows), (0, 128 - cols)))
        turned = buckets[::-1]
        places = jnp.concatenate([turned[n - 1 :], -jnp.ones((1,), jnp.int32), turned[: n - 1]])[None]
        table = Table(t8_one, t8_two, places)
        out_p1, vecs, table, *ce_one = tail(
            table, Comms(Scatter([pieces(dp_one), pieces(vgs)], True), table, PlaneScatter(out_one[:2])), 8
        )
        return closing(
            shape, bias_table.shape[1], (rows, cols), cut, x, y, gx, gy, table, vecs,
            out_p1, ce_one[1], ce_one[0], out_one[3], out_one[2], out_mid[2],
        )
    else:
        distances = offset_sums(t8_one + t8_two, n)
        table = jnp.dot(selector.T, distances.T, precision=lax.Precision.HIGHEST)
        table = lax.psum(table, ("dp", "rep"))

        def spread(dp, de, dc, vec):
            po = scatter_sum(dp, 0, 1)[0]
            return po[:, :cut], po[:, cut:], scatter_sum(de, 0, 1)[0], scatter_sum(dc, 0, 1).T, scatter_sum(vec, 0, 1)

        grads_one = spread(dp_one, de_one, dc_one, vg_one)
        grads_two = spread(dp_two, de_two, dc_two, vg_two)
    return (
        x.reshape(shape), y.reshape(shape), gx.reshape(shape), gy.reshape(shape), table,
        *grads_one, *grads_two,
    )


def solution(mesh):
    rows3, rows2 = P(("dp", "rep"), None, None), P(("dp", "rep"), None)
    weights = (P("dp", "rep"),) * 4 + (P("rep", "dp"),)
    square = mesh.shape["dp"] == 8 and mesh.shape["rep"] == 4
    return jax.shard_map(
        functools.partial(shards, square),
        mesh=mesh,
        in_specs=(rows3, rows3, rows2, rows2, rows2, P(), P(), *weights, *weights, rows3, rows3),
        out_specs=(rows3, rows3, rows3, rows3, P(), *weights, *weights),
        check_vma=False,
    )
```

```python
import functools
import types
import jax
import jax.numpy as jnp
from jax import lax
from jax.experimental import pallas as pl
from jax.experimental.pallas import tpu as pltpu
from jax.sharding import PartitionSpec as P

F32 = jnp.float32
BF = jnp.bfloat16
LOG2E = 1.4426950408889634
NEG = -1e30
FLOOR = -1e29
VM = 60 * 1024 * 1024
NT = (((1,), (1,)), ((), ()))
TN = (((0,), (0,)), ((), ()))


def nt(a, b):
    return lax.dot_general(a, b, NT, preferred_element_type=F32)


def tn(a, b):
    return lax.dot_general(a, b, TN, preferred_element_type=F32)


def nn(a, b):
    return jnp.dot(a, b, preferred_element_type=F32)


def whole(shape):
    return pl.BlockSpec(shape, lambda *_: (0,) * len(shape))


def params(number=None):
    if number is None:
        return pltpu.CompilerParams(vmem_limit_bytes=VM)
    return pltpu.CompilerParams(vmem_limit_bytes=VM, collective_id=number, has_side_effects=True)


MESH = pl.DeviceIdType.MESH
ANY = pl.BlockSpec(memory_space=pl.ANY)
SEMS = 24


class Place:
    def __init__(self):
        self.dp = lax.axis_index("dp")
        self.rep = lax.axis_index("rep")
        self.z, self.x = self.dp // 2, self.dp % 2
        self.y, self.c = self.rep // 2, self.rep % 2
        self.dx, self.dy, self.dc = 1 - 2 * self.x, 2 - 4 * self.y, 1 - 2 * self.c
        self.across_x = (self.dp + self.dx, self.rep)
        self.across_y = (self.dp, self.rep + self.dy)
        self.other_core = (self.dp, self.rep + self.dc)

    def plane(self, k):
        return ((self.z + k) % 4, self.x)

    def to_plane(self, k):
        return (((self.z + k) % 4) * 2 + self.x, self.rep)

    def from_plane(self, k):
        return ((self.z + 4 - k) % 4) * 2 + self.x

    def greet(self):
        barrier = pltpu.get_barrier_semaphore()
        peers = [self.to_plane(k) for k in (1, 2, 3)] + [self.across_x, self.across_y, self.other_core]
        for peer in peers:
            pl.semaphore_signal(barrier, inc=1, device_id=peer, device_id_type=MESH)
        pl.semaphore_wait(barrier, len(peers))


def remote(src, dst, send, recv, peer):
    return pltpu.make_async_remote_copy(
        src_ref=src, dst_ref=dst, send_sem=send, recv_sem=recv, device_id=peer, device_id_type=MESH
    )


def block_of(full, rep, dp, rows, cols):
    if len(full.shape) == 3:
        return full.at[rep, pl.ds(pl.multiple_of(dp * rows, rows), rows)]
    return full.at[pl.ds(pl.multiple_of(rep * rows, rows), rows), pl.ds(pl.multiple_of(dp * cols, cols), cols)]


def plane_of(full, rep, z, rows, cols):
    if len(full.shape) == 3:
        return full.at[rep, pl.ds(pl.multiple_of(z * 2 * rows, 2 * rows), 2 * rows)]
    lanes = pl.ds(pl.multiple_of(z * 2 * cols, 2 * cols), 2 * cols)
    return full.at[pl.ds(pl.multiple_of(rep * rows, rows), rows), lanes]


def gather_steps(shard, full, send, recv):
    me = Place()
    rows, cols = shard.shape
    blk = lambda rep, dp: block_of(full, rep, dp, rows, cols)
    rep_y = me.rep + me.dy
    src = lambda k: shard if k == 0 else blk(me.rep, me.from_plane(k))
    own = lambda k: blk(me.rep, me.from_plane(k))
    z_copy = lambda k: remote(shard, own(0), send.at[k - 1], recv.at[k - 1], me.to_plane(k))
    z_land = lambda k: remote(own(k), own(k), send.at[k - 1], recv.at[k - 1], me.to_plane(k))
    x_copy = lambda k: remote(src(k), own(k), send.at[3 + k], recv.at[3 + k], me.across_x)
    y_copy = lambda k: remote(src(k), own(k), send.at[7 + k], recv.at[7 + k], me.across_y)
    x_spot = lambda k: blk(me.rep, me.from_plane(k) + me.dx)
    y_spot = lambda k: blk(rep_y, me.from_plane(k))
    d_spot = lambda k: blk(rep_y, me.from_plane(k) + me.dx)
    x_land = lambda k: remote(x_spot(k), x_spot(k), send.at[3 + k], recv.at[3 + k], me.across_x)
    y_land = lambda k: remote(y_spot(k), y_spot(k), send.at[7 + k], recv.at[7 + k], me.across_y)
    d_land = lambda k: remote(d_spot(k), d_spot(k), send.at[11 + k], recv.at[11 + k], me.across_x)

    def d_copy(k):
        spot = blk(me.rep + (1 - me.c) * me.dy, me.from_plane(k) + me.c * me.dx)
        peer = (me.dp + (1 - me.c) * me.dx, me.rep + me.c * me.dy)
        return remote(spot, spot, send.at[11 + k], recv.at[11 + k], peer)

    pair = lambda rep, k: plane_of(full, rep, (me.z + 4 - k) % 4, rows, cols)
    mine = lambda j, k: pair(rep_y if j else me.rep, k)
    theirs = lambda j, k: pair((rep_y if j else me.rep) + me.dc, k)
    c_copy = lambda j, k: remote(mine(j, k), mine(j, k), send.at[15 + 4 * j + k], recv.at[15 + 4 * j + k], me.other_core)
    c_land = lambda j, k: remote(
        theirs(j, k), theirs(j, k), send.at[15 + 4 * j + k], recv.at[15 + 4 * j + k], me.other_core
    )
    place = lambda k: pltpu.make_async_copy(shard, own(k), send.at[23 + k])

    def spread(k):
        z_land(k).wait_recv()
        x_copy(k).start()
        y_copy(k).start()

    def forward(k):
        x_land(k).wait_recv()
        y_land(k).wait_recv()
        d_copy(k).start()

    def swap(k):
        if k == 0:
            place(k).wait()
        d_land(k).wait_recv()
        for j in range(2):
            c_copy(j, k).start()

    def end():
        for k in range(4):
            for j in range(2):
                c_land(j, k).wait_recv()
                c_copy(j, k).wait_send()
            if k:
                z_copy(k).wait_send()
            x_copy(k).wait_send()
            y_copy(k).wait_send()
            d_copy(k).wait_send()

    def reach():
        for k in (1, 3, 2):
            z_copy(k).start()
        place(0).start()

    def near():
        x_copy(0).start()
        y_copy(0).start()

    return types.SimpleNamespace(reach=reach, near=near, spread=spread, forward=forward, swap=swap, end=end)


class Comms:
    def __init__(self, *parts):
        self.parts = parts
        self.arrays = [a for part in parts for a in part.arrays]
        self.outputs = [o for part in parts for o in part.outputs]
        self.scratch = [s for part in parts for s in part.scratch]

    def plan(self, ins, outs, scratch):
        plans, i, o, s = [], 0, 0, 0
        for part in self.parts:
            ni, no, ns = len(part.arrays), len(part.outputs), len(part.scratch)
            plans.append(part.plan(ins[i : i + ni], outs[o : o + no], scratch[s : s + ns]))
            i, o, s = i + ni, o + no, s + ns

        def begin():
            Place().greet()
            for plan in plans:
                plan[0]()

        def end():
            for plan in plans:
                plan[2]()

        return begin, sorted((entry for plan in plans for entry in plan[1]), key=lambda entry: entry[0]), end


def scatter_ticks(g, parts, out, inside, send, recv):
    held, other, diag, near, far, planes = parts
    me = Place()
    first = (me.dp + (1 - me.c) * me.dx, me.rep + me.c * me.dy)
    second = (me.dp + me.c * me.dx, me.rep + (1 - me.c) * me.dy)
    flip_y, flip_x = 1 - 2 * me.y, me.dx
    at_first = (me.y + me.c * flip_y, me.x + (1 - me.c) * flip_x)
    at_second = (me.y + (1 - me.c) * flip_y, me.x + me.c * flip_x)
    at_diag = (me.y + flip_y, me.x + flip_x)
    c_copy = lambda j: remote(g.at[2 * j + 1 - me.c], other.at[j], send.at[j], recv.at[j], me.other_core)
    load = lambda j: pltpu.make_async_copy(g.at[2 * j + me.c], held.at[j], send.at[2 + j])
    region = lambda at: held.at[at[0], :, at[1]]
    diag_copy = remote(region(at_diag), diag, send.at[4], recv.at[4], first)
    near_copy = remote(region(at_first), near, send.at[5], recv.at[5], first)
    far_copy = remote(region(at_second), far, send.at[6], recv.at[6], second)
    z_copy = lambda k: remote(
        held.at[me.y, (me.z + k) % 4, me.x], planes.at[k - 1], send.at[6 + k], recv.at[6 + k], me.to_plane(k)
    )

    def add(spot, *terms):
        total = held[spot].astype(F32)
        for ref, i in terms:
            total = total + ref[i].astype(F32)
        held[spot] = total.astype(held.dtype)

    def begin():
        for j in range(2):
            c_copy(j).start()
            load(j).start()

    def fold(j):
        def run():
            c_copy(j).wait_recv()
            load(j).wait()

            @pl.loop(0, 4)
            def _(zz):
                for xx in range(2):
                    add((j, zz, xx), (other, (j, zz, xx)))

            if j == 1:
                diag_copy.start()
                near_copy.start()
        return run

    def pass_on():
        diag_copy.wait_recv()

        @pl.loop(0, 4)
        def _(zz):
            add((at_second[0], zz, at_second[1]), (diag, zz))

        far_copy.start()

    def planes_out():
        near_copy.wait_recv()
        far_copy.wait_recv()

        @pl.loop(0, 4)
        def _(zz):
            add((me.y, zz, me.x), (near, zz), (far, zz))

        if inside:
            for k in (1, 3, 2):
                z_copy(k).start()
        else:
            for k in range(4):
                out[k] = held[me.y, (me.z + k) % 4, me.x]

    def finish():
        if inside:
            total = held[me.y, me.z, me.x].astype(F32)
            for k in (1, 2, 3):
                z_copy(k).wait_recv()
                total = total + planes[k - 1].astype(F32)
            out[...] = total

    def end():
        for j in range(2):
            c_copy(j).wait_send()
        diag_copy.wait_send()
        near_copy.wait_send()
        far_copy.wait_send()
        if inside:
            for k in (1, 2, 3):
                z_copy(k).wait_send()

    return begin, [fold(0), fold(1), pass_on, planes_out, finish], end


class Scatter:
    def __init__(self, grads, inside=False):
        self.arrays, self.inside = list(grads), inside
        self.outputs, self.scratch = [], []
        for g in grads:
            a, b = g.shape[3:]
            out = jax.ShapeDtypeStruct((a, b), F32) if inside else jax.ShapeDtypeStruct((4, a, b), g.dtype)
            self.outputs.append((out, whole(out.shape)))
            planes = (3, a, b) if inside else (1, 8, 128)
            for shape in ((2, 4, 2, a, b), (2, 4, 2, a, b), (4, a, b), (4, a, b), (4, a, b), planes):
                self.scratch.append(pltpu.VMEM(shape, g.dtype))
        self.scratch += [pltpu.SemaphoreType.DMA((len(self.arrays), 10))] * 2

    def plan(self, grads, outs, scratch):
        send, recv = scratch[-2:]
        parts = [
            scatter_ticks(g, scratch[6 * i : 6 * i + 6], outs[i], self.inside, send.at[i], recv.at[i])
            for i, g in enumerate(grads)
        ]

        def begin():
            for part in parts:
                part[0]()

        def end():
            for part in parts:
                part[2]()

        timed = []
        for i, part in enumerate(parts):
            times = (4 + 2 * i, 5 + 2 * i, 22 + 6.5 * i, 36 + 8 * i, 100 + i)
            timed += list(zip(times, part[1]))
        return begin, timed, end


class PlaneScatter:
    def __init__(self, blocks):
        self.arrays = list(blocks)
        self.outputs, self.scratch = [], []
        for b in blocks:
            out = jax.ShapeDtypeStruct(b.shape[1:], F32)
            self.outputs.append((out, whole(out.shape)))
            self.scratch += [pltpu.VMEM(b.shape[1:], b.dtype), pltpu.VMEM((3, *b.shape[1:]), b.dtype)]
        self.scratch += [pltpu.SemaphoreType.DMA((len(self.arrays), 4)), pltpu.SemaphoreType.DMA((len(self.arrays), 3))]

    def plan(self, blocks, outs, scratch):
        me = Place()
        send, recv = scratch[-2:]
        each = []
        for i, b in enumerate(blocks):
            own, landed = scratch[2 * i : 2 * i + 2]
            copies = [remote(b.at[k], landed.at[k - 1], send.at[i, k], recv.at[i, k - 1], me.to_plane(k)) for k in (1, 3, 2)]
            each.append((pltpu.make_async_copy(b.at[0], own, send.at[i, 0]), copies, own, landed, outs[i]))

        def begin():
            for load, copies, *_ in each:
                load.start()
                for copy in copies:
                    copy.start()

        def end():
            for load, copies, own, landed, out in each:
                load.wait()
                for copy in copies:
                    copy.wait()
                total = own[...].astype(F32)
                for k in range(3):
                    total = total + landed[k].astype(F32)
                out[...] = total

        return begin, [], end


def run_at(step, sub, subs, steps, pace, timed):
    for s in range(steps):
        point = s * subs + sub
        chosen = [tick for t, tick in timed if round(t / pace) == point]
        if chosen:
            @pl.when(step == s)
            def _():
                for tick in chosen:
                    tick()


def run_rest(subs, steps, pace, timed):
    for t, tick in timed:
        if round(t / pace) >= subs * steps:
            tick()


def call(name, body, steps, ticked, subs, pace, inputs, outputs, scratch, comm, number):
    given = [] if comm is None else comm.arrays
    made = [] if comm is None else comm.outputs

    def kernel(*refs):
        cut, at = [], 0
        for size in (len(inputs), len(given), len(outputs), len(made), len(scratch)):
            cut.append(refs[at : at + size])
            at += size
        ins, c_in, outs, c_out, own = cut
        step = pl.program_id(0)
        if comm is None:
            after = body(step, lambda sub: None, ins, outs, own)
            if after:
                pl.when(step == steps - 1)(after)
            return
        begin, timed, end = comm.plan(c_in, c_out, refs[at:])
        pl.when(step == 0)(begin)
        after = body(step, lambda sub: run_at(step, sub, subs, ticked, pace, timed), ins, outs, own)

        @pl.when(step == steps - 1)
        def _():
            run_rest(subs, ticked, pace, timed)
            end()
            if after:
                after()

    return pl.pallas_call(
        kernel,
        grid=(steps,),
        in_specs=[spec for _, spec in inputs] + [ANY] * len(given),
        out_specs=[spec for _, spec in outputs] + [spec for _, spec in made],
        out_shape=[shape for shape, _ in outputs] + [shape for shape, _ in made],
        scratch_shapes=scratch + ([] if comm is None else comm.scratch),
        compiler_params=params(None if comm is None else number),
        name=name,
    )(*[a for a, _ in inputs], *given)


def full(a):
    return a, whole(a.shape)


def shape_of(*dims, dtype=BF):
    return jax.ShapeDtypeStruct(dims, dtype)


def gelu_parts(z):
    e = jnp.exp2(z * z * (-0.5 * LOG2E))
    den = 1.0 + (0.3275911 * 0.7071067811865476) * jnp.abs(z)
    t = pl.reciprocal(den, approx=True)
    t = t * (2.0 - den * t)
    poly = t * (0.127414796 + t * (-0.142248368 + t * (0.7107068705 + t * (-0.7265760135 + t * 0.5307027145))))
    tail = poly * e
    phi = jnp.where(z < 0, tail, 1.0 - tail)
    return z * phi, phi + z * (e * 0.3989422804014327)


def moments(v):
    centered = v - jnp.mean(v, axis=-1, keepdims=True)
    rs = lax.rsqrt(jnp.mean(centered * centered, axis=-1, keepdims=True) + 1e-05)
    return centered * rs, rs


def bias_bases(buckets, bias_table, n):
    selector = (buckets[:, None] == jnp.arange(bias_table.shape[0], dtype=jnp.int32)[None, :]).astype(F32)
    per_offset = jnp.dot(selector, bias_table.astype(F32), precision=lax.Precision.HIGHEST).T
    heads = per_offset.shape[0]
    zero = jnp.zeros((heads, 1), F32)
    base = jnp.concatenate([per_offset[:, n - 1 :], zero, per_offset[:, : n - 1]], axis=1)
    flipped = per_offset[:, ::-1]
    base_t = jnp.concatenate([flipped[:, n - 1 :], zero, flipped[:, : n - 1]], axis=1) * LOG2E
    return selector, base, base_t


def build_bias(h, base, base_t, bias, bias_t):
    n = bias.shape[1]
    for src, dst, at in ((base, bias, h), (base_t, bias_t, 0)):
        row = jnp.broadcast_to(src[h], (n, 2 * n))
        dst[at] = pltpu.roll(row, 0, 1, stride=1, stride_axis=0)[:, :n].astype(dst.dtype)


def build_masks(marks, mask, mask_t):
    n = mask.shape[1]
    rows = jnp.concatenate([ref[...] for ref in marks], axis=0).astype(F32)
    seg_r, perm_r, pred_r = rows[0:1], rows[1:2], rows[2:3]
    for lo in range(0, n, 128):
        at = slice(lo, lo + 128)

        def col(k):
            piece = jnp.broadcast_to(rows[k : k + 1, at], (128, 128))
            return piece.T[:, :1]

        seg_c, perm_c, pred_c = col(0), col(1), col(2)
        same = (seg_c == seg_r) & (seg_r != 6.0)
        shown = pred_r == 0.0
        mask[0, at, :] = jnp.where(same & (shown | (perm_r <= perm_c)), 0.0, NEG)
        mask[1, at, :] = jnp.where(same & (shown | (perm_r < perm_c)), 0.0, NEG)
        same = (seg_c == seg_r) & (seg_c != 6.0)
        shown = pred_c == 0.0
        mask_t[at, :n] = jnp.where(same & (shown | (perm_c <= perm_r)), 0.0, NEG)
        mask_t[at, n:] = jnp.where(same & (shown | (perm_c < perm_r)), 0.0, NEG)


def project_streams(raw, xy, vec, layer, q_o, k_o, v_o, pf, of):
    n, d = xy.shape[1:]
    pairs = d // 128
    w = pf.shape[1] // raw.shape[0]
    pf[...] = jnp.concatenate([raw[r, :, :w] for r in range(raw.shape[0])], axis=1)
    of[...] = jnp.concatenate([raw[r, :, w:] for r in range(raw.shape[0])], axis=1)
    bq, bv = vec[layer, 0:1], vec[layer, 1:2]
    x = xy[0]
    qc = nn(x, pf[:, :d]) + bq
    qq = nn(xy[1], pf[:, :d]) + bq
    kk = nn(x, pf[:, d : 2 * d])
    vv = nn(x, pf[:, 2 * d :]) + bv
    for c in range(pairs):
        at = slice(128 * c, 128 * c + 128)
        q_o[c, :n] = qc[:, at].astype(BF)
        q_o[c, n:] = qq[:, at].astype(BF)
        k_o[c] = kk[:, at].astype(BF)
        v_o[c] = vv[:, at].astype(BF)


def attend_pair(p, tick, bias, mask, q_o, k_o, v_o, ctx_o, lse_s):
    n = mask.shape[1]
    rows_at = n // 2
    k, v = k_o[p], v_o[p]
    lane = lax.broadcasted_iota(jnp.int32, (1, 128), 1)
    low = lane < 64
    vx = jnp.concatenate([v, jnp.ones_like(v)], axis=1)
    k0 = jnp.where(low, k, 0)
    k1 = jnp.where(low, 0, k)
    for s in range(2):
        for lo in range(0, n, rows_at):
            tick(2 * s + lo // rows_at)
            at = slice(lo, lo + rows_at)
            to = slice(s * n + lo, s * n + lo + rows_at)
            q = q_o[p, to]
            parts = []
            for hh, kh in ((0, k0), (1, k1)):
                sc = (nt(q, kh) * 0.125 + bias[2 * p + hh, at].astype(F32)) * LOG2E + mask[s, at]
                m = jnp.maximum(jnp.max(sc, axis=-1, keepdims=True), FLOOR)
                e = jnp.exp2(sc - m).astype(BF)
                r = nn(e, vx)
                tot = r[:, 128:]
                tot = jnp.where(tot > 0, tot, 1.0)
                lse = m + jnp.log2(tot)
                lse_s[to] = jnp.where(lane == 2 * p + hh, lse, lse_s[to])
                parts.append(r[:, :128] / tot)
            ctx_o[p, to] = jnp.where(low, parts[0], parts[1]).astype(BF)


TIMES = (0.1, 0.15, 0.2, 0.3, 0.5, 0.52, 0.55, 0.7, 0.8, 0.93)
DEPTH = 1


def forward_kernel(
    square, vec_shape, heads,
    x_in, y_in, seg, perm, pred, base, base_t, vec_one, vec_two, *refs,
):
    count = 6 if square else 7
    weights, refs = refs[:count], refs[count:]
    (bias_t, mask_t, q_o, k_o, v_o, ctx_h, lse_o, pf_h, of_h, xh1_o, nl_o, act_o, gp_o, xh2_o, rs1_o, rs2_o,
     ins_h, rc_o, rq_o, vec_o) = refs[:20]
    refs = refs[20:]
    if square:
        fulls, refs = refs[:7], refs[7:]
        vec_land, vec_src, send, recv = refs[-4:]
        weights = [vec_src, *weights]
    else:
        fulls = weights
    bias, mask, xy, raw, cts, act_s, second_s, lse_s, pf, of, ctx_o, load_sem = refs[:12]
    n, d = x_in.shape
    pairs = d // 128
    chunks, _, fw = raw.shape
    blocks = n // xh1_o.shape[0]
    tb = n // blocks
    step = pl.program_id(0)
    span = pairs + 4 * blocks
    layer = (step >= heads + span).astype(jnp.int32)
    spot = step - heads - layer * span
    starts = []
    for l in range(2):
        lo = heads + l * span
        starts += [lo, lo + pairs, lo + pairs + 2 * blocks]
    sizes = [pairs, 2 * blocks, 2 * blocks] * 2

    points = {}
    load = lambda j: pltpu.make_async_copy(fulls[1 + j], (raw, raw, cts)[j % 3], load_sem.at[0])

    def put(at, sub, *actions):
        points.setdefault((at, sub), []).extend(actions)

    if square:
        items = [gather_steps(w, f, send.at[i], recv.at[i]) for i, (w, f) in enumerate(zip(weights, fulls))]
        vec_item, items = items[0], items[1:]
        rows, cols = vec_shape
        do = lambda action, *ks: [functools.partial(action, k) for k in ks]

        def open_all():
            Place().greet()
            blocks = [jnp.pad(ref[...].astype(F32), ((0, 8 - rows), (0, 128 - cols))) for ref in (vec_one, vec_two)]
            vec_src[...] = jnp.concatenate(blocks, axis=0).astype(BF)
            vec_item.near()
            vec_item.reach()
            items[0].near()
            items[0].reach()

        put(0, 0, open_all)
        put(2, 0, *do(vec_item.spread, 1, 3, 2), *do(vec_item.forward, 0))
        put(4, 0, *do(vec_item.forward, 1, 2, 3), *do(items[0].spread, 1))
        put(6, 0, *do(vec_item.swap, 0, 1, 2, 3), *do(items[0].forward, 0))
        put(8, 0, *do(items[0].spread, 3))
        put(9, 0, *do(items[0].forward, 1), *do(items[0].swap, 0))
        put(10, 0, *do(items[0].spread, 2), items[1].reach)
        put(11, 0, *do(items[0].forward, 3), *do(items[0].swap, 1))
        def open_next(j):
            item = items[j] if j < 6 else None
            return [item.near, *do(item.spread, 1, 3, 2)] if item else []

        def reach(j):
            return [items[j].reach] if j < 6 else []

        first = [
            *do(items[0].forward, 2), *do(items[0].swap, 3), *open_next(1), *reach(2), *do(items[0].swap, 2),
            vec_item.end, items[0].end,
        ] + (open_next(2) + reach(3) if DEPTH == 2 else [])
        for j in range(1, 6):
            lo, count = starts[j - 1], sizes[j - 1] * 4
            item = items[j]
            t = TIMES
            plan = [
                (t[0], do(item.forward, 0)), (t[1], do(item.forward, 1)), (t[2], do(item.forward, 2)),
                (t[3], do(item.forward, 3)), (t[4], open_next(j + DEPTH)), (t[5], do(item.swap, 0)),
                (t[6], do(item.swap, 1) + reach(j + DEPTH + 1)), (t[7], do(item.swap, 2)), (t[8], do(item.swap, 3)),
                (t[9], [item.end, load(j).start]),
            ]
            for part, actions in plan:
                point = int(part * count)
                put(lo + point // 4, point % 4, *actions)

    def tick(sub):
        for (at, which), actions in points.items():
            if which == sub and actions:
                @pl.when(step == at)
                def _():
                    for action in actions:
                        action()

    def arrive(j, then=None):
        @pl.when(step == starts[j])
        def _():
            if square and j == 0:
                for action in first:
                    action()
            if not square or j == 0:
                load(j).start()
            if then:
                then()
            load(j).wait()

    def vectors():
        if not square:
            copy = pltpu.make_async_copy(weights[0], vec_o, load_sem.at[1])
            copy.start()
            copy.wait()
            return
        copy = pltpu.make_async_copy(fulls[0], vec_land, load_sem.at[1])
        copy.start()
        copy.wait()
        vec_o[...] = jnp.zeros_like(vec_o)
        for l in range(2):
            for r in range(4):
                pieces = [vec_land[r, 16 * i + 8 * l : 16 * i + 8 * l + rows, :cols] for i in range(d // cols)]
                vec_o[l, rows * r : rows * r + rows] = jnp.concatenate(pieces, axis=1).astype(F32)

    keep = lambda ref, out, sem: pltpu.make_async_copy(ref, out.at[layer], load_sem.at[sem])

    @pl.when(step < heads)
    def _():
        tick_prep = tick
        tick_prep(0)
        build_bias(step, base, base_t, bias, bias_t)

    @pl.when(step == 0)
    def _():
        build_masks((seg, perm, pred), mask, mask_t)
        xy[0] = x_in[...]
        xy[1] = y_in[...]
        keep(xy, ins_h, 5).start()
        keep(xy, ins_h, 5).wait()
        lse_s[...] = jnp.zeros_like(lse_s)

    arrive(0, vectors)
    arrive(3)

    @pl.when((spot >= 0) & (spot < pairs))
    def _():
        @pl.when(spot == 0)
        def _():
            project_streams(raw, xy, vec_o, layer, q_o, k_o, v_o, pf, of)
            keep(pf, pf_h, 2).start()
            keep(of, of_h, 3).start()

        attend_pair(spot, tick, bias, mask, q_o, k_o, v_o, ctx_o, lse_s)

        @pl.when(spot == pairs - 1)
        def _():
            for lo in range(0, 2 * n, 128):
                lse_o[:, lo : lo + 128] = lse_s[lo : lo + 128].T[: lse_o.shape[0]]
            keep(ctx_o, ctx_h, 4).start()
            keep(pf, pf_h, 2).wait()
            keep(of, of_h, 3).wait()

    arrive(1)
    arrive(4)

    @pl.when((spot >= pairs) & (spot < pairs + 2 * blocks))
    def _():
        t = spot - pairs
        rows = pl.ds(pl.multiple_of(t * tb, tb), tb)
        inner = pl.ds(pl.multiple_of(t % blocks * tb, tb), tb)
        vec = vec_o.at[layer]
        z = xy[t // blocks, inner].astype(F32)
        cx = jnp.concatenate([ctx_o[c, rows] for c in range(pairs)], axis=1)
        xh1, rs1 = moments(z + (nn(cx, of[...]) + vec[2:3]))
        normed = xh1 * vec[3:4] + vec[4:5]
        nl = normed.astype(BF)
        xh1_o[...] = xh1.astype(BF)
        nl_o[...] = nl
        rs1_o[...] = jnp.broadcast_to(rs1, rs1_o.shape)
        second_s[rows] = normed + vec[5:6]
        for f in range(chunks):
            tick(f)
            at = slice(f * fw, f * fw + fw)
            act, gp = gelu_parts(nn(nl, raw[f]) + vec[8 + f : 9 + f])
            act = act.astype(BF)
            act_o[:, at] = act
            act_s[rows, at] = act
            gp_o[:, at] = gp.astype(BF)

    arrive(2)
    arrive(5)

    @pl.when(spot >= pairs + 2 * blocks)
    def _():
        t = spot - pairs - 2 * blocks
        rows = pl.ds(pl.multiple_of(t * tb, tb), tb)
        inner = pl.ds(pl.multiple_of(t % blocks * tb, tb), tb)
        vec = vec_o.at[layer]
        second = second_s[rows]
        for f in range(chunks):
            tick(f)
            at = slice(f * fw, f * fw + fw)
            second = second + nt(act_s[rows, at], cts[:, at])
        xh2, rs2 = moments(second)
        xh2_o[...] = xh2.astype(BF)
        rs2_o[...] = jnp.broadcast_to(rs2, rs2_o.shape)
        res = (xh2 * vec[6:7] + vec[7:8]).astype(BF)

        @pl.when(t == 0)
        def _():
            keep(ctx_o, ctx_h, 4).wait()

        @pl.when(layer == 0)
        def _():
            xy[t // blocks, inner] = res

        @pl.when((layer == 0) & (t == 2 * blocks - 1))
        def _():
            copy = pltpu.make_async_copy(xy, ins_h.at[1], load_sem.at[5])
            copy.start()
            copy.wait()

        @pl.when((layer == 1) & (t < blocks))
        def _():
            rc_o[...] = res

        @pl.when((layer == 1) & (t >= blocks))
        def _():
            rq_o[...] = res


def forward(x, y, marks, base, base_t, vectors, weights, square, heads):
    n, d = x.shape
    pairs = d // 128
    reps = 4
    vec_shape = vectors[0].shape
    if square:
        rows = [(4, 8 * 16, 128)] + [(4, 8 * a.shape[0], a.shape[1]) for a in weights]
        rows[3] = rows[6] = (4 * weights[2].shape[0], 8 * weights[2].shape[1])
        made = [(shape_of(*s), ANY) for s in rows]
        fw = weights[1].shape[1]
    else:
        made = []
        fw = weights[2].shape[2]
    ff = reps * fw
    blocks = 2
    tb = n // blocks
    span = pairs + 4 * blocks
    layer = lambda s: jnp.where(s >= heads + span, 1, 0)
    tok = lambda s: jnp.clip(s - heads - layer(s) * span - pairs, 0, 2 * blocks - 1)
    down = lambda s: jnp.clip(s - heads - layer(s) * span - pairs - 2 * blocks, 0, 2 * blocks - 1)
    per_layer = lambda *dims: (shape_of(2, *dims), pl.BlockSpec((None, *dims), lambda s: (layer(s), *(0,) * len(dims))))
    f32_layer = lambda *dims: (shape_of(2, *dims, dtype=F32), pl.BlockSpec((None, *dims), lambda s: (layer(s), *(0,) * len(dims))))
    blocked = lambda width, at, dtype=BF: (
        shape_of(2, 2 * n, width, dtype=dtype), pl.BlockSpec((None, tb, width), lambda s: (layer(s), at(s), 0))
    )
    end = heads + 2 * span
    outputs = [
        (shape_of(heads, n, n, dtype=F32), pl.BlockSpec((1, n, n), lambda s: (jnp.minimum(s, heads - 1), 0, 0))),
        (shape_of(n, 2 * n, dtype=F32), whole((n, 2 * n))),
        per_layer(pairs, 2 * n, 128), per_layer(pairs, n, 128), per_layer(pairs, n, 128), (shape_of(2, pairs, 2 * n, 128), ANY),
        f32_layer(16, 2 * n), (shape_of(2, d, 3 * d), ANY), (shape_of(2, d, d), ANY),
        blocked(d, tok), blocked(d, tok), blocked(ff, tok), blocked(ff, tok), blocked(d, down),
        blocked(128, tok, F32), blocked(128, down, F32),
        (shape_of(2, 2, n, d), ANY),
        (shape_of(n, d), pl.BlockSpec((tb, d), lambda s: (jnp.clip(s - (end - 2 * blocks), 0, blocks - 1), 0))),
        (shape_of(n, d), pl.BlockSpec((tb, d), lambda s: (jnp.clip(s - (end - blocks), 0, blocks - 1), 0))),
        (shape_of(2, 16, d, dtype=F32), whole((2, 16, d))),
    ]
    scratch = [
        pltpu.VMEM((heads, n, n), BF), pltpu.VMEM((2, n, n), F32), pltpu.VMEM((2, n, d), BF),
        pltpu.VMEM((reps, d, fw), BF), pltpu.VMEM((d, ff), BF), pltpu.VMEM((2 * n, ff), BF),
        pltpu.VMEM((2 * n, d), F32), pltpu.VMEM((2 * n, 128), F32),
        pltpu.VMEM((d, 3 * d), BF), pltpu.VMEM((d, d), BF), pltpu.VMEM((pairs, 2 * n, 128), BF),
        pltpu.SemaphoreType.DMA((6,)),
    ]
    if square:
        scratch += [pltpu.VMEM(made[0][0].shape, BF), pltpu.VMEM((16, 128), BF)] + [pltpu.SemaphoreType.DMA((7, SEMS))] * 2
    outs = pl.pallas_call(
        functools.partial(forward_kernel, square, vec_shape, heads),
        grid=(end,),
        in_specs=[whole(a.shape) for a in (x, y, *marks)] + [whole((heads, 1, 2 * n))] * 2 + [whole(vec_shape)] * 2
        + [ANY] * len(weights),
        out_specs=[spec for _, spec in outputs + made],
        out_shape=[shape for shape, _ in outputs + made],
        scratch_shapes=scratch,
        compiler_params=params(1 if square else None),
        name="forward",
    )(x, y, *marks, base.reshape(heads, 1, 2 * n), base_t.reshape(heads, 1, 2 * n), *vectors, *weights)
    (bias_t, mask_t, q, k, v, ctx, lse, pf, of, xh1, nl, act, gp, xh2, rs1, rs2, both, rc, rq, vec) = outs[:20]
    fulls = outs[20:] if square else weights
    return types.SimpleNamespace(
        bias_t=bias_t, mask_t=mask_t, att=(q, k, v, lse, pf), post=(ctx, xh1, nl, gp, xh2, rs1, rs2, act, of),
        both=both, content=rc, query=rq, vec=vec, fulls=fulls[1:],
    )


def norm_back(g, xh, rs, gain):
    a = g * gain
    return rs * (a - jnp.mean(a, axis=-1, keepdims=True) - xh * jnp.mean(a * xh, axis=-1, keepdims=True))


def rowsum(v):
    return jnp.sum(v, axis=0, keepdims=True)


def post_bwd_body(step, tick, ins, outs, own):
    gc, gq, ctx, xh1, nl, gp, xh2, rs1, rs2, act, of, ew, ct, vec = ins
    first_o, gctx_o, vg_o, do_o, *made = outs
    gh_s, nl_t, gf_t, cx_t, ga_s = own
    t = step
    tb, d = gc.shape
    chunks, fw = ew.shape[0], ew.shape[2]
    blocks = chunks // 2

    @pl.when(t == 0)
    def _():
        vg_o[...] = jnp.zeros_like(vg_o)

    @pl.when(t < 2 * blocks)
    def _():
        g = jnp.where(t < blocks, gc[...].astype(F32), gq[...].astype(F32))
        xh = xh2[...].astype(F32)
        vg_o[6:7] += rowsum(g * xh)
        vg_o[7:8] += rowsum(g)
        gs = norm_back(g, xh, rs2[:, :1], vec[6:7])
        gf = gs.astype(BF)
        vg_o[5:6] += rowsum(gf.astype(F32))
        gn = gs
        spot = pl.ds(pl.multiple_of(t * tb, tb), tb)
        for f in range(chunks):
            tick(f)
            at = slice(f * fw, f * fw + fw)
            gh = (nn(gf, ct[:, at]) * gp[:, at].astype(F32)).astype(BF)
            gh_s[f, spot] = gh
            vg_o[8 + f : 9 + f] += rowsum(gh.astype(F32))
            gn = gn + nt(gh, ew[f])
        xh = xh1[...].astype(F32)
        vg_o[3:4] += rowsum(gn * xh)
        vg_o[4:5] += rowsum(gn)
        first = norm_back(gn, xh, rs1[:, :1], vec[3:4])
        first_o[...] = first
        ga = first.astype(BF)
        vg_o[2:3] += rowsum(ga.astype(F32))
        ga_s[spot] = ga
        gx = nt(ga, of[...]).astype(BF)
        cx = jnp.concatenate([ctx[c] for c in range(ctx.shape[0])], axis=1)
        for c in range(ctx.shape[0]):
            gctx_o[c] = gx[:, 128 * c : 128 * c + 128]
        nl_t[:, spot] = nl[...].T
        gf_t[:, spot] = gf.T
        cx_t[:, spot] = cx.T

    @pl.when(t == 2 * blocks)
    def _():
        do_o[...] = nn(cx_t[...], ga_s[...]).astype(BF)

    @pl.when(t >= 2 * blocks)
    def _():
        for i in range(chunks):
            tick(i)
        de = nn(nl_t[...], gh_s[t - 2 * blocks]).astype(BF)
        dc = nn(gf_t[...], act[...]).astype(BF)
        if len(made) == 2:
            made[0][0] = de
            made[1][...] = dc
            return
        for i in range(2):
            half = fw // 2
            made[i][0] = de[:, half * i : half * i + half]
            reps, across, a, b = made[2 + i].shape
            for r in range(reps):
                for x in range(across):
                    made[2 + i][r, x] = dc[a * (2 * r + i) : a * (2 * r + i) + a, b * x : b * x + b]


def post_bwd(layer, gc, gq, kept, ew, ct, vec, comm, number, split):
    ctx, xh1, nl, gp, xh2, rs1, rs2, act, of = kept
    n, d = gc.shape
    chunks, fw = ew.shape[0], ew.shape[2]
    ff = chunks * fw
    pairs = ctx.shape[1]
    blocks = chunks // 2
    tb = n // blocks
    last = 2 * blocks - 1
    tok = lambda width: pl.BlockSpec((tb, width), lambda t: (jnp.minimum(t, last), 0))
    tok3 = pl.BlockSpec((pairs, tb, 128), lambda t: (0, jnp.minimum(t, last), 0))
    kept_tok = lambda width: pl.BlockSpec((None, tb, width), lambda t: (layer, jnp.minimum(t, last), 0))
    of_layer = lambda a: (a, pl.BlockSpec((None, *a.shape[1:]), lambda t: (layer, 0, 0)))
    part = lambda t: jnp.maximum(t - last - 1, 0)
    if split:
        reps, owners = split
        across = owners // chunks
        de = shape_of(chunks, d, fw // 2), pl.BlockSpec((1, d, fw // 2), lambda t: (part(t), 0, 0))
        dc = (
            shape_of(reps, owners, d // reps // 2, ff // owners),
            pl.BlockSpec((reps, across, d // reps // 2, ff // owners), lambda t: (0, part(t), 0, 0)),
        )
        made = [de, de, dc, dc]
    else:
        de = shape_of(chunks, d, fw), pl.BlockSpec((1, d, fw), lambda t: (part(t), 0, 0))
        made = [de, (shape_of(d, ff), pl.BlockSpec((d, fw), lambda t: (0, part(t))))]
    return call(
        "post_bwd", post_bwd_body, 2 * blocks + chunks, 2 * blocks + chunks, chunks, 1.7,
        [
            (gc, pl.BlockSpec((tb, d), lambda t: (jnp.minimum(t, blocks - 1), 0))),
            (gq, pl.BlockSpec((tb, d), lambda t: (jnp.clip(t - blocks, 0, blocks - 1), 0))),
            (ctx, pl.BlockSpec((None, pairs, tb, 128), lambda t: (layer, 0, jnp.minimum(t, last), 0))),
            (xh1, kept_tok(d)), (nl, kept_tok(d)), (gp, kept_tok(ff)), (xh2, kept_tok(d)),
            (rs1, kept_tok(128)), (rs2, kept_tok(128)),
            (act, pl.BlockSpec((None, 2 * n, fw), lambda t: (layer, 0, part(t)))),
            of_layer(of), full(ew), full(ct), of_layer(vec),
        ],
        [
            (shape_of(2 * n, d, dtype=F32), tok(d)), (shape_of(pairs, 2 * n, 128), tok3),
            (shape_of(16, d, dtype=F32), whole((16, d))), (shape_of(d, d), whole((d, d))),
            *made,
        ],
        [
            pltpu.VMEM((chunks, 2 * n, fw), BF),
            pltpu.VMEM((d, 2 * n), BF), pltpu.VMEM((d, 2 * n), BF), pltpu.VMEM((d, 2 * n), BF),
            pltpu.VMEM((2 * n, d), BF),
        ],
        comm, number,
    )


def attn_bwd_body(layer, step, tick, ins, outs, own):
    q, k, v, go, lse, bias_t, mask_t, *late = ins
    gx_o, gy_o, bg_o, t8_o, *dp_o = outs
    dq_s, dk_s, dv_s, diag, dk_a, dv_a, xy, first, pf, do, dp_s, sem = own
    p = step
    n, d = xy.shape[1:]
    pairs = d // 128
    wide = diag.shape[2]
    cols = n // 2

    both, first_h, pf_h, do_h = late
    loads = [
        pltpu.make_async_copy(both.at[layer], xy, sem.at[0]), pltpu.make_async_copy(first_h, first, sem.at[1]),
        pltpu.make_async_copy(pf_h.at[layer], pf, sem.at[2]), pltpu.make_async_copy(do_h, do, sem.at[3]),
    ]
    stores = [
        pltpu.make_async_copy(first.at[pl.ds(0, n)], gx_o, sem.at[4]),
        pltpu.make_async_copy(first.at[pl.ds(n, n)], gy_o, sem.at[5]),
    ]
    wide_o = d // len(dp_o)
    for i, out in enumerate(dp_o):
        stores.append(pltpu.make_async_copy(dp_s.at[:, :, pl.ds(wide_o * i, wide_o)], out, sem.at[6 + i]))

    @pl.when(p == 0)
    def _():
        for copy in loads:
            copy.start()

    @pl.when(p < pairs)
    def _():
        low = lax.broadcasted_iota(jnp.int32, (1, 128), 1) < 64
        only = lambda a, hh: jnp.where(low, a, 0) if hh == 0 else jnp.where(low, 0, a)
        diag[...] = jnp.zeros_like(diag)
        ka, va = k[0], v[0]
        for i, lo in enumerate(range(0, 2 * n, cols)):
            tick(i)
            at = slice(lo, lo + cols)
            i0 = lo % n
            qa, ga = q[0, at], go[0, at]
            dq = dk = dv = None
            for hh in range(2):
                km, vm = only(ka, hh), only(va, hh)
                lrow = lse[pl.ds(2 * p + hh, 1), at]
                sc = nt(km, qa) * (0.125 * LOG2E) + (bias_t[hh, :, i0 : i0 + cols] + mask_t[:, at])
                pr = jnp.exp2(sc - lrow)
                gp = nt(vm, ga)
                ds = pr * (gp - rowsum(pr * gp))
                dsb = ds.astype(BF)
                dv_h = nn(pr.astype(BF), only(ga, hh))
                dk_h = nn(dsb, only(qa, hh))
                dq_h = tn(dsb, km)
                dq, dk, dv = (dq_h, dk_h, dv_h) if hh == 0 else (dq + dq_h, dk + dk_h, dv + dv_h)
                for b in range(n // 128):
                    off = n - 128 - 128 * b + i0
                    diag[hh, :, off : off + cols] += ds[128 * b : 128 * b + 128]
            dq_s[p, at] = (dq * 0.125).astype(BF)
            if i == 0:
                dk_a[...] = dk
                dv_a[...] = dv
            else:
                dk_a[...] += dk
                dv_a[...] += dv
        dk_s[p] = (dk_a[...] * 0.125).astype(BF)
        dv_s[p] = dv_a[...].astype(BF)
        for hh in range(2):
            total = jnp.zeros((8, 2 * n), F32)
            for g in range(16):
                piece = jnp.concatenate([diag[hh, 8 * g : 8 * g + 8], jnp.zeros((8, 2 * n - wide), F32)], axis=1)
                total = total + (pltpu.roll(piece, 2 * n - 8 * g, 1) if g else piece)
            t8_o[hh] = total

    @pl.when(p == pairs)
    def _():
        for copy in loads:
            copy.wait()
        cat = lambda ref, at: jnp.concatenate([ref[c, at] for c in range(pairs)], axis=1)
        gqc, gqq = cat(dq_s, slice(0, n)), cat(dq_s, slice(n, 2 * n))
        gk, gv = cat(dk_s, slice(0, n)), cat(dv_s, slice(0, n))
        first[:n] = first[:n] + nt(gqc, pf[:, :d]) + nt(gk, pf[:, d : 2 * d]) + nt(gv, pf[:, 2 * d :])
        first[n:] = first[n:] + nt(gqq, pf[:, :d])
        stores[0].start()
        stores[1].start()
        bg_o[...] = jnp.zeros_like(bg_o)
        bg_o[0:1] = rowsum(gqc.astype(F32)) + rowsum(gqq.astype(F32))
        bg_o[1:2] = rowsum(gv.astype(F32))
        xt, yt = xy[0].T, xy[1].T
        grads = jnp.concatenate([
            (nn(xt, gqc) + nn(yt, gqq)).astype(BF),
            nn(xt, gk).astype(BF), nn(xt, gv).astype(BF)], axis=1)
        reps = dp_s.shape[0]
        w, u = 3 * d // reps, d // reps
        for r in range(reps):
            sides = [grads[:, r * w : r * w + w], do[:, r * u : r * u + u]]
            dp_s[r] = jnp.concatenate(sides, axis=1)
        for copy in stores[2:]:
            copy.start()

    def after():
        for copy in stores:
            copy.wait()

    return after


def attn_bwd(layer, kept, go, bias_t, mask_t, both, first, do, reps, parts, comm, number):
    q, k, v, lse, pf = kept
    n, d = first.shape[0] // 2, first.shape[1]
    packed = (reps, d, 4 * d // reps)
    pairs = d // 128
    pair = lambda *block: pl.BlockSpec(block, lambda p: (jnp.minimum(p, pairs - 1), 0, 0))
    kept_pair = lambda rows: pl.BlockSpec((None, 1, rows, 128), lambda p: (layer, jnp.minimum(p, pairs - 1), 0, 0))
    of_layer = lambda a: (a, pl.BlockSpec((None, *a.shape[1:]), lambda t: (layer, 0, 0)))
    return call(
        "attn_bwd", functools.partial(attn_bwd_body, layer), pairs + 1, pairs, 4, 1.5,
        [
            (q, kept_pair(2 * n)), (k, kept_pair(n)), (v, kept_pair(n)), (go, pair(1, 2 * n, 128)),
            of_layer(lse), (bias_t, pair(2, n, n)), full(mask_t),
            (both, ANY), (first, ANY), (pf, ANY), (do, ANY),
        ],
        [
            (shape_of(n, d, dtype=F32), ANY), (shape_of(n, d, dtype=F32), ANY),
            (shape_of(8, d, dtype=F32), whole((8, d))), (shape_of(2 * pairs, 8, 2 * n, dtype=F32), pair(2, 8, 2 * n)),
        ]
        + [(shape_of(reps, d, packed[2] // parts), ANY)] * parts,
        [
            pltpu.VMEM((pairs, 2 * n, 128), BF),
            pltpu.VMEM((pairs, n, 128), BF), pltpu.VMEM((pairs, n, 128), BF),
            pltpu.VMEM((2, 128, 2 * n - 128), F32), pltpu.VMEM((n, 128), F32), pltpu.VMEM((n, 128), F32),
            pltpu.VMEM((2, n, d), BF), pltpu.VMEM((2 * n, d), F32), pltpu.VMEM((d, 3 * d), BF), pltpu.VMEM((d, d), BF),
            pltpu.VMEM(packed, BF), pltpu.SemaphoreType.DMA((8,)),
        ],
        comm, number,
    )


def offset_sums(t8, n):
    total = sum(jnp.roll(t8[:, r], -(n - 128 + r), axis=1) for r in range(t8.shape[1]))
    return jnp.concatenate([total[:, 1:n][:, ::-1], total[:, :1], total[:, n + 1 :][:, ::-1]], axis=1)


def turn(v, shift):
    return pltpu.roll(v, v.shape[1] - shift, 1)


def table_sums(first, second, places, n):
    heads, eight, wide = first.shape
    v = turn((first[...] + second[...]).reshape(heads * eight, wide), n - 128)
    row = lax.broadcasted_iota(jnp.int32, (heads * eight, 1), 0) % eight
    for bit in (1, 2, 4):
        v = jnp.where(row // bit % 2 == 1, turn(v, bit), v)
    sums = jnp.sum(v.reshape(heads, eight, wide), axis=1)
    pick = jnp.where(lax.broadcasted_iota(jnp.int32, (32, wide), 0) == places[...], 1.0, 0.0).astype(BF)
    out = 0.0
    for _ in range(3):
        piece = sums.astype(BF)
        out = out + nt(pick, piece)
        sums = sums - piece.astype(F32)
    return out


def table_ticks(own, table, held, landed, planes, send, recv):
    me = Place()
    peers = (me.other_core, me.across_x, me.across_y)
    step = lambda s: remote(held.at[s], landed.at[s], send.at[s], recv.at[s], peers[s])
    z_copy = lambda k: remote(held.at[3], planes.at[me.z], send.at[2 + k], recv.at[2 + k], me.to_plane(k))
    z_land = lambda k: remote(held.at[3], planes.at[me.from_plane(k) // 2], send.at[2 + k], recv.at[2 + k], me.to_plane(k))

    def begin():
        held[0] = own()
        step(0).start()

    def next_step(s):
        def run():
            step(s).wait_recv()
            held[s + 1] = held[s] + landed[s]
            if s < 2:
                step(s + 1).start()
            else:
                planes[me.z] = held[3]
                for k in (1, 2, 3):
                    z_copy(k).start()
        return run

    def end():
        for k in (1, 2, 3):
            z_land(k).wait_recv()
        table[...] = (planes[0] + planes[1]) + (planes[2] + planes[3])
        for s in range(3):
            step(s).wait_send()
        for k in (1, 2, 3):
            z_copy(k).wait_send()

    return begin, [next_step(s) for s in range(3)], end


class Table:
    def __init__(self, t8_one, t8_two, places):
        vmem = pl.BlockSpec(memory_space=pltpu.VMEM)
        self.arrays = []
        self.inputs = [(t8_one, vmem), (t8_two, vmem), (places, vmem)]
        self.outputs = [(shape_of(32, 128, dtype=F32), vmem)]
        self.scratch = [
            pltpu.VMEM((4, 32, 128), F32), pltpu.VMEM((3, 32, 128), F32), pltpu.VMEM((4, 32, 128), F32),
            pltpu.SemaphoreType.DMA((6,)), pltpu.SemaphoreType.DMA((6,)),
        ]

    def plan(self, ins, outs, scratch):
        t8_one, t8_two, places = self.refs
        heads, _, wide = t8_one.shape

        def own():
            sums = table_sums(t8_one, t8_two, places, wide // 2)
            return jnp.concatenate([sums, jnp.zeros((sums.shape[0], 128 - heads), F32)], axis=1)

        begin, ticks, end = table_ticks(own, outs[0], *scratch)
        return begin, [(6 + 5 * i, tick) for i, tick in enumerate(ticks)], end


def tail_kernel(table, comm, *refs):
    table.refs = refs[:3]
    at = 3 + len(comm.arrays)
    to = at + len(comm.outputs)
    begin, timed, end = comm.plan(refs[3:at], refs[at:to], refs[to:])
    begin()
    for _, tick in timed:
        tick()
    end()


def tail(table, comm, number):
    return pl.pallas_call(
        functools.partial(tail_kernel, table, comm),
        in_specs=[spec for _, spec in table.inputs] + [ANY] * len(comm.arrays),
        out_specs=[spec for _, spec in comm.outputs],
        out_shape=[shape for shape, _ in comm.outputs],
        scratch_shapes=comm.scratch,
        compiler_params=params(number),
        name="tail",
    )(*[a for a, _ in table.inputs], *comm.arrays)


def closing_kernel(heads, table_in, vecs, *refs):
    moved, grads, outs = refs[:4], refs[4:16], refs[16:]
    for src, dst in zip(moved, outs[:4]):
        dst[...] = src[...]
    outs[4][...] = table_in[...].T[:heads]
    for l in range(2):
        po_a, po_b, c_a, c_b, e_a, e_b = grads[6 * l : 6 * l + 6]
        p, o, e, c, v = outs[5 + 5 * l : 10 + 5 * l]
        rows, cols = v.shape
        po = jnp.concatenate([po_a[...], po_b[...]], axis=1)
        p[...] = po[:, : p.shape[1]]
        o[...] = po[:, p.shape[1] :]
        e[...] = jnp.concatenate([e_a[...], e_b[...]], axis=1)
        c[...] = jnp.concatenate([c_a[...], c_b[...]], axis=0)
        v[...] = vecs[rows * l : rows * l + rows, :cols]


def closing(shape, heads, vec_shape, cut, moved, table, vecs, grads):
    outs = [shape_of(*a.shape, dtype=a.dtype) for a in moved] + [shape_of(heads, table.shape[0], dtype=F32)]
    for po, _, c, _, e, _ in grads:
        rows, lanes = po.shape[0], 2 * po.shape[1]
        dims = (rows, cut), (rows, lanes - cut), (e.shape[0], 2 * e.shape[1]), (2 * c.shape[0], c.shape[1]), vec_shape
        outs += [shape_of(*dim, dtype=F32) for dim in dims]
    vmem = pl.BlockSpec(memory_space=pltpu.VMEM)
    outs = pl.pallas_call(
        functools.partial(closing_kernel, heads),
        in_specs=[vmem] * 18,
        out_specs=[vmem] * 15,
        out_shape=outs,
        compiler_params=params(),
        name="closing",
    )(table, vecs, *moved, *grads[0], *grads[1])
    outs = [a.reshape(shape) for a in outs[:4]] + list(outs[4:])
    for i in (4, 8, 13):
        outs[i] = outs[i].T
    return tuple(outs)


def plain_gather(both, expand, contract, vectors):
    rows = lambda a, dim: lax.all_gather(a, "dp", axis=dim, tiled=True)
    po = lax.all_gather(rows(both, 0), "rep", axis=0)
    ew = lax.all_gather(rows(expand, 0), "rep", axis=0)
    ct = lax.all_gather(rows(contract, 1), "rep", axis=0, tiled=True)
    vec = lax.all_gather(rows(vectors, 1), "rep", axis=0, tiled=True).astype(F32)
    return po, ew, ct, vec


def scatter_sum(a, rep_dim, dp_dim):
    a = lax.psum_scatter(a, "rep", scatter_dimension=rep_dim, tiled=True)
    return lax.psum_scatter(a, "dp", scatter_dimension=dp_dim, tiled=True).astype(F32)


def shards(
    square,
    content_stream, query_stream, segments, perm_order, predicted, buckets, bias_table,
    project_one, output_one, expand_one, contract_one, vectors_one,
    project_two, output_two, expand_two, contract_two, vectors_two,
    content_cotangent, query_cotangent,
):
    shape = content_stream.shape
    n, d = shape[1:]
    reps = 3 * d // project_one.shape[1]
    flat = lambda a: a.reshape(n, d)
    selector, base, base_t = bias_bases(buckets, bias_table, n)
    one = (jnp.concatenate([project_one, output_one], axis=1), expand_one, contract_one.T, vectors_one)
    two = (jnp.concatenate([project_two, output_two], axis=1), expand_two, contract_two.T, vectors_two)
    rows, cols = vectors_one.shape
    if square:
        weights = [*one[:3], *two[:3]]
    else:
        full_one, full_two = plain_gather(*one), plain_gather(*two)
        both = jnp.pad(jnp.stack([full_one[3], full_two[3]]), ((0, 0), (0, 16 - 4 * rows), (0, 0)))
        weights = [both, *full_one[:3], *full_two[:3]]
    kept = forward(
        flat(content_stream), flat(query_stream), (segments, perm_order, predicted), base, base_t,
        (vectors_one, vectors_two), weights, square, bias_table.shape[1],
    )
    bias_t, mask_t = kept.bias_t, kept.mask_t
    ew, ct = (kept.fulls[1], kept.fulls[4]), (kept.fulls[2], kept.fulls[5])
    x, y = kept.content, kept.query
    def back_post(layer, gx, gy, comm, number):
        split = (4, 8) if square else None
        return post_bwd(layer, gx, gy, kept.post, ew[layer], ct[layer], kept.vec, comm, number, split)

    def back_attn(layer, gctx, first, do, comm, number):
        return attn_bwd(layer, kept.att, gctx, bias_t, mask_t, kept.both, first, do, reps, 2 if square else 1, comm, number)

    pieces = lambda a: a.reshape(4, 4, 2, a.shape[-2] if a.ndim == 4 else a.shape[1] // 8, a.shape[-1])
    sent = lambda grads, blocks: Comms(Scatter([pieces(a) for a in grads]), *[PlaneScatter(b) for b in blocks]) if square else None
    first, gctx, vg_two, do, *halves = back_post(1, flat(content_cotangent), flat(query_cotangent), None, 0)
    gx, gy, bg_two, t8_two, *made = back_attn(1, gctx, first, do, sent(halves[2:] + halves[:1], []), 5)
    if square:
        dp_two, blocks_two = made[:2], made[2:]
    else:
        (dp_two,), (de_two, dc_two) = made, halves
    first, gctx, vg_one, do, *made = back_post(
        0, gx, gy, sent(halves[1:2] + list(dp_two), [blocks_two]) if square else None, 6
    )
    halves, made = (made[:4], made[4:]) if square else (made, [])
    blocks_mid, sum_two = made[:3], made[3:]
    gx, gy, bg_one, t8_one, *made = back_attn(0, gctx, first, do, sent(halves[2:] + halves[:2], [blocks_mid]), 7)
    if square:
        dp_one, blocks_one, sum_mid = made[:2], made[2:6], made[6:]
    else:
        (dp_one,), (de_one, dc_one) = made, halves
    vg_one = jnp.concatenate([bg_one[:2], vg_one[2:12]], axis=0)
    vg_two = jnp.concatenate([bg_two[:2], vg_two[2:12]], axis=0)
    cut = project_one.shape[1]
    if square:
        vgs = jnp.stack([vg_one, vg_two]).reshape(2, 4, rows, 8, cols).transpose(1, 3, 0, 2, 4)
        vgs = jnp.pad(vgs.reshape(4, 8, 2 * rows, cols), ((0, 0), (0, 0), (0, 8 - 2 * rows), (0, 128 - cols)))
        turned = buckets[::-1]
        places = jnp.concatenate([turned[n - 1 :], -jnp.ones((1,), jnp.int32), turned[: n - 1]])[None]
        table = Table(t8_one, t8_two, places)
        po_a, po_b, vecs, table, c_a, c_b, e_a, e_b = tail(
            table, Comms(Scatter([pieces(a) for a in (*dp_one, vgs)], True), table, PlaneScatter(blocks_one)), 8
        )
        grads = [[po_a, po_b, c_a, c_b, e_a, e_b], [sum_mid[1], sum_mid[2], *sum_two, sum_mid[0]]]
        return closing(shape, bias_table.shape[1], (rows, cols), cut, (x, y, gx, gy), table, vecs, grads)
    else:
        distances = offset_sums(t8_one + t8_two, n)
        table = jnp.dot(selector.T, distances.T, precision=lax.Precision.HIGHEST)
        table = lax.psum(table, ("dp", "rep"))

        def spread(dp, de, dc, vec):
            po = scatter_sum(dp, 0, 1)[0]
            return po[:, :cut], po[:, cut:], scatter_sum(de, 0, 1)[0], scatter_sum(dc, 0, 1).T, scatter_sum(vec, 0, 1)

        grads_one = spread(dp_one, de_one, dc_one, vg_one)
        grads_two = spread(dp_two, de_two, dc_two, vg_two)
    return (
        x.reshape(shape), y.reshape(shape), gx.reshape(shape), gy.reshape(shape), table,
        *grads_one, *grads_two,
    )


def solution(mesh):
    rows3, rows2 = P(("dp", "rep"), None, None), P(("dp", "rep"), None)
    weights = (P("dp", "rep"),) * 4 + (P("rep", "dp"),)
    square = mesh.shape["dp"] == 8 and mesh.shape["rep"] == 4
    return jax.shard_map(
        functools.partial(shards, square),
        mesh=mesh,
        in_specs=(rows3, rows3, rows2, rows2, rows2, P(), P(), *weights, *weights, rows3, rows3),
        out_specs=(rows3, rows3, rows3, rows3, P(), *weights, *weights),
        check_vma=False,
    )
```
